32 devices in a mesh: seqs: 4 (over y, x), span: 8 (over z, core).
Axes of the slice: x: 2, y: 2, z: 4, core: 2. Of those that a mesh axis runs over, the one named last changes fastest.
Arguments:
- tokens: bfloat16 [4, 2, 512, 2048], P('seqs', None, 'span'), may hold values from -6 to 6
- attn_weight: bfloat16 [2048, 8448], P(('seqs', 'span')), may hold values from -0.1875 to 0.1875
- mlp_weight: bfloat16 [2048, 16896], P(('seqs', 'span')), may hold values from -0.125 to 0.125
- norm1_gain: bfloat16 [2048], P(('seqs', 'span')), may hold values from 0.5 to 1.5
- norm2_gain: bfloat16 [2048], P(('seqs', 'span')), may hold values from 0.5 to 1.5
- gate_bias: bfloat16 [256], P(('seqs', 'span')), may hold values from 1 to 8
- lengths: int32 [4, 2, 4], P('seqs'), may hold values from 1 to 509, as said below
- cotangent: bfloat16 [4, 2, 512, 2048], P('seqs', None, 'span'), may hold values from -6 to 6
Outputs:
- mixed: bfloat16 [4, 2, 512, 2048], P('seqs', None, 'span')
- grad_tokens: float32 [4, 2, 512, 2048], P('seqs', None, 'span')
- grad_attn: float32 [2048, 8448], P(('seqs', 'span'))
- grad_mlp: float32 [2048, 16896], P(('seqs', 'span'))
- grad_gain1: float32 [2048], P(('seqs', 'span'))
- grad_gain2: float32 [2048], P(('seqs', 'span'))
- grad_bias: float32 [256], P(('seqs', 'span'))
The draws below stay inside these ranges and needn't reach their ends.
Inputs may be any that keep to these rules, and one draw needn't show every extreme that they name: In every row lengths[g, p, :] the 4 lengths add up to 512; one document of each row, its place drawn from the seed, begins in the first 64 positions and ends in the last 64.
All inputs are finite; a program needn't handle non-finite values.
Results may differ from the reference program's by a relative error of at most 0.018.
Values may be sent and summed in bfloat16 or wider, within the bound.
No kernel may reach another device: no remote copies, remote signals or barrier semaphores. Data moves between devices by JAX's collectives and lax.ppermute only.
A program may use at most 512 MiB of HBM per device.

```python
import jax
import jax.numpy as jnp
from jax import lax

D = 2048
HEADS = 4
HEAD_DIM = 512
SLOTS = 64
FF = 5632
BLOCK_TOK = 64
PHASES = 2
DOCS = 4
GROUPS = 4
SEQ_LEN = 512
GATE_COLS = 256
ATTN_COLS = 8448
MLP_COLS = 16896


def draw_lengths(key, part):
    key = jax.random.fold_in(key, 7)
    key_short, key_row, key_place = jax.random.split(key, 3)
    row_total = GROUPS * PHASES
    short_top = BLOCK_TOK // 4
    shorts = jax.random.randint(key_short, (row_total, DOCS - 1), 1, short_top + 1, dtype=jnp.int32)
    chosen = jax.random.randint(key_row, (), 0, row_total, dtype=jnp.int32)
    row_ids = jnp.arange(row_total, dtype=jnp.int32)
    shorts = jnp.where((row_ids == chosen)[:, None], 1, shorts).astype(jnp.int32)
    long_pos = jax.random.randint(key_place, (row_total,), 0, DOCS, dtype=jnp.int32)
    doc_idx = jnp.arange(DOCS, dtype=jnp.int32)
    source = jnp.where(doc_idx[None, :] < long_pos[:, None], doc_idx[None, :], doc_idx[None, :] - 1)
    source = jnp.clip(source, 0, DOCS - 2).astype(jnp.int32)
    picked = jnp.take_along_axis(shorts, source, axis=1)
    long_len = (SEQ_LEN - jnp.sum(shorts, axis=1)).astype(jnp.int32)
    lengths_all = jnp.where(doc_idx[None, :] == long_pos[:, None], long_len[:, None], picked)
    return lengths_all.reshape(GROUPS, PHASES, DOCS).astype(jnp.int32)


def levels(key, shape, cuts, least, high):
    def one(position, parts):
        steps = jax.random.uniform(jax.random.fold_in(jax.random.fold_in(key, 6), position), (parts,), jnp.float32, least / len(cuts), high / len(cuts))
        return jnp.repeat(jnp.exp(steps), shape[position] // parts).reshape((-1,) + (1,) * (len(shape) - position - 1))

    level = one(*cuts[0])
    for cut in cuts[1:]:
        level = level * one(*cut)
    return level


def gaussian(own_key, extent, width, limit, cuts=(), held_as=jnp.bfloat16):
    array = jax.random.normal(own_key, extent, jnp.float32) * width
    if len(cuts) > 0:
        array = levels(own_key, extent, cuts, -0.22, 0.18) * array
    return jnp.clip(array, min=-limit, max=limit).astype(held_as)


def setup_inputs(seed: int = 0) -> dict:
    keys = jax.random.split(jax.random.key(seed), 9)
    tokens = gaussian(keys[0], (GROUPS, PHASES, SEQ_LEN, D), 1.0, 6.0, ((0, 4), (2, 8)))
    attn_weight = gaussian(keys[1], (D, ATTN_COLS), (D // 2) ** -0.5, 0.1875, ((0, 32),))
    mlp_weight = gaussian(keys[2], (D, MLP_COLS), D ** -0.5, 0.125, ((0, 32),))
    norm1_gain = jnp.clip(1.0 + 0.1 * jax.random.normal(keys[3], (D,), jnp.float32), 0.5, 1.5).astype(jnp.bfloat16)
    norm2_gain = jnp.clip(1.0 + 0.1 * jax.random.normal(keys[4], (D,), jnp.float32), 0.5, 1.5).astype(jnp.bfloat16)
    gate_bias = jnp.clip(1.0 + 7.0 * jax.random.uniform(keys[5], (GATE_COLS,), jnp.float32) ** levels(keys[5], (GATE_COLS,), ((0, 32),), -0.2, 0.2), 1.0, 8.0).astype(jnp.bfloat16)
    lengths = draw_lengths(jax.random.fold_in(keys[8], 71), 0)
    cotangent = gaussian(keys[7], (GROUPS, PHASES, SEQ_LEN, D), 1.0, 6.0, ((0, 4), (2, 8)))
    return {"tokens": tokens, "attn_weight": attn_weight, "mlp_weight": mlp_weight, "norm1_gain": norm1_gain, "norm2_gain": norm2_gain, "gate_bias": gate_bias, "lengths": lengths, "cotangent": cotangent}


NORM_EPS = 1e-05
GATE_SOFTENING = 8.0
HIGHEST = lax.Precision.HIGHEST

@jax.custom_vjp
def low(v):
    return lax.optimization_barrier(v.astype(jnp.bfloat16)).astype(jnp.float32)

@jax.custom_vjp
def low_back(v):
    return v

def low_keep(v):
    return (low(v), None)

def low_pass(kept, grad):
    return (grad,)

def back_keep(v):
    return (v, None)

def back_low(kept, grad):
    return (low(grad),)
low.defvjp(low_keep, low_pass)
low_back.defvjp(back_keep, back_low)

def matmul(left_side, right_side):
    return jnp.dot(left_side, right_side, precision=HIGHEST, preferred_element_type=jnp.float32)

def rms_scale(values):
    return lax.rsqrt(lax.optimization_barrier(jnp.mean(values * values, axis=-1, keepdims=True)) + NORM_EPS)

def logarithmic_sigmoid(values):
    return jnp.minimum(values, 0.0) - jnp.log1p(jnp.exp(-jnp.abs(values)))

def segment_ids(lengths_row, positions):
    offsets = (jnp.cumsum(lengths_row) - lengths_row).astype(jnp.int32)
    return lax.optimization_barrier(jnp.sum((positions[:, None] >= offsets[None, 1:]).astype(jnp.int32), axis=1)).astype(jnp.int32)

def build_masks(lengths_row, positions, start_pos):
    segments = segment_ids(lengths_row, positions)
    before = segment_ids(lengths_row, jnp.reshape(start_pos - 1, (1,)).astype(jnp.int32))[0]
    previous = jnp.where(start_pos > 0, before, -1)
    order_idx = jnp.arange(positions.shape[0], dtype=jnp.int32)
    same_mask = ((segments[:, None] == segments[None, :]) & (order_idx[:, None] >= order_idx[None, :])).astype(jnp.float32)
    carry_mask = (segments == previous).astype(jnp.float32)
    last_mask = (segments == segments[-1]).astype(jnp.float32)
    return (same_mask, carry_mask, last_mask)

def head_output(query_part, key_part, value_part, gate_part, same_mask, carry_mask, keys_in, values_in):
    scale_factor = query_part.shape[-1] ** (-0.5)
    cumulative = jnp.cumsum(gate_part, axis=0)
    written = -jnp.expm1(gate_part)
    decay_pairs = jnp.exp(jnp.minimum(cumulative[:, None, :] - cumulative[None, :, :], 0.0)) * same_mask[:, :, None]
    weighted = decay_pairs * written[None, :, :]
    affinity = matmul(query_part, key_part.T) * scale_factor
    entering = jnp.exp(cumulative) * carry_mask[:, None]
    scores = lax.optimization_barrier(jnp.sum(affinity[:, :, None] * weighted, axis=1)) + entering * matmul(query_part, keys_in.T) * scale_factor
    shifted = scores - lax.optimization_barrier(jnp.max(scores, axis=1, keepdims=True))
    exp_scores = jnp.exp(shifted)
    slot_probs = exp_scores / lax.optimization_barrier(jnp.sum(exp_scores, axis=1, keepdims=True))
    mixing = lax.optimization_barrier(jnp.sum(slot_probs[:, None, :] * weighted, axis=2))
    slot_output = matmul(mixing, value_part) + matmul(slot_probs * entering, values_in)
    return slot_output * rms_scale(slot_output)

def head_states(key_part, value_part, gate_part, last_mask, carry_mask):
    cumulative = jnp.cumsum(gate_part, axis=0)
    written = -jnp.expm1(gate_part)
    tail_weight = jnp.exp(cumulative[-1][None, :] - cumulative) * written * last_mask[:, None]
    new_keys = matmul(tail_weight.T, key_part)
    new_values = matmul(tail_weight.T, value_part)
    fade_out = jnp.exp(cumulative[-1]) * carry_mask[-1]
    return (new_keys, new_values, fade_out)

def sequence_mix(features, logged_gate, lengths_row):
    blocks = SEQ_LEN // BLOCK_TOK

    def heads_first(values, inner_dim):
        return values.reshape(blocks, BLOCK_TOK, HEADS, inner_dim).transpose(0, 2, 1, 3)
    query_all = heads_first(features[:, :D], HEAD_DIM)
    key_all = heads_first(features[:, D:2 * D], HEAD_DIM)
    value_all = heads_first(features[:, 2 * D:], HEAD_DIM)
    gate_all = heads_first(logged_gate, SLOTS)
    starts = jnp.arange(blocks, dtype=jnp.int32) * BLOCK_TOK

    def block_step(state_pair, one_item):
        query_part, key_part, value_part, gate_part, start_pos = one_item
        positions = start_pos + jnp.arange(BLOCK_TOK, dtype=jnp.int32)
        same_mask, carry_mask, last_mask = build_masks(lengths_row, positions, start_pos)
        normed = jax.vmap(head_output, in_axes=(0, 0, 0, 0, None, None, 0, 0))(query_part, key_part, value_part, gate_part, same_mask, carry_mask, state_pair[0], state_pair[1])
        new_keys, new_values, fade_out = jax.vmap(head_states, in_axes=(0, 0, 0, None, None))(key_part, value_part, gate_part, last_mask, carry_mask)
        next_pair = (fade_out[..., None] * state_pair[0] + new_keys, fade_out[..., None] * state_pair[1] + new_values)
        return (next_pair, normed)
    initial = (jnp.zeros((HEADS, SLOTS, HEAD_DIM), jnp.float32), jnp.zeros((HEADS, SLOTS, HEAD_DIM), jnp.float32))
    unused, all_outputs = lax.scan(jax.checkpoint(block_step), initial, (query_all, key_all, value_all, gate_all, starts))
    return all_outputs.transpose(0, 2, 1, 3).reshape(SEQ_LEN, D)

def sequence_forward(sequence_x, lengths_row, attn_w, mlp_w, gain_one, gain_two, bias_vec):
    input_one = low(sequence_x * rms_scale(sequence_x) * gain_one)
    pre_feats = low_back(matmul(input_one, attn_w[:, :3 * D]))
    gate_before_activation = low_back(matmul(input_one, attn_w[:, 3 * D:3 * D + GATE_COLS]) + bias_vec)
    features = low(pre_feats * jax.nn.sigmoid(pre_feats))
    logged_gate = logarithmic_sigmoid(gate_before_activation) / GATE_SOFTENING
    slot_rows = sequence_mix(features, logged_gate, lengths_row)
    attn_out = low_back(matmul(low(slot_rows), attn_w[:, 3 * D + GATE_COLS:].T))
    after_attn = sequence_x + attn_out
    input_two = low(after_attn * rms_scale(after_attn) * gain_two)
    gate_up = matmul(input_two, mlp_w[:, :2 * FF])
    gate_pre = low_back(gate_up[:, :FF])
    up_pre = low_back(gate_up[:, FF:])
    hidden = low(gate_pre * jax.nn.sigmoid(gate_pre) * up_pre)
    mlp_out = low_back(matmul(hidden, mlp_w[:, 2 * FF:].T))
    return after_attn + mlp_out

def reference(tokens, attn_weight, mlp_weight, norm1_gain, norm2_gain, gate_bias, lengths, cotangent):
    params = tuple((item_arr.astype(jnp.float32) for item_arr in (tokens, attn_weight, mlp_weight, norm1_gain, norm2_gain, gate_bias)))
    length_rows = lengths.reshape(GROUPS * PHASES, DOCS).astype(jnp.int32)

    def forward(input_all, attn_w, mlp_w, gain_one, gain_two, bias_vec):
        flat_input = input_all.reshape(GROUPS * PHASES, SEQ_LEN, D)

        def one_sequence(scan_carry, one_item):
            result_rows = jax.checkpoint(sequence_forward)(one_item[0], one_item[1], attn_w, mlp_w, gain_one, gain_two, bias_vec)
            return (scan_carry, result_rows)
        unused, all_outputs = lax.scan(one_sequence, jnp.zeros((), jnp.float32), (flat_input, length_rows))
        return all_outputs.reshape(input_all.shape)
    output_full, pull_back = jax.vjp(forward, *params)
    gradients = pull_back(cotangent.astype(jnp.float32))
    return (output_full.astype(jnp.bfloat16), gradients[0], gradients[1], gradients[2], gradients[3], gradients[4], gradients[5])
```

```python
import functools
import jax
import jax.numpy as jnp
from jax import lax
from jax.experimental import pallas as pl
from jax.experimental.pallas import tpu as pltpu
from jax.sharding import PartitionSpec as P

BLOCK = 64
SUB = 16
SLOTS = 64
HEAD_DIM = 512
NORM_EPS = 1e-05


def mm(a, b, dims):
    return lax.dot_general(
        a.astype(jnp.bfloat16), b.astype(jnp.bfloat16), (dims, ((), ())), preferred_element_type=jnp.float32
    )


def halves(a):
    if a.dtype == jnp.bfloat16:
        return a, None
    high = a.astype(jnp.bfloat16)
    return high, (a - high.astype(jnp.float32)).astype(jnp.bfloat16)


def fine(a, b, dims):
    (a_high, a_low), (b_high, b_low) = halves(a), halves(b)
    out = mm(a_high, b_high, dims)
    if b_low is not None:
        out = out + mm(a_high, b_low, dims)
    if a_low is not None:
        out = out + mm(a_low, b_high, dims)
    return out


NN, NT, TN = ((1,), (0,)), ((1,), (1,)), ((0,), (0,))


def nn(a, b):
    return mm(a, b, NN)


def nt(a, b):
    return mm(a, b, NT)


def tn(a, b):
    return mm(a, b, TN)


def exact(a, b):
    return lax.dot_general(
        a, b, (((1,), (0,)), ((), ())), precision=lax.Precision.HIGHEST, preferred_element_type=jnp.float32
    )


def iota(shape, dim):
    return lax.broadcasted_iota(jnp.int32, shape, dim)


def block_decay(gate, write, seg_col, seg_row, seg_prev):
    row, col = iota((BLOCK, BLOCK), 0), iota((BLOCK, BLOCK), 1)
    same = jnp.where((seg_col == seg_row) & (row >= col), 1.0, 0.0)
    lower = jnp.where(row >= col, 1.0, 0.0)
    cum = exact(lower, gate)
    total = cum[BLOCK - 1 :]
    carry = jnp.where(seg_col == seg_prev, 1.0, 0.0)
    last = jnp.where(seg_col == seg_col[BLOCK - 1 :], 1.0, 0.0)
    enter = jnp.exp(cum) * carry
    tail = jnp.exp(total - cum) * last
    fade = jnp.exp(total) * carry[BLOCK - 1 :]
    falls, rises = [], []
    for i in range(1, BLOCK // SUB):
        base = cum[i * SUB - 1 : i * SUB]
        falls.append(jnp.exp(cum[i * SUB : (i + 1) * SUB] - base))
        rises.append(jnp.exp(base - cum[: i * SUB]))
    return same, cum, enter, tail, fade, falls, rises


def diagonal(square):
    return jnp.concatenate([square[i : i + SUB, i : i + SUB] for i in range(0, BLOCK, SUB)], axis=0)


def undiagonal(strip):
    row, col = iota((BLOCK, BLOCK), 0), iota((BLOCK, BLOCK), 1)
    wide = jnp.concatenate([strip] * (BLOCK // SUB), axis=1)
    return jnp.where(row // SUB == col // SUB, wide, 0.0)


def parts(values):
    return values.reshape(BLOCK // SUB, SUB, values.shape[-1])


def decay_at(cum, j):
    cum_parts = parts(cum)
    return jnp.exp(jnp.minimum(cum_parts - cum_parts[:, j : j + 1], 0.0))


def over_sources(pairs, cum, write, falls, rises):
    strip = parts(diagonal(pairs))
    write_parts = parts(write)
    near = jnp.zeros((BLOCK // SUB, SUB, SLOTS), jnp.float32)
    for j in range(SUB):
        near = near + strip[:, :, j : j + 1] * (decay_at(cum, j) * write_parts[:, j : j + 1])
    near = near.reshape(BLOCK, SLOTS)
    far = [jnp.zeros((SUB, SLOTS), jnp.float32)]
    for i in range(1, BLOCK // SUB):
        rows = pairs[i * SUB : (i + 1) * SUB, : i * SUB]
        far.append(falls[i - 1] * fine(rows, rises[i - 1] * write[: i * SUB], NN))
    return near + jnp.concatenate(far, axis=0)


def over_slots(values, cum, write, falls, rises):
    value_parts, write_parts = parts(values), parts(write)
    lane = iota((BLOCK // SUB, SUB, SUB), 2)
    strip = jnp.zeros((BLOCK // SUB, SUB, SUB), jnp.float32)
    for j in range(SUB):
        term = value_parts * (decay_at(cum, j) * write_parts[:, j : j + 1])
        strip = jnp.where(lane == j, jnp.sum(term, axis=2, keepdims=True), strip)
    out = undiagonal(strip.reshape(BLOCK, SUB))
    far = [jnp.zeros((SUB, BLOCK), jnp.float32)]
    for i in range(1, BLOCK // SUB):
        rows = values[i * SUB : (i + 1) * SUB] * falls[i - 1]
        piece = fine(rows, rises[i - 1] * write[: i * SUB], NT)
        far.append(jnp.concatenate([piece, jnp.zeros((SUB, BLOCK - i * SUB), jnp.float32)], axis=1))
    return out + jnp.concatenate(far, axis=0)


def over_targets(pairs_values, cum, falls, rises):
    row = iota((BLOCK // SUB, SUB, SLOTS), 1)
    near = jnp.zeros((BLOCK // SUB, SUB, SLOTS), jnp.float32)
    strips = [(parts(diagonal(p)), parts(v)) for p, v in pairs_values]
    for j in range(SUB):
        term = sum(strip[:, :, j : j + 1] * value for strip, value in strips) * decay_at(cum, j)
        near = jnp.where(row == j, jnp.sum(term, axis=1, keepdims=True), near)
    out = near.reshape(BLOCK, SLOTS)
    far = jnp.zeros((BLOCK, SLOTS), jnp.float32)
    for i in range(1, BLOCK // SUB):
        here = slice(i * SUB, (i + 1) * SUB)
        piece = sum(fine(p[here, : i * SUB], v[here] * falls[i - 1], TN) for p, v in pairs_values)
        piece = rises[i - 1] * piece
        far = far + jnp.concatenate([piece, jnp.zeros((BLOCK - i * SUB, SLOTS), jnp.float32)], axis=0)
    return out + far


def load_block(i, q_ref, k_ref, v_ref, gate_ref, write_ref, segc_ref, segr_ref):
    here = pl.ds(pl.multiple_of(i * BLOCK, BLOCK), BLOCK)
    seg_col = segc_ref[here, :]
    seg_row = segr_ref[i]
    before = segc_ref[pl.ds(jnp.maximum(i * BLOCK - 1, 0), 1), :]
    seg_prev = jnp.where(i > 0, before, -1)
    return here, q_ref[here, :], k_ref[here, :], v_ref[here, :], gate_ref[here, :], write_ref[here, :], seg_col, seg_row, seg_prev


def forward_kernel(q_ref, k_ref, v_ref, gate_ref, write_ref, segc_ref, segr_ref,
                   low_ref, out_ref, score_ref, prob_ref, pair_ref, mix_ref, keys_ref, values_ref, key_state, value_state):
    scale = HEAD_DIM ** -0.5
    key_state[...] = jnp.zeros_like(key_state)
    value_state[...] = jnp.zeros_like(value_state)

    def step(i, _):
        here, q, k, v, gate, write, seg_col, seg_row, seg_prev = load_block(i, q_ref, k_ref, v_ref, gate_ref, write_ref, segc_ref, segr_ref)
        same, cum, enter, tail, fade, falls, rises = block_decay(gate, write, seg_col, seg_row, seg_prev)
        keys_in, values_in = key_state[...], value_state[...]
        keys_ref[i], values_ref[i] = keys_in, values_in
        keep = fade.reshape(SLOTS, 1)
        send = tail * write
        key_state[...] = keep * keys_in + tn(send, k)
        value_state[...] = keep * values_in + fine(send, v, TN)
        pairs = nt(q, k) * same
        score = scale * (over_sources(pairs, cum, write, falls, rises) + enter * nt(q, keys_in))
        prob = jnp.exp(score - jnp.max(score, axis=1, keepdims=True))
        prob = prob / jnp.sum(prob, axis=1, keepdims=True)
        mix = over_slots(prob, cum, write, falls, rises) * same
        out = fine(mix, v, NN) + fine(prob * enter, values_in, NN)
        scaled = out * lax.rsqrt(jnp.mean(out * out, axis=1, keepdims=True) + NORM_EPS)
        low_ref[here, :] = scaled.astype(jnp.bfloat16)
        out_ref[here, :] = out
        score_ref[here, :] = score
        prob_ref[here, :] = prob
        pair_ref[here, :] = pairs
        mix_ref[here, :] = mix
        return 0

    lax.fori_loop(0, q_ref.shape[0] // BLOCK, step, 0)


def backward_kernel(q_ref, k_ref, v_ref, gate_ref, write_ref, segc_ref, segr_ref,
                    out_ref, score_ref, prob_ref, pair_ref, mix_ref, keys_ref, values_ref, don_ref,
                    dq_ref, dk_ref, dv_ref, dgate_ref, key_state, value_state, key_next, value_next):
    scale = HEAD_DIM ** -0.5
    blocks = q_ref.shape[0] // BLOCK
    for state in (key_state, value_state, key_next, value_next):
        state[...] = jnp.zeros_like(state)

    def step(lap, _):
        i = blocks - 1 - lap
        here, q, k, v, gate, write, seg_col, seg_row, seg_prev = load_block(i, q_ref, k_ref, v_ref, gate_ref, write_ref, segc_ref, segr_ref)
        same, cum, enter, tail, fade, falls, rises = block_decay(gate, write, seg_col, seg_row, seg_prev)
        last = jnp.where(seg_col == seg_col[BLOCK - 1 :], 1.0, 0.0)
        score, prob, pairs, mix = score_ref[here, :], prob_ref[here, :], pair_ref[here, :], mix_ref[here, :]
        keys_in, values_in = keys_ref[i], values_ref[i]
        out, don = out_ref[here, :], don_ref[here, :]
        unit = lax.rsqrt(jnp.mean(out * out, axis=1, keepdims=True) + NORM_EPS)
        normed = out * unit
        dout = unit * (don - normed * jnp.mean(don * normed, axis=1, keepdims=True))
        dmix = fine(dout, v, NT) * same
        dprob = over_sources(dmix, cum, write, falls, rises) + enter * fine(dout, values_in, NT)
        inner = prob * dprob
        dscore = inner - prob * jnp.sum(inner, axis=1, keepdims=True)
        slope = scale * dscore
        dpairs = over_slots(slope, cum, write, falls, rises) * same
        dcross = slope * enter
        dkeys, dvalues = key_state[...], value_state[...]
        send = tail * write
        dq_ref[here, :] = nn(dpairs, k) + nn(dcross, keys_in)
        dk_ref[here, :] = tn(dpairs, q) + nn(send, dkeys)
        dv_ref[here, :] = tn(mix, dout) + nn(send, dvalues)
        heard = over_targets([(pairs, slope), (dmix, prob)], cum, falls, rises)
        heard = heard + tail * (nt(k, dkeys) + nt(v, dvalues))
        ones = jnp.ones((8, HEAD_DIM), jnp.float32)
        held = lax.dot_general(ones, dkeys * key_next[...] + dvalues * value_next[...], (((1,), (1,)), ((), ())),
                               precision=lax.Precision.HIGHEST, preferred_element_type=jnp.float32)[:1]
        upper = same.T
        flow = exact(upper, dscore * score + inner - write * heard)
        dgate_ref[here, :] = flow - jnp.exp(gate) * heard + last * held
        keep = fade.reshape(SLOTS, 1)
        key_state[...] = keep * dkeys + tn(dcross, q)
        value_state[...] = keep * dvalues + fine(prob * enter, dout, TN)
        key_next[...], value_next[...] = keys_in, values_in
        return 0

    lax.fori_loop(0, blocks, step, 0)


def vmem_call(kernel, outs, scratch, flops, args, limit=48):
    nbytes = sum(a.size * a.dtype.itemsize for a in args) + sum(o.size * o.dtype.itemsize for o in outs)
    return pl.pallas_call(
        kernel,
        out_shape=outs,
        in_specs=[pl.BlockSpec(memory_space=pltpu.VMEM)] * len(args),
        out_specs=[pl.BlockSpec(memory_space=pltpu.VMEM)] * len(outs),
        scratch_shapes=scratch,
        cost_estimate=pl.CostEstimate(flops=flops, bytes_accessed=nbytes, transcendentals=0),
        compiler_params=pltpu.CompilerParams(vmem_limit_bytes=limit * 2**20),
    )(*args)


def forward_mix(q, k, v, gate, write, seg):
    length = q.shape[0]
    blocks = length // BLOCK
    shape = jax.ShapeDtypeStruct
    slots = shape((length, SLOTS), jnp.float32)
    states = shape((blocks, SLOTS, HEAD_DIM), jnp.float32)
    state = pltpu.VMEM((SLOTS, HEAD_DIM), jnp.float32)
    outs = [shape((length, HEAD_DIM), jnp.bfloat16), shape((length, HEAD_DIM), jnp.float32), slots, slots, slots, slots, states, states]
    args = (q, k, v, gate, write, seg.reshape(length, 1), seg.reshape(blocks, 1, BLOCK))
    return vmem_call(forward_kernel, outs, [state] * 2, 8 * length * HEAD_DIM * SLOTS * 2, args)


def backward_mix(q, k, v, gate, write, seg, saved, don):
    length = q.shape[0]
    blocks = length // BLOCK
    shape = jax.ShapeDtypeStruct
    wide = shape((length, HEAD_DIM), jnp.float32)
    state = pltpu.VMEM((SLOTS, HEAD_DIM), jnp.float32)
    outs = [wide, wide, wide, shape((length, SLOTS), jnp.float32)]
    args = (q, k, v, gate, write, seg.reshape(length, 1), seg.reshape(blocks, 1, BLOCK), *saved, don)
    return vmem_call(backward_kernel, outs, [state] * 4, 20 * length * HEAD_DIM * SLOTS * 2, args)


HEADS = 4
FF = 5632
GATE_SOFTENING = 8.0


def dot(a, b, dims, kind=jnp.float32):
    out = lax.dot_general(a, b, (dims, ((), ())), preferred_element_type=jnp.float32)
    return out.astype(kind)


def rms_scale(values):
    return lax.rsqrt(jnp.mean(values * values, axis=-1, keepdims=True) + NORM_EPS)


def swish(values):
    return values * jax.nn.sigmoid(values)


def swish_slope(values):
    sigmoid_val = jax.nn.sigmoid(values)
    return sigmoid_val * (1.0 + values * (1.0 - sigmoid_val))


def logarithmic_sigmoid(values):
    return jnp.minimum(values, 0.0) - jnp.log1p(jnp.exp(-jnp.abs(values)))


def plus(a, b):
    return (a.astype(jnp.float32) + b.astype(jnp.float32)).astype(a.dtype)


def behind(value, *others):
    return lax.optimization_barrier((value, others))[0]


def tn_pair_kernel(a_ref, b_ref, c_ref, d_ref, e_ref, f_ref, out_ref):
    first, width = dot(a_ref[...], b_ref[...], TN), b_ref.shape[1]
    if e_ref.shape[1] == 1:
        extra = e_ref[...] * f_ref[...]
        out_ref[:, : width - 128] = first[:, : width - 128].astype(jnp.bfloat16)
        out_ref[:, width - 128 : width] = (first[:, width - 128 :] + extra).astype(jnp.bfloat16)
    else:
        out_ref[:, :width] = first.astype(jnp.bfloat16)
    out_ref[:, width:] = dot(c_ref[...], d_ref[...], TN, jnp.bfloat16)


def tn_pair(a, b, c, d, block, e=None, f=None):
    length, rows = a.shape
    cols = b.shape[1] + d.shape[1]
    if e is None:
        e, f = jnp.zeros((rows, 128), jnp.float32), jnp.zeros((1, 128), jnp.float32)
    whole = lambda v: pl.BlockSpec(v.shape, lambda i: (0, 0))
    strip = pl.BlockSpec((length, block), lambda i: (0, i))
    return pl.pallas_call(
        tn_pair_kernel,
        grid=(rows // block,),
        in_specs=[strip, whole(b), strip, whole(d), pl.BlockSpec((block, e.shape[1]), lambda i: (i, 0)), whole(f)],
        out_specs=pl.BlockSpec((block, cols), lambda i: (i, 0)),
        out_shape=jax.ShapeDtypeStruct((rows, cols), jnp.bfloat16),
        cost_estimate=pl.CostEstimate(flops=2 * length * rows * cols, bytes_accessed=2 * rows * cols, transcendentals=0),
        compiler_params=pltpu.CompilerParams(vmem_limit_bytes=48 * 2**20),
    )(a, b, c, d, e, f)


def hidden_kernel(width, x_ref, y_ref, w_ref, hid_ref, grad_ref, acc):
    step = pl.program_id(0)

    @pl.when(step == 0)
    def _():
        acc[...] = jnp.zeros_like(acc)

    acc[:, : 2 * width] += dot(x_ref[...], w_ref[:, : 2 * width], NN)
    acc[:, 2 * width :] += dot(y_ref[...], w_ref[:, 2 * width : 3 * width], NN)

    @pl.when(step == pl.num_programs(0) - 1)
    def _():
        gate, up, back = acc[:, :width], acc[:, width : 2 * width], acc[:, 2 * width :]
        sig = jax.nn.sigmoid(gate)
        act = gate * sig
        hid_ref[...] = (act * up).astype(jnp.bfloat16)
        grad_ref[:, :width] = (back * up * (sig * (1.0 + gate * (1.0 - sig)))).astype(jnp.bfloat16)
        grad_ref[:, width:] = (back * act).astype(jnp.bfloat16)


def hidden_and_grads(x, y, weights, width, cols, block):
    length, depth = x.shape
    strip = pl.BlockSpec((length, block), lambda i: (0, i))
    return pl.pallas_call(
        functools.partial(hidden_kernel, width),
        grid=(depth // block,),
        in_specs=[strip, strip, pl.BlockSpec((block, cols), lambda i: (i, 0))],
        out_specs=[pl.BlockSpec((length, n * width), lambda i: (0, 0)) for n in (1, 2)],
        out_shape=[jax.ShapeDtypeStruct((length, n * width), jnp.bfloat16) for n in (1, 2)],
        scratch_shapes=[pltpu.VMEM((length, 3 * width), jnp.float32)],
        cost_estimate=pl.CostEstimate(flops=6 * length * depth * width, bytes_accessed=6 * depth * width, transcendentals=0),
        compiler_params=pltpu.CompilerParams(vmem_limit_bytes=56 * 2**20),
    )(x, y, weights)


class Layout:
    def __init__(self, phases):
        self.seqs, self.span, self.phases = lax.axis_size("seqs"), lax.axis_size("span"), phases
        self.ranks = self.span // phases
        self.half = self.ranks // phases
        place = lax.axis_index("span")
        self.rank, self.phase = place // phases, place % phases
        self.slot = (self.rank % self.half) * phases + self.phase
        self.groups = [
            [s * self.span + z * phases + c for s in range(self.seqs) for c in range(phases)]
            for z in range(self.ranks)
        ]

    def across(self, value, k):
        step = k * self.phases
        return lax.ppermute(value, "span", [(i, i ^ step) for i in range(self.span)])

    def outward(self, k):
        pairs = []
        for i in range(self.span):
            z, c = divmod(i, self.phases)
            slot = (z % self.half) * self.phases + c
            pairs.append((i, (slot ^ k) * self.phases + z // self.half))
        return pairs

    def swap(self, value):
        mine = lax.dynamic_index_in_dim(value, self.phase, 0, False)
        other = lax.dynamic_index_in_dim(value, 1 - self.phase, 0, False)
        got = lax.ppermute(other, "span", [(i, i ^ 1) for i in range(self.span)])
        first = self.phase == 0
        return jnp.stack([jnp.where(first, mine, got), jnp.where(first, got, mine)])

    def between(self, value, pairs):
        p = self.phases
        return lax.ppermute(value, "span", [(a * p + c, b * p + c) for a, b in pairs for c in range(p)])

    def spread_near(self, value, step=1):
        if self.ranks != 4:
            return [self.across(value, k) for k in range(step, self.ranks, step)]
        return [self.across(value, 1), self.between(value, [(1, 2), (2, 1)])]

    def spread_far(self, got):
        if self.ranks != 4:
            return got
        near, middle = behind(got)
        inner = self.between(near, [(1, 2), (2, 1)])
        outer = self.between(middle, [(1, 0), (2, 3)])
        inner, outer = behind([inner, outer])
        last = self.between(inner, [(1, 0), (2, 3)])
        end = (self.rank == 0) | (self.rank == 3)
        return [near, jnp.where(end, outer, inner), jnp.where(end, last, middle)]

    def in_order(self, pieces, first, axis=0):
        size = pieces[0].shape[axis]
        shape = list(pieces[0].shape)
        shape[axis] = len(pieces) * size
        out = jnp.zeros(shape, pieces[0].dtype)
        for k, piece in enumerate(pieces):
            out = lax.dynamic_update_slice_in_dim(out, piece, (first ^ k) * size, axis)
        return out

    def gather(self, value):
        return self.in_order([value] + self.spread_far(self.spread_near(value)), self.rank)

    def piece(self, value, k):
        size = value.shape[0] // self.ranks
        return lax.dynamic_slice_in_dim(value, (self.rank ^ k) * size, size, 0)

    def split(self, value):
        return [self.piece(value, k) for k in range(self.ranks)]

    def sum_far(self, pieces):
        if self.ranks != 4:
            return [self.across(pieces[k], k) for k in range(1, self.ranks)]
        return [self.between(pieces[3], [(0, 1), (3, 2)])]

    def sum_middle(self, pieces, got):
        if self.ranks != 4:
            return got
        inner = self.between(plus(pieces[2], got[0]), [(1, 2), (2, 1)])
        outer = self.between(pieces[2], [(0, 1), (3, 2)])
        return behind([inner, outer])

    def sum_near(self, pieces, got):
        if self.ranks != 4:
            return got
        inner, outer = got
        return [self.across(plus(pieces[1], inner), 1), self.between(plus(pieces[3], outer), [(1, 2), (2, 1)])]

    def total(self, pieces, got):
        out = pieces[0].astype(jnp.float32)
        for piece in got:
            out = out + piece.astype(jnp.float32)
        return out

    def deal(self, blocks, *gates):
        pieces = []
        for k in range(self.ranks):
            block = lax.dynamic_index_in_dim(blocks, self.slot ^ k, 0, False) if blocks.shape[0] > 1 else blocks[0]
            pieces.append(lax.ppermute(block, "span", self.outward(k)))
        return self.in_order(behind(pieces, *gates), self.rank)

    def home(self, rows_of, step=1):
        blocks = rows_of.reshape(self.ranks, -1, rows_of.shape[1])
        pieces = []
        for k in range(0, self.ranks, step):
            block = lax.dynamic_index_in_dim(blocks, self.rank ^ k, 0, False)
            pieces.append(lax.ppermute(block, "span", [(b, a) for a, b in self.outward(k)]))
        return pieces

    def fetch(self, value):
        return lax.all_gather(value, ("seqs", "span"), axis=0, tiled=True, axis_index_groups=self.groups)

    def share(self, value):
        return lax.psum_scatter(
            value, ("seqs", "span"), scatter_dimension=0, tiled=True, axis_index_groups=self.groups
        )


def segment_ids(lengths_row, count):
    offsets = jnp.cumsum(lengths_row) - lengths_row
    positions = jnp.arange(count, dtype=jnp.int32)
    return jnp.sum((positions[:, None] >= offsets[None, 1:]).astype(jnp.int32), axis=1)


def local(tokens, attn_weight, mlp_weight, norm1_gain, norm2_gain, gate_bias, lengths, cotangent):
    phases, block_len, width = tokens.shape[1:]
    at = Layout(phases)
    rows = attn_weight.shape[0]
    ranks, copies = at.ranks, at.ranks // HEADS
    proj_cols = 3 * width + HEADS * SLOTS
    share_ff = FF // ranks
    qkv = 3 * HEAD_DIM
    gate_end = qkv + SLOTS
    bias_len = gate_bias.shape[0]
    head = at.rank // copies

    def by_head(part, inner):
        return part.reshape(rows, -1, HEADS, inner).transpose(2, 0, 1, 3).reshape(HEADS, rows, -1)

    extra = jnp.zeros((rows, SLOTS), jnp.bfloat16)
    extra = extra.at[0, :bias_len].set(gate_bias).at[1, :rows].set(norm1_gain).at[2, :rows].set(norm2_gain)
    in_blocks = jnp.concatenate(
        [
            by_head(attn_weight[:, : 3 * width], HEAD_DIM),
            by_head(attn_weight[:, 3 * width : proj_cols], SLOTS),
            jnp.broadcast_to(extra, (HEADS, rows, SLOTS)),
        ],
        axis=2,
    )
    rest = at.swap(tokens[0]).reshape(-1, width)
    dy = at.swap(cotangent[0]).reshape(-1, width)
    mlp_blocks = mlp_weight.reshape(rows, 3, ranks, share_ff).transpose(2, 0, 1, 3).reshape(ranks, rows, -1)
    in_dealt = at.deal(jnp.repeat(in_blocks, copies, axis=0), rest, dy, mlp_blocks)
    w_in = at.fetch(in_dealt)
    late_blocks = jnp.concatenate(
        [mlp_blocks, jnp.broadcast_to(attn_weight[:, proj_cols:], (ranks, rows, width))], axis=2
    )
    late_dealt = at.deal(behind(late_blocks, in_dealt))
    w_late = at.fetch(behind(late_dealt, w_in))
    w_gate_up, w_down = w_late[:, : 2 * share_ff], w_late[:, 2 * share_ff : 3 * share_ff]
    w_out = w_late[:, 3 * share_ff :]
    x_all = at.gather(behind(rest, late_dealt))

    extras = w_in.reshape(-1, rows, w_in.shape[1])[:, :3, gate_end:]
    bias = lax.dynamic_slice_in_dim(extras[:, 0, :bias_len].reshape(-1), head * SLOTS, SLOTS, 0)
    gain_one = extras[:, 1, :rows].reshape(-1).astype(jnp.float32)
    gain_two = extras[:, 2, :rows].reshape(-1).astype(jnp.float32)

    x_float = x_all.astype(jnp.float32)
    in_one = (x_float * rms_scale(x_float) * gain_one).astype(jnp.bfloat16)
    projected = dot(in_one, w_in, NN)
    pre = projected[:, :qkv]
    feats = swish(pre).astype(jnp.bfloat16)
    q, k, v = feats[:, :HEAD_DIM], feats[:, HEAD_DIM : 2 * HEAD_DIM], feats[:, 2 * HEAD_DIM :]
    hf = projected[:, qkv:gate_end] + bias.astype(jnp.float32)
    gate = logarithmic_sigmoid(hf) / GATE_SOFTENING
    write = -jnp.expm1(gate)
    lengths_row = lax.dynamic_index_in_dim(lengths[0], at.phase, 0, False)
    seg = segment_ids(lengths_row, x_all.shape[0])
    dy_near = at.spread_near(behind(dy, x_all))
    low, *saved = forward_mix(q, k, v, gate, write, seg)
    low_near = at.spread_near(behind(low, dy_near), copies)
    low_all = at.in_order([low] + at.spread_far(low_near), head, 1)

    dy_far = at.spread_far(behind(dy_near, low_all))
    after_all = x_float + dot(low_all, w_out, NT)
    in_two = (after_all * rms_scale(after_all) * gain_two).astype(jnp.bfloat16)
    after = at.piece(after_all, 0)
    scale_two = rms_scale(after)
    normed_two = after * scale_two

    dyl = at.in_order([dy] + dy_far, at.rank)
    mlp_cols = 3 * share_ff if share_ff % 128 == 0 else w_late.shape[1]
    hidden, grad_gate_up = hidden_and_grads(in_two, dyl, w_late, share_ff, mlp_cols, 512)
    two_part = dot(grad_gate_up, w_gate_up, NT, jnp.bfloat16)
    two_pieces = at.split(two_part)
    two_far = at.sum_far(two_pieces)
    hidden_later, grad_later = behind((hidden, grad_gate_up), two_pieces)
    grad_mlp_w = tn_pair(in_two, grad_later, dyl, hidden_later, 256)
    share_mlp = at.share(grad_mlp_w)
    two_middle = at.sum_middle(two_pieces, behind(two_far, grad_mlp_w))
    mlp_part = dot(behind(hidden, grad_mlp_w), w_down, NT, jnp.bfloat16)
    two_near = at.sum_near(two_pieces, behind(two_middle, mlp_part))
    back_two = at.total(two_pieces, two_near)
    scaled_two = back_two * gain_two

    grad_after = dy.astype(jnp.float32) + scale_two * (
        scaled_two - normed_two * jnp.mean(scaled_two * normed_two, axis=1, keepdims=True)
    )
    dal = at.gather(grad_after.astype(jnp.bfloat16))
    mlp_pieces = at.split(behind(mlp_part, dal))
    mlp_far = at.sum_far(mlp_pieces)

    w_out_head = lax.dynamic_slice_in_dim(w_late, 3 * share_ff + head * HEAD_DIM, HEAD_DIM, 1)
    don = dot(behind(dal, mlp_pieces), w_out_head, NN)
    dq, dk, dv, dgate = backward_mix(q, k, v, gate, write, seg, saved, don)
    grad_pre = (jnp.concatenate([dq, dk, dv], axis=1) * swish_slope(pre)).astype(jnp.bfloat16)
    grad_hf = (dgate * jax.nn.sigmoid(-hf) / GATE_SOFTENING).astype(jnp.bfloat16)
    grad_proj = jnp.concatenate([grad_pre, grad_hf, jnp.zeros_like(grad_hf)], axis=1)
    bias_grad = jnp.sum(grad_hf.astype(jnp.float32), axis=0)
    bias_grad = jnp.concatenate([jnp.zeros((gate_end,), jnp.float32), bias_grad])
    row_ids = jnp.arange(width, dtype=jnp.int32)
    owners = SLOTS // bias_len
    holds = ((row_ids % rows == 0) & (row_ids // (rows * owners) == head)).astype(jnp.float32)
    mlp_middle = at.sum_middle(mlp_pieces, behind(mlp_far, grad_proj))
    grad_proj = behind(grad_proj, mlp_far)
    grad_attn_w = tn_pair(in_one, grad_proj, dal, low, 512, holds[:, None], bias_grad[None, -128:])
    share_attn = at.share(behind(grad_attn_w, share_mlp))
    one_part = dot(behind(grad_proj, grad_attn_w), w_in, NT, jnp.bfloat16)
    one_pieces = at.split(one_part)
    mlp_near = at.sum_near(mlp_pieces, behind(mlp_middle, grad_attn_w))
    one_far = at.sum_far(behind(one_pieces, mlp_middle))
    one_middle = at.sum_middle(one_pieces, one_far)
    mlp_out = at.total(mlp_pieces, behind(mlp_near, one_far))
    mixed_rows = (after + mlp_out).astype(jnp.bfloat16)
    mixed = at.swap(mixed_rows.reshape(phases, block_len, width))[None]
    one_near = at.sum_near(one_pieces, one_middle)
    back_one = at.total(one_pieces, one_near) / copies
    scaled_one = back_one * gain_one
    rest_float = rest.astype(jnp.float32)
    scale_one = rms_scale(rest_float)
    normed_one = rest_float * scale_one
    grad_rows = grad_after + scale_one * (
        scaled_one - normed_one * jnp.mean(scaled_one * normed_one, axis=1, keepdims=True)
    )
    grad_tokens = at.swap(grad_rows.reshape(phases, block_len, width))[None]

    mlp_home = at.home(behind(share_mlp, back_one))
    attn_home = at.home(share_attn, copies)

    gate_up_weight = mlp_weight[:, : 2 * FF].astype(jnp.float32)
    down = at.in_order([p[:, 2 * share_ff :] for p in mlp_home], at.slot, 1).astype(jnp.float32)
    gates = at.in_order([p[:, :share_ff] for p in mlp_home], at.slot, 1).astype(jnp.float32)
    ups = at.in_order([p[:, share_ff : 2 * share_ff] for p in mlp_home], at.slot, 1).astype(jnp.float32)
    grad_mlp = jnp.concatenate([gates, ups, down], axis=1)
    gain_grad_two = jnp.sum(grad_mlp[:, : 2 * FF] * gate_up_weight, axis=1) / norm2_gain.astype(jnp.float32)

    slot_head = at.slot // copies
    parts = [
        at.in_order([p[:, j * HEAD_DIM : (j + 1) * HEAD_DIM] for p in attn_home], slot_head, 1) for j in range(3)
    ]
    parts.append(at.in_order([p[:, qkv:gate_end] for p in attn_home], slot_head, 1))
    parts.append(at.in_order([p[:, gate_end + SLOTS :] for p in attn_home], slot_head, 1))
    grad_attn = jnp.concatenate(parts, axis=1).astype(jnp.float32)
    attn_float = attn_weight[:, :proj_cols].astype(jnp.float32)
    gain_grad_one = jnp.sum(grad_attn[:, :proj_cols] * attn_float, axis=1) / norm1_gain.astype(jnp.float32)
    bias_sums = sum(p[0, gate_end : gate_end + SLOTS].astype(jnp.float32) for p in attn_home)
    owner = lax.axis_index("seqs") * at.span + lax.axis_index("span")
    bias_home = lax.dynamic_slice_in_dim(bias_sums, owner % owners * bias_len, bias_len, 0)
    return (mixed, grad_tokens, grad_attn, grad_mlp, gain_grad_one, gain_grad_two, bias_home)


def solution(mesh):
    placed = (
        P("seqs", None, "span", None),
        P(("seqs", "span"), None),
        P(("seqs", "span"), None),
        P(("seqs", "span")),
        P(("seqs", "span")),
        P(("seqs", "span")),
        P("seqs", None, None),
        P("seqs", None, "span", None),
    )
    return jax.shard_map(
        local,
        mesh=mesh,
        in_specs=placed,
        out_specs=(
            P("seqs", None, "span", None),
            P("seqs", None, "span", None),
            P(("seqs", "span"), None),
            P(("seqs", "span"), None),
            P(("seqs", "span")),
            P(("seqs", "span")),
            P(("seqs", "span")),
        ),
        check_vma=False,
    )
```

```python
import functools
import jax
import jax.numpy as jnp
from jax import lax
from jax.experimental import pallas as pl
from jax.experimental.pallas import tpu as pltpu
from jax.sharding import PartitionSpec as P

BLOCK = 64
GATE_SOFTENING = 8.0
SUB = 16
SLOTS = 64
HEAD_DIM = 512
NORM_EPS = 1e-05


def mm(a, b, dims):
    return lax.dot_general(
        a.astype(jnp.bfloat16), b.astype(jnp.bfloat16), (dims, ((), ())), preferred_element_type=jnp.float32
    )


def halves(a):
    if a.dtype == jnp.bfloat16:
        return a, None
    high = a.astype(jnp.bfloat16)
    return high, (a - high.astype(jnp.float32)).astype(jnp.bfloat16)


def fine(a, b, dims):
    (a_high, a_low), (b_high, b_low) = halves(a), halves(b)
    out = mm(a_high, b_high, dims)
    if b_low is not None:
        out = out + mm(a_high, b_low, dims)
    if a_low is not None:
        out = out + mm(a_low, b_high, dims)
    return out


NN, NT, TN = ((1,), (0,)), ((1,), (1,)), ((0,), (0,))


def nn(a, b):
    return mm(a, b, NN)


def nt(a, b):
    return mm(a, b, NT)


def tn(a, b):
    return mm(a, b, TN)


def exact(a, b):
    return lax.dot_general(
        a, b, (((1,), (0,)), ((), ())), precision=lax.Precision.HIGHEST, preferred_element_type=jnp.float32
    )


def iota(shape, dim):
    return lax.broadcasted_iota(jnp.int32, shape, dim)


def block_decay(gate, write, seg_col, seg_row, seg_prev):
    row, col = iota((BLOCK, BLOCK), 0), iota((BLOCK, BLOCK), 1)
    same = jnp.where((seg_col == seg_row) & (row >= col), 1.0, 0.0)
    lower = jnp.where(row >= col, 1.0, 0.0)
    cum = exact(lower, gate)
    total = cum[BLOCK - 1 :]
    carry = jnp.where(seg_col == seg_prev, 1.0, 0.0)
    last = jnp.where(seg_col == seg_col[BLOCK - 1 :], 1.0, 0.0)
    enter = jnp.exp(cum) * carry
    tail = jnp.exp(total - cum) * last
    fade = jnp.exp(total) * carry[BLOCK - 1 :]
    falls, rises = [], []
    for i in range(1, BLOCK // SUB):
        base = cum[i * SUB - 1 : i * SUB]
        falls.append(jnp.exp(cum[i * SUB : (i + 1) * SUB] - base))
        rises.append(jnp.exp(base - cum[: i * SUB]))
    return same, cum, enter, tail, fade, falls, rises


def diagonal(square):
    return jnp.concatenate([square[i : i + SUB, i : i + SUB] for i in range(0, BLOCK, SUB)], axis=0)


def undiagonal(strip):
    row, col = iota((BLOCK, BLOCK), 0), iota((BLOCK, BLOCK), 1)
    wide = jnp.concatenate([strip] * (BLOCK // SUB), axis=1)
    return jnp.where(row // SUB == col // SUB, wide, 0.0)


def parts(values):
    return values.reshape(BLOCK // SUB, SUB, values.shape[-1])


def decay_at(cum, j):
    cum_parts = parts(cum)
    return jnp.exp(jnp.minimum(cum_parts - cum_parts[:, j : j + 1], 0.0))


def over_sources(pairs, cum, write, falls, rises):
    strip = parts(diagonal(pairs))
    write_parts = parts(write)
    near = jnp.zeros((BLOCK // SUB, SUB, SLOTS), jnp.float32)
    for j in range(SUB):
        near = near + strip[:, :, j : j + 1] * (decay_at(cum, j) * write_parts[:, j : j + 1])
    near = near.reshape(BLOCK, SLOTS)
    far = [jnp.zeros((SUB, SLOTS), jnp.float32)]
    for i in range(1, BLOCK // SUB):
        rows = pairs[i * SUB : (i + 1) * SUB, : i * SUB]
        far.append(falls[i - 1] * fine(rows, rises[i - 1] * write[: i * SUB], NN))
    return near + jnp.concatenate(far, axis=0)


def over_slots(values, cum, write, falls, rises):
    value_parts, write_parts = parts(values), parts(write)
    lane = iota((BLOCK // SUB, SUB, SUB), 2)
    strip = jnp.zeros((BLOCK // SUB, SUB, SUB), jnp.float32)
    for j in range(SUB):
        term = value_parts * (decay_at(cum, j) * write_parts[:, j : j + 1])
        strip = jnp.where(lane == j, jnp.sum(term, axis=2, keepdims=True), strip)
    out = undiagonal(strip.reshape(BLOCK, SUB))
    far = [jnp.zeros((SUB, BLOCK), jnp.float32)]
    for i in range(1, BLOCK // SUB):
        rows = values[i * SUB : (i + 1) * SUB] * falls[i - 1]
        piece = fine(rows, rises[i - 1] * write[: i * SUB], NT)
        far.append(jnp.concatenate([piece, jnp.zeros((SUB, BLOCK - i * SUB), jnp.float32)], axis=1))
    return out + jnp.concatenate(far, axis=0)


def over_targets(pairs_values, cum, falls, rises):
    row = iota((BLOCK // SUB, SUB, SLOTS), 1)
    near = jnp.zeros((BLOCK // SUB, SUB, SLOTS), jnp.float32)
    strips = [(parts(diagonal(p)), parts(v)) for p, v in pairs_values]
    for j in range(SUB):
        term = sum(strip[:, :, j : j + 1] * value for strip, value in strips) * decay_at(cum, j)
        near = jnp.where(row == j, jnp.sum(term, axis=1, keepdims=True), near)
    out = near.reshape(BLOCK, SLOTS)
    far = jnp.zeros((BLOCK, SLOTS), jnp.float32)
    for i in range(1, BLOCK // SUB):
        here = slice(i * SUB, (i + 1) * SUB)
        piece = sum(fine(p[here, : i * SUB], v[here] * falls[i - 1], TN) for p, v in pairs_values)
        piece = rises[i - 1] * piece
        far = far + jnp.concatenate([piece, jnp.zeros((BLOCK - i * SUB, SLOTS), jnp.float32)], axis=0)
    return out + far


QKV = 3 * HEAD_DIM
GATE_END = QKV + SLOTS


def load_block(i, proj_ref, bias_ref, segc_ref, segr_ref):
    here = pl.ds(pl.multiple_of(i * BLOCK, BLOCK), BLOCK)
    pre = proj_ref[here, :QKV]
    sig = jax.nn.sigmoid(pre)
    feats = (pre * sig).astype(jnp.bfloat16)
    q, k, v = (feats[:, n * HEAD_DIM : (n + 1) * HEAD_DIM] for n in range(3))
    logits = proj_ref[here, QKV:GATE_END] + bias_ref[...]
    gate = (jnp.minimum(logits, 0.0) - jnp.log1p(jnp.exp(-jnp.abs(logits)))) / GATE_SOFTENING
    seg_prev = jnp.where(i > 0, segc_ref[pl.ds(jnp.maximum(i * BLOCK - 1, 0), 1), :], -1)
    return here, pre, sig, q, k, v, logits, gate, -small_exp(gate), segc_ref[here, :], segr_ref[i], seg_prev


def small_exp(x):
    near = x * (1.0 + x / 2 * (1.0 + x / 3 * (1.0 + x / 4 * (1.0 + x / 5 * (1.0 + x / 6)))))
    return jnp.where(x > -0.1, near, jnp.exp(x) - 1.0)


def forward_kernel(proj_ref, bias_ref, segc_ref, segr_ref, low_ref, out_hbm, small_hbm, states_hbm,
                   out_ref, small_ref, states_ref, state, sems):
    scale = HEAD_DIM ** -0.5
    blocks = proj_ref.shape[0] // BLOCK
    state[...] = jnp.zeros_like(state)

    def copies(i):
        here = pl.ds(pl.multiple_of(i * BLOCK, BLOCK), BLOCK)
        return [
            pltpu.make_async_copy(a, b, sems.at[n, i])
            for n, (a, b) in enumerate(
                [
                    (out_ref.at[here], out_hbm.at[here]),
                    (small_ref.at[here], small_hbm.at[here]),
                    (states_ref.at[i], states_hbm.at[i]),
                ]
            )
        ]

    def step(i, _):
        here, _, _, q, k, v, _, gate, write, seg_col, seg_row, seg_prev = load_block(i, proj_ref, bias_ref, segc_ref, segr_ref)
        same, cum, enter, tail, fade, falls, rises = block_decay(gate, write, seg_col, seg_row, seg_prev)
        keys_in, values_in = state[:SLOTS], state[SLOTS:]
        states_ref[i] = state[...]
        keep = fade.reshape(SLOTS, 1)
        send = tail * write
        state[:SLOTS] = keep * keys_in + tn(send, k)
        state[SLOTS:] = keep * values_in + fine(send, v, TN)
        pairs = nt(q, k) * same
        score = scale * (over_sources(pairs, cum, write, falls, rises) + enter * nt(q, keys_in))
        prob = jnp.exp(score - jnp.max(score, axis=1, keepdims=True))
        prob = prob / jnp.sum(prob, axis=1, keepdims=True)
        mix = over_slots(prob, cum, write, falls, rises) * same
        out = fine(mix, v, NN) + fine(prob * enter, values_in, NN)
        low_ref[here, :] = (out * lax.rsqrt(jnp.mean(out * out, axis=1, keepdims=True) + NORM_EPS)).astype(jnp.bfloat16)
        out_ref[here, :] = out
        small_ref[here, :] = jnp.concatenate([score, prob, pairs, mix], axis=1)
        for copy in copies(i):
            copy.start()
        return 0

    lax.fori_loop(0, blocks, step, 0, unroll=4)

    def finish(i, _):
        for copy in copies(i):
            copy.wait()
        return 0

    lax.fori_loop(0, blocks, finish, 0)


def backward_kernel(proj_ref, bias_ref, segc_ref, segr_ref, out_ref, small_ref, states_ref, don_ref,
                    grad_ref, bias_grad_ref, state, state_next):
    scale = HEAD_DIM ** -0.5
    blocks = proj_ref.shape[0] // BLOCK
    state[...] = jnp.zeros_like(state)
    state_next[...] = jnp.zeros_like(state)
    bias_grad_ref[...] = jnp.zeros_like(bias_grad_ref)

    def step(lap, _):
        i = blocks - 1 - lap
        here, pre, sig, q, k, v, logits, gate, write, seg_col, seg_row, seg_prev = load_block(i, proj_ref, bias_ref, segc_ref, segr_ref)
        same, cum, enter, tail, fade, falls, rises = block_decay(gate, write, seg_col, seg_row, seg_prev)
        last = jnp.where(seg_col == seg_col[BLOCK - 1 :], 1.0, 0.0)
        score, prob, pairs, mix = (small_ref[here, n * SLOTS : (n + 1) * SLOTS] for n in range(4))
        states_in = states_ref[i]
        keys_in, values_in = states_in[:SLOTS], states_in[SLOTS:]
        out, don = out_ref[here, :], don_ref[here, :]
        unit = lax.rsqrt(jnp.mean(out * out, axis=1, keepdims=True) + NORM_EPS)
        normed = out * unit
        dout = unit * (don - normed * jnp.mean(don * normed, axis=1, keepdims=True))
        dmix = fine(dout, v, NT) * same
        dprob = over_sources(dmix, cum, write, falls, rises) + enter * fine(dout, values_in, NT)
        inner = prob * dprob
        dscore = inner - prob * jnp.sum(inner, axis=1, keepdims=True)
        slope = scale * dscore
        dpairs = over_slots(slope, cum, write, falls, rises) * same
        dcross = slope * enter
        dstate = state[...]
        dkeys, dvalues = dstate[:SLOTS], dstate[SLOTS:]
        send = tail * write
        dfeats = jnp.concatenate(
            [
                nn(dpairs, k) + nn(dcross, keys_in),
                tn(dpairs, q) + nn(send, dkeys),
                tn(mix, dout) + nn(send, dvalues),
            ],
            axis=1,
        )
        grad_ref[here, :QKV] = (dfeats * (sig * (1.0 + pre * (1.0 - sig)))).astype(jnp.bfloat16)
        heard = over_targets([(pairs, slope), (dmix, prob)], cum, falls, rises)
        heard = heard + tail * (nt(k, dkeys) + nt(v, dvalues))
        product = dstate * state_next[...]
        held = lax.dot_general(jnp.ones((8, HEAD_DIM), jnp.float32), product[:SLOTS] + product[SLOTS:],
                               (((1,), (1,)), ((), ())), precision=lax.Precision.HIGHEST, preferred_element_type=jnp.float32)[:1]
        flow = exact(same.T, dscore * score + inner - write * heard)
        dgate = flow - (1.0 - write) * heard + last * held
        dlogits = (dgate * jax.nn.sigmoid(-logits) / GATE_SOFTENING).astype(jnp.bfloat16)
        grad_ref[here, QKV:] = jnp.concatenate([dlogits, jnp.zeros_like(dlogits)], axis=1)
        bias_grad_ref[...] += jnp.sum(dlogits.astype(jnp.float32), axis=0, keepdims=True)
        keep = fade.reshape(SLOTS, 1)
        state[:SLOTS] = keep * dkeys + tn(dcross, q)
        state[SLOTS:] = keep * dvalues + fine(prob * enter, dout, TN)
        state_next[...] = states_in
        return 0

    lax.fori_loop(0, blocks, step, 0)


VMEM = pl.BlockSpec(memory_space=pltpu.VMEM)


def slot_call(kernel, outs, out_specs, scratch, args, cost):
    return pl.pallas_call(
        kernel,
        out_shape=outs,
        in_specs=[VMEM] * len(args),
        out_specs=out_specs,
        scratch_shapes=scratch,
        cost_estimate=pl.CostEstimate(flops=cost, bytes_accessed=0, transcendentals=0),
        compiler_params=pltpu.CompilerParams(vmem_limit_bytes=58 * 2**20),
    )(*args)


def forward_mix(proj, bias, seg):
    length = proj.shape[0]
    blocks = length // BLOCK
    shapes = [(length, HEAD_DIM), (length, 4 * SLOTS), (blocks, 2 * SLOTS, HEAD_DIM)]
    outs = [jax.ShapeDtypeStruct((length, HEAD_DIM), jnp.bfloat16)] + [jax.ShapeDtypeStruct(n, jnp.float32) for n in shapes]
    specs = [VMEM] + [pl.BlockSpec(memory_space=pltpu.HBM)] * 3
    scratch = [pltpu.VMEM(n, jnp.float32) for n in shapes]
    scratch += [pltpu.VMEM((2 * SLOTS, HEAD_DIM), jnp.float32), pltpu.SemaphoreType.DMA((3, blocks))]
    args = (proj, bias.reshape(1, SLOTS), seg.reshape(length, 1), seg.reshape(blocks, 1, BLOCK))
    return slot_call(forward_kernel, outs, specs, scratch, args, 12 * 10**9)


def backward_mix(proj, bias, seg, saved, don):
    length = proj.shape[0]
    blocks = length // BLOCK
    outs = [jax.ShapeDtypeStruct(proj.shape, jnp.bfloat16), jax.ShapeDtypeStruct((1, SLOTS), jnp.float32)]
    scratch = [pltpu.VMEM((2 * SLOTS, HEAD_DIM), jnp.float32)] * 2
    args = (proj, bias.reshape(1, SLOTS), seg.reshape(length, 1), seg.reshape(blocks, 1, BLOCK), *saved, don)
    return slot_call(backward_kernel, outs, [VMEM] * 2, scratch, args, 16 * 10**9)


HEADS = 4
FF = 5632


def dot(a, b, dims, kind=jnp.float32):
    out = lax.dot_general(a, b, (dims, ((), ())), preferred_element_type=jnp.float32)
    return out.astype(kind)


def rms_scale(values):
    return lax.rsqrt(jnp.mean(values * values, axis=-1, keepdims=True) + NORM_EPS)


def plus(a, b):
    return (a.astype(jnp.float32) + b.astype(jnp.float32)).astype(a.dtype)


def behind(value, *others):
    return lax.optimization_barrier((value, others))[0]


def tn_pair_kernel(a_ref, b_ref, c_ref, d_ref, out_ref):
    width = b_ref.shape[1]
    out_ref[:, :width] = dot(a_ref[...], b_ref[...], TN, jnp.bfloat16)
    out_ref[:, width:] = dot(c_ref[...], d_ref[...], TN, jnp.bfloat16)


def tn_kernel(a_ref, b_ref, out_ref):
    out_ref[...] = dot(a_ref[...], b_ref[...], TN, jnp.bfloat16)


def tn_extra_kernel(a_ref, b_ref, e_ref, f_ref, out_ref):
    out, last = dot(a_ref[...], b_ref[...], TN), b_ref.shape[1] - 128
    out_ref[:, :last] = out[:, :last].astype(jnp.bfloat16)
    out_ref[:, last:] = (out[:, last:] + e_ref[...] * f_ref[...]).astype(jnp.bfloat16)


def weight_grads(kernel, block, *operands):
    length, rows = operands[0].shape
    cols = sum(v.shape[1] for v in operands[1:4:2]) if kernel is tn_pair_kernel else operands[1].shape[1]
    whole = lambda v: pl.BlockSpec(v.shape, lambda i: (0, 0))
    strip = pl.BlockSpec((length, block), lambda i: (0, i))
    specs = [strip, whole(operands[1])]
    if kernel is tn_pair_kernel:
        specs += [strip, whole(operands[3])]
    elif kernel is tn_extra_kernel:
        specs += [pl.BlockSpec((block, 1), lambda i: (i, 0)), whole(operands[3])]
    return pl.pallas_call(
        kernel,
        grid=(rows // block,),
        in_specs=specs,
        out_specs=pl.BlockSpec((block, cols), lambda i: (i, 0)),
        out_shape=jax.ShapeDtypeStruct((rows, cols), jnp.bfloat16),
        cost_estimate=pl.CostEstimate(flops=2 * length * rows * cols, bytes_accessed=2 * rows * cols, transcendentals=0),
        compiler_params=pltpu.CompilerParams(vmem_limit_bytes=48 * 2**20),
    )(*operands)


def hidden_kernel(width, x_ref, y_ref, w_ref, hid_ref, grad_ref, acc):
    step = pl.program_id(0)

    @pl.when(step == 0)
    def _():
        acc[...] = jnp.zeros_like(acc)

    acc[:, : 2 * width] += dot(x_ref[...], w_ref[:, : 2 * width], NN)
    acc[:, 2 * width :] += dot(y_ref[...], w_ref[:, 2 * width : 3 * width], NN)

    @pl.when(step == pl.num_programs(0) - 1)
    def _():
        gate, up, back = acc[:, :width], acc[:, width : 2 * width], acc[:, 2 * width :]
        sig = jax.nn.sigmoid(gate)
        act = gate * sig
        hid_ref[...] = (act * up).astype(jnp.bfloat16)
        grad_ref[:, :width] = (back * up * (sig * (1.0 + gate * (1.0 - sig)))).astype(jnp.bfloat16)
        grad_ref[:, width:] = (back * act).astype(jnp.bfloat16)


def hidden_and_grads(x, y, weights, width, cols, block):
    length, depth = x.shape
    strip = pl.BlockSpec((length, block), lambda i: (0, i))
    return pl.pallas_call(
        functools.partial(hidden_kernel, width),
        grid=(depth // block,),
        in_specs=[strip, strip, pl.BlockSpec((block, cols), lambda i: (i, 0))],
        out_specs=[pl.BlockSpec((length, n * width), lambda i: (0, 0)) for n in (1, 2)],
        out_shape=[jax.ShapeDtypeStruct((length, n * width), jnp.bfloat16) for n in (1, 2)],
        scratch_shapes=[pltpu.VMEM((length, 3 * width), jnp.float32)],
        cost_estimate=pl.CostEstimate(flops=6 * length * depth * width, bytes_accessed=6 * depth * width, transcendentals=0),
        compiler_params=pltpu.CompilerParams(vmem_limit_bytes=56 * 2**20),
    )(x, y, weights)


def place_kernel(axis, choices, place_ref, *refs):
    pieces, out_ref = refs[:-1], refs[-1]
    size = pieces[0].shape[axis]

    def put(k, piece):
        start = pl.multiple_of((place_ref[0] ^ k) * size, size)
        where = (pl.ds(start, size), slice(None)) if axis == 0 else (slice(None), pl.ds(start, size))
        out_ref[where] = piece[...]

    for k, choice in enumerate(choices):
        if len(choice) == 1:
            put(k, pieces[choice[0]])
        else:
            pl.when(place_ref[1] == 1)(functools.partial(put, k, pieces[choice[0]]))
            pl.when(place_ref[1] == 0)(functools.partial(put, k, pieces[choice[1]]))


def place_pieces(pieces, choices, first, end, axis=0):
    shape = list(pieces[0].shape)
    shape[axis] *= len(choices)
    vmem = pl.BlockSpec(memory_space=pltpu.VMEM)
    nbytes = 4 * shape[0] * shape[1]
    return pl.pallas_call(
        functools.partial(place_kernel, axis, choices),
        out_shape=jax.ShapeDtypeStruct(shape, pieces[0].dtype),
        in_specs=[pl.BlockSpec(memory_space=pltpu.SMEM)] + [vmem] * len(pieces),
        out_specs=vmem,
        cost_estimate=pl.CostEstimate(flops=0, bytes_accessed=nbytes, transcendentals=0),
        compiler_params=pltpu.CompilerParams(vmem_limit_bytes=48 * 2**20),
    )(jnp.stack([first, end]).astype(jnp.int32), *pieces)


def tokens_kernel(choices, place_ref, gain_ref, *refs):
    pieces, (x_ref, normed_ref) = refs[:-2], refs[-2:]
    size = pieces[0].shape[0]

    def put(k, piece):
        here = pl.ds(pl.multiple_of((place_ref[0] ^ k) * size, size), size)
        x_ref[here, :] = piece[...]
        values = piece[...].astype(jnp.float32)
        normed_ref[here, :] = (values * rms_scale(values) * gain_ref[...]).astype(jnp.bfloat16)

    for k, choice in enumerate(choices):
        if len(choice) == 1:
            put(k, pieces[choice[0]])
        else:
            pl.when(place_ref[1] == 1)(functools.partial(put, k, pieces[choice[0]]))
            pl.when(place_ref[1] == 0)(functools.partial(put, k, pieces[choice[1]]))


def place_tokens(pieces, choices, first, end, gain):
    size, width = pieces[0].shape
    shape = jax.ShapeDtypeStruct((len(choices) * size, width), jnp.bfloat16)
    return pl.pallas_call(
        functools.partial(tokens_kernel, choices),
        out_shape=[shape] * 2,
        in_specs=[pl.BlockSpec(memory_space=pltpu.SMEM)] + [VMEM] * (len(pieces) + 1),
        out_specs=[VMEM] * 2,
        cost_estimate=pl.CostEstimate(flops=0, bytes_accessed=10 * len(choices) * size * width, transcendentals=0),
        compiler_params=pltpu.CompilerParams(vmem_limit_bytes=48 * 2**20),
    )(jnp.stack([first, end]).astype(jnp.int32), gain, *pieces)


class Layout:
    def __init__(self, phases):
        self.seqs, self.span, self.phases = lax.axis_size("seqs"), lax.axis_size("span"), phases
        self.ranks = self.span // phases
        self.half = self.ranks // phases
        place = lax.axis_index("span")
        self.rank, self.phase = place // phases, place % phases
        self.slot = (self.rank % self.half) * phases + self.phase
        self.groups = [
            [s * self.span + z * phases + c for s in range(self.seqs) for c in range(phases)]
            for z in range(self.ranks)
        ]

    def across(self, value, k):
        step = k * self.phases
        return lax.ppermute(value, "span", [(i, i ^ step) for i in range(self.span)])

    def outward(self, k):
        pairs = []
        for i in range(self.span):
            z, c = divmod(i, self.phases)
            slot = (z % self.half) * self.phases + c
            pairs.append((i, (slot ^ k) * self.phases + z // self.half))
        return pairs

    def swap(self, value):
        mine = lax.dynamic_index_in_dim(value, self.phase, 0, False)
        other = lax.dynamic_index_in_dim(value, 1 - self.phase, 0, False)
        got = lax.ppermute(other, "span", [(i, i ^ 1) for i in range(self.span)])
        first = self.phase == 0
        return jnp.stack([jnp.where(first, mine, got), jnp.where(first, got, mine)])

    def between(self, value, pairs):
        p = self.phases
        return lax.ppermute(value, "span", [(a * p + c, b * p + c) for a, b in pairs for c in range(p)])

    def spread_near(self, value, step=1):
        if self.ranks != 4:
            return [self.across(value, k) for k in range(step, self.ranks, step)]
        return [self.across(value, 1), self.between(value, [(1, 2), (2, 1)]), self.between(value, [(0, 3), (3, 0)])]

    def spread_far(self, got):
        if self.ranks != 4:
            return got
        near, middle, ends = got
        near, middle = behind((near, middle))
        inner = self.between(near, [(1, 2), (2, 1)])
        return [near, middle, ends, inner, self.between(middle, [(1, 0), (2, 3)])]

    def choices(self, got):
        if self.ranks == 4:
            near, middle, ends, inner, outer = got
            return [near, outer, inner, ends, middle], ((0,), (1,), (2, 3), (4, 5))
        return got, tuple((k,) for k in range(len(got) + 1))

    def joined(self, own, got, axis=0, step=1):
        pieces, choices = self.choices(got)
        end = (self.rank == 0) | (self.rank == self.ranks - 1)
        return place_pieces([own, *pieces], choices, self.rank // step, end, axis)

    def dealt(self, pieces):
        return place_pieces(pieces, tuple((k,) for k in range(len(pieces))), self.rank, self.rank)

    def in_order(self, pieces, first, axis=0):
        size = pieces[0].shape[axis]
        shape = list(pieces[0].shape)
        shape[axis] = len(pieces) * size
        out = jnp.zeros(shape, pieces[0].dtype)
        for k, piece in enumerate(pieces):
            out = lax.dynamic_update_slice_in_dim(out, piece, (first ^ k) * size, axis)
        return out

    def spread(self, value):
        return behind(self.spread_far(self.spread_near(value)))

    def gather(self, value):
        return self.joined(value, self.spread(value))

    def piece(self, value, k):
        size = value.shape[0] // self.ranks
        return lax.dynamic_slice_in_dim(value, (self.rank ^ k) * size, size, 0)

    def split(self, value):
        return [self.piece(value, k) for k in range(self.ranks)]

    def sum_far(self, pieces):
        if self.ranks != 4:
            return [self.across(pieces[k], k) for k in range(1, self.ranks)]
        inner, outer = (self.between(pieces[2], pairs) for pairs in ([(1, 2), (2, 1)], [(0, 1), (3, 2)]))
        return [inner, outer, self.between(pieces[3], [(0, 3), (3, 0)])]

    def sum_near(self, pieces, got):
        if self.ranks != 4:
            return got
        inner, outer, ends = got
        inner, outer = behind((inner, outer))
        near = self.across(plus(pieces[1], inner), 1)
        return [near, self.between(plus(pieces[3], outer), [(1, 2), (2, 1)]), ends]

    def total(self, pieces, got):
        out = pieces[0].astype(jnp.float32)
        for piece in got:
            out = out + piece.astype(jnp.float32)
        return out

    def deal(self, blocks):
        return [lax.ppermute(block, "span", self.outward(k)) for k, block in enumerate(blocks)]

    def home(self, rows_of, places):
        blocks = rows_of.reshape(self.ranks, -1, rows_of.shape[1])
        pieces = []
        for k in places:
            block = lax.dynamic_index_in_dim(blocks, self.rank ^ k, 0, False)
            pieces.append(lax.ppermute(block, "span", [(b, a) for a, b in self.outward(k)]))
        return pieces

    def fetch(self, value):
        return lax.all_gather(value, ("seqs", "span"), axis=0, tiled=True, axis_index_groups=self.groups)

    def share(self, value):
        return lax.psum_scatter(
            value, ("seqs", "span"), scatter_dimension=0, tiled=True, axis_index_groups=self.groups
        )


def segment_ids(lengths_row, count):
    offsets = jnp.cumsum(lengths_row) - lengths_row
    positions = jnp.arange(count, dtype=jnp.int32)
    return jnp.sum((positions[:, None] >= offsets[None, 1:]).astype(jnp.int32), axis=1)


def local(tokens, attn_weight, mlp_weight, norm1_gain, norm2_gain, gate_bias, lengths, cotangent):
    phases, block_len, width = tokens.shape[1:]
    at = Layout(phases)
    rows = attn_weight.shape[0]
    ranks, copies = at.ranks, at.ranks // HEADS
    proj_cols = 3 * width + HEADS * SLOTS
    share_ff = FF // ranks
    qkv = 3 * HEAD_DIM
    gate_end = qkv + SLOTS
    bias_len = gate_bias.shape[0]
    head = at.rank // copies

    def columns(weight, *cuts):
        return [lax.dynamic_slice_in_dim(weight, start, size, 1) for start, size in cuts]

    extra = jnp.zeros((rows, SLOTS), jnp.bfloat16)
    extra = extra.at[0, :bias_len].set(gate_bias).at[1, :rows].set(norm1_gain).at[2, :rows].set(norm2_gain)
    in_blocks, late_blocks = [], []
    for j in range(ranks):
        to = at.slot ^ j
        cuts = [(n * width + to // copies * HEAD_DIM, HEAD_DIM) for n in range(3)]
        cuts.append((3 * width + to // copies * SLOTS, SLOTS))
        in_blocks.append(jnp.concatenate(columns(attn_weight, *cuts) + [extra], axis=1))
    for j in range(ranks):
        cuts = [(n * FF + (at.slot ^ j) * share_ff, share_ff) for n in range(3)]
        late_blocks.append(jnp.concatenate(columns(mlp_weight, *cuts), axis=1))
    in_pieces = at.deal(in_blocks)
    out_own = attn_weight[:, proj_cols:]
    out_near = at.spread_near(behind(out_own, in_blocks))

    rest = at.swap(tokens[0]).reshape(-1, width)
    dy = at.swap(cotangent[0]).reshape(-1, width)
    shard = rest.shape[0]
    in_pieces, out_near = behind((in_pieces, out_near, rest, dy, late_blocks))[:2]
    w_in = at.fetch(at.dealt(in_pieces))
    x_near = at.spread_near(behind(rest, in_pieces))
    out_got = behind(at.spread_far(out_near), x_near)
    both_got = behind(at.spread_far(x_near))
    out_rows = at.swap(at.joined(out_own, out_got).reshape(phases, at.half * rows, width))
    out_rows = out_rows.reshape(phases, at.half, rows, width).swapaxes(0, 1).reshape(-1, width)
    w_out = at.fetch(out_rows)
    late_pieces = at.deal(behind(late_blocks, both_got))

    extras = w_in.reshape(-1, rows, w_in.shape[1])[:, :3, gate_end:]
    bias = lax.dynamic_slice_in_dim(extras[:, 0, :bias_len].reshape(-1), head * SLOTS, SLOTS, 0).astype(jnp.float32)
    gain_one = extras[:, 1, :rows].reshape(1, -1).astype(jnp.float32)
    gain_two = extras[:, 2, :rows].reshape(1, -1).astype(jnp.float32)
    lengths_row = lax.dynamic_index_in_dim(lengths[0], at.phase, 0, False)
    seg = segment_ids(lengths_row, ranks * shard)
    both_got, bias, gain_one, gain_two, seg = behind((both_got, bias, gain_one, gain_two, seg))

    got, choices = at.choices(both_got)
    end = (at.rank == 0) | (at.rank == ranks - 1)
    x_all, in_one = place_tokens([rest, *got], choices, at.rank, end, gain_one)
    projected = dot(in_one, w_in, NN)
    projected = behind(projected, late_pieces[0], late_pieces[1])
    low, *saved = forward_mix(projected, bias, seg)
    low_near = at.spread_near(low, copies)
    w_mlp = at.fetch(at.dealt(behind(late_pieces, low)))
    w_gate_up, w_down = w_mlp[:, : 2 * share_ff], w_mlp[:, 2 * share_ff :]
    low_got = behind(at.spread_far(low_near))
    low_all = at.joined(low, low_got, 1, copies)

    dy_near = at.spread_near(behind(dy, low_got))
    dy_far = at.spread_far(dy_near)
    after_all = x_all.astype(jnp.float32) + dot(low_all, w_out, NT)
    in_two = (after_all * rms_scale(after_all) * gain_two).astype(jnp.bfloat16)
    after = at.piece(after_all, 0)
    scale_two = rms_scale(after)
    normed_two = after * scale_two

    dyl = at.joined(dy, behind(dy_far, after_all))
    hidden, grad_gate_up = hidden_and_grads(in_two, dyl, w_mlp, share_ff, w_mlp.shape[1], 512)
    two_part = dot(grad_gate_up, w_gate_up, NT, jnp.bfloat16)
    two_pieces = at.split(two_part)
    two_far = at.sum_far(two_pieces)
    hidden_later, grad_later = behind((hidden, grad_gate_up), two_pieces)
    grad_mlp_w = weight_grads(tn_pair_kernel, 256, in_two, grad_later, dyl, hidden_later)
    share_mlp = at.share(grad_mlp_w)
    two_far = behind(two_far, grad_mlp_w)
    mlp_part = dot(behind(hidden, grad_mlp_w), w_down, NT, jnp.bfloat16)
    two_near = behind(at.sum_near(two_pieces, two_far), mlp_part)
    back_two = at.total(two_pieces, two_near)
    scaled_two = back_two * gain_two

    grad_after = dy.astype(jnp.float32) + scale_two * (
        scaled_two - normed_two * jnp.mean(scaled_two * normed_two, axis=1, keepdims=True)
    )
    dal = grad_after.astype(jnp.bfloat16)
    don_all = dot(dal, w_out, NN, jnp.bfloat16)
    don_blocks = [
        lax.dynamic_slice_in_dim(don_all, (at.rank ^ j) // copies * HEAD_DIM, HEAD_DIM, 1) for j in range(ranks)
    ]
    don_got = behind([at.across(don_blocks[j], j) for j in range(1, ranks)])
    each = tuple((j,) for j in range(ranks))
    don = place_pieces([don_blocks[0], *don_got], each, at.rank, at.rank)
    dal_parts = dal.reshape(shard, at.seqs, ranks, -1)
    dal_blocks = [lax.dynamic_index_in_dim(dal_parts, at.rank ^ j, 2, False).reshape(shard, -1) for j in range(ranks)]
    dal_blocks = behind(dal_blocks, don_got)
    dal_got = [at.across(dal_blocks[j], j) for j in range(1, ranks)]
    mlp_pieces = at.split(behind(mlp_part, don_got))
    mlp_far = at.sum_far(mlp_pieces)

    grad_proj, bias_grad = backward_mix(projected, bias, seg, saved, don)

    bias_grad = jnp.concatenate([jnp.zeros_like(bias_grad), bias_grad], axis=1)
    row_ids = jnp.arange(width, dtype=jnp.int32)
    owners = SLOTS // bias_len
    holds = ((row_ids % rows == 0) & (row_ids // (rows * owners) == head)).astype(jnp.float32)
    mlp_near = at.sum_near(mlp_pieces, behind(mlp_far, grad_proj))
    mlp_far, dal_got, grad_proj = behind((mlp_far, dal_got, grad_proj))
    mlp_near = at.sum_near(mlp_pieces, mlp_far)
    grad_in_w = weight_grads(tn_extra_kernel, 512, in_one, grad_proj, holds[:, None], bias_grad)
    share_in = at.share(behind(grad_in_w, share_mlp))
    one_part = dot(behind(grad_proj, grad_in_w), w_in, NT, jnp.bfloat16)
    one_pieces = behind(at.split(one_part), mlp_near)
    one_far = at.sum_far(one_pieces)
    quarter = ranks // 4
    home_first = at.home(behind(share_mlp, one_pieces), range(2 * quarter))
    dal_rows = place_pieces([dal_blocks[0], *dal_got], each, at.rank, at.rank)
    dal_rows = behind(dal_rows, one_pieces)
    grad_out_w = weight_grads(tn_kernel, min(512, dal_rows.shape[1]), dal_rows, low_all)
    share_out = at.share(grad_out_w)
    mlp_out = at.total(mlp_pieces, mlp_near)
    mixed_rows = (after + mlp_out).astype(jnp.bfloat16)
    mixed = at.swap(mixed_rows.reshape(phases, block_len, width))[None]
    one_far, home_first, mixed = behind((one_far, home_first, mixed), grad_out_w)
    one_near = at.sum_near(one_pieces, one_far)
    home_second = at.home(behind(share_mlp, home_first), range(2 * quarter, ranks))
    in_home = at.home(behind(share_in, home_first), range(0, ranks, copies))
    back_one = at.total(one_pieces, behind(one_near, home_second[0])) / copies
    scaled_one = back_one * gain_one
    rest_float = rest.astype(jnp.float32)
    scale_one = rms_scale(rest_float)
    normed_one = rest_float * scale_one
    grad_rows = grad_after + scale_one * (
        scaled_one - normed_one * jnp.mean(scaled_one * normed_one, axis=1, keepdims=True)
    )
    grad_tokens = at.swap(grad_rows.reshape(phases, block_len, width))[None]

    mlp_home = home_first + home_second
    gate_up_weight = mlp_weight[:, : 2 * FF].astype(jnp.float32)
    down = at.in_order([p[:, 2 * share_ff :] for p in mlp_home], at.slot, 1).astype(jnp.float32)
    gates = at.in_order([p[:, :share_ff] for p in mlp_home], at.slot, 1).astype(jnp.float32)
    ups = at.in_order([p[:, share_ff : 2 * share_ff] for p in mlp_home], at.slot, 1).astype(jnp.float32)
    grad_mlp = jnp.concatenate([gates, ups, down], axis=1)
    gain_grad_two = jnp.sum(grad_mlp[:, : 2 * FF] * gate_up_weight, axis=1) / norm2_gain.astype(jnp.float32)

    slot_head = at.slot // copies
    parts = [
        at.in_order([p[:, j * HEAD_DIM : (j + 1) * HEAD_DIM] for p in in_home], slot_head, 1) for j in range(3)
    ]
    for j in range(HEADS):
        parts.append(sum(jnp.where(slot_head ^ n == j, p[:, qkv:gate_end], 0) for n, p in enumerate(in_home)))
    parts.append(share_out)
    grad_attn = jnp.concatenate(parts, axis=1).astype(jnp.float32)
    attn_float = attn_weight[:, :proj_cols].astype(jnp.float32)
    gain_grad_one = jnp.sum(grad_attn[:, :proj_cols] * attn_float, axis=1) / norm1_gain.astype(jnp.float32)
    bias_sums = sum(p[0, gate_end : gate_end + SLOTS].astype(jnp.float32) for p in in_home)
    owner = lax.axis_index("seqs") * at.span + lax.axis_index("span")
    bias_home = lax.dynamic_slice_in_dim(bias_sums, owner % owners * bias_len, bias_len, 0)
    return (mixed, grad_tokens, grad_attn, grad_mlp, gain_grad_one, gain_grad_two, bias_home)


def solution(mesh):
    placed = (
        P("seqs", None, "span", None),
        P(("seqs", "span"), None),
        P(("seqs", "span"), None),
        P(("seqs", "span")),
        P(("seqs", "span")),
        P(("seqs", "span")),
        P("seqs", None, None),
        P("seqs", None, "span", None),
    )
    return jax.shard_map(
        local,
        mesh=mesh,
        in_specs=placed,
        out_specs=(
            P("seqs", None, "span", None),
            P("seqs", None, "span", None),
            P(("seqs", "span"), None),
            P(("seqs", "span"), None),
            P(("seqs", "span")),
            P(("seqs", "span")),
            P(("seqs", "span")),
        ),
        check_vma=False,
    )
```

```python
import functools
import jax
import jax.numpy as jnp
from jax import lax
from jax.experimental import pallas as pl
from jax.experimental.pallas import tpu as pltpu
from jax.sharding import PartitionSpec as P

BLOCK = 64
GATE_SOFTENING = 8.0
SUB = 16
SLOTS = 64
HEAD_DIM = 512
NORM_EPS = 1e-05


def mm(a, b, dims):
    return lax.dot_general(
        a.astype(jnp.bfloat16), b.astype(jnp.bfloat16), (dims, ((), ())), preferred_element_type=jnp.float32
    )


def halves(a):
    if a.dtype == jnp.bfloat16:
        return a, None
    high = a.astype(jnp.bfloat16)
    return high, (a - high.astype(jnp.float32)).astype(jnp.bfloat16)


def fine(a, b, dims):
    (a_high, a_low), (b_high, b_low) = halves(a), halves(b)
    out = mm(a_high, b_high, dims)
    if b_low is not None:
        out = out + mm(a_high, b_low, dims)
    if a_low is not None:
        out = out + mm(a_low, b_high, dims)
    return out


NN, NT, TN = ((1,), (0,)), ((1,), (1,)), ((0,), (0,))


def nn(a, b):
    return mm(a, b, NN)


def nt(a, b):
    return mm(a, b, NT)


def tn(a, b):
    return mm(a, b, TN)


def exact(a, b):
    return lax.dot_general(
        a, b, (((1,), (0,)), ((), ())), precision=lax.Precision.HIGHEST, preferred_element_type=jnp.float32
    )


def iota(shape, dim):
    return lax.broadcasted_iota(jnp.int32, shape, dim)


def block_decay(gate, write, seg_col, seg_row, seg_prev):
    row, col = iota((BLOCK, BLOCK), 0), iota((BLOCK, BLOCK), 1)
    same = jnp.where((seg_col == seg_row) & (row >= col), 1.0, 0.0)
    lower = jnp.where(row >= col, 1.0, 0.0)
    cum = exact(lower, gate)
    total = cum[BLOCK - 1 :]
    carry = jnp.where(seg_col == seg_prev, 1.0, 0.0)
    last = jnp.where(seg_col == seg_col[BLOCK - 1 :], 1.0, 0.0)
    enter = jnp.exp(cum) * carry
    tail = jnp.exp(total - cum) * last
    fade = jnp.exp(total) * carry[BLOCK - 1 :]
    falls, rises = [], []
    for i in range(1, BLOCK // SUB):
        base = cum[i * SUB - 1 : i * SUB]
        falls.append(jnp.exp(cum[i * SUB : (i + 1) * SUB] - base))
        rises.append(jnp.exp(base - cum[: i * SUB]))
    return same, cum, enter, tail, fade, falls, rises


def diagonal(square):
    return jnp.concatenate([square[i : i + SUB, i : i + SUB] for i in range(0, BLOCK, SUB)], axis=0)


def undiagonal(strip):
    row, col = iota((BLOCK, BLOCK), 0), iota((BLOCK, BLOCK), 1)
    wide = jnp.concatenate([strip] * (BLOCK // SUB), axis=1)
    return jnp.where(row // SUB == col // SUB, wide, 0.0)


def parts(values):
    return values.reshape(BLOCK // SUB, SUB, values.shape[-1])


def decay_at(cum, j):
    cum_parts = parts(cum)
    return jnp.exp(jnp.minimum(cum_parts - cum_parts[:, j : j + 1], 0.0))


def over_sources(pairs, cum, write, falls, rises):
    strip = parts(diagonal(pairs))
    write_parts = parts(write)
    near = jnp.zeros((BLOCK // SUB, SUB, SLOTS), jnp.float32)
    for j in range(SUB):
        near = near + strip[:, :, j : j + 1] * (decay_at(cum, j) * write_parts[:, j : j + 1])
    near = near.reshape(BLOCK, SLOTS)
    far = [jnp.zeros((SUB, SLOTS), jnp.float32)]
    for i in range(1, BLOCK // SUB):
        rows = pairs[i * SUB : (i + 1) * SUB, : i * SUB]
        far.append(falls[i - 1] * fine(rows, rises[i - 1] * write[: i * SUB], NN))
    return near + jnp.concatenate(far, axis=0)


def over_slots(values, cum, write, falls, rises):
    value_parts, write_parts = parts(values), parts(write)
    lane = iota((BLOCK // SUB, SUB, SUB), 2)
    strip = jnp.zeros((BLOCK // SUB, SUB, SUB), jnp.float32)
    for j in range(SUB):
        term = value_parts * (decay_at(cum, j) * write_parts[:, j : j + 1])
        strip = jnp.where(lane == j, jnp.sum(term, axis=2, keepdims=True), strip)
    out = undiagonal(strip.reshape(BLOCK, SUB))
    far = [jnp.zeros((SUB, BLOCK), jnp.float32)]
    for i in range(1, BLOCK // SUB):
        rows = values[i * SUB : (i + 1) * SUB] * falls[i - 1]
        piece = fine(rows, rises[i - 1] * write[: i * SUB], NT)
        far.append(jnp.concatenate([piece, jnp.zeros((SUB, BLOCK - i * SUB), jnp.float32)], axis=1))
    return out + jnp.concatenate(far, axis=0)


def over_targets(pairs_values, cum, falls, rises):
    row = iota((BLOCK // SUB, SUB, SLOTS), 1)
    near = jnp.zeros((BLOCK // SUB, SUB, SLOTS), jnp.float32)
    strips = [(parts(diagonal(p)), parts(v)) for p, v in pairs_values]
    for j in range(SUB):
        term = sum(strip[:, :, j : j + 1] * value for strip, value in strips) * decay_at(cum, j)
        near = jnp.where(row == j, jnp.sum(term, axis=1, keepdims=True), near)
    out = near.reshape(BLOCK, SLOTS)
    far = jnp.zeros((BLOCK, SLOTS), jnp.float32)
    for i in range(1, BLOCK // SUB):
        here = slice(i * SUB, (i + 1) * SUB)
        piece = sum(fine(p[here, : i * SUB], v[here] * falls[i - 1], TN) for p, v in pairs_values)
        piece = rises[i - 1] * piece
        far = far + jnp.concatenate([piece, jnp.zeros((BLOCK - i * SUB, SLOTS), jnp.float32)], axis=0)
    return out + far


QKV = 3 * HEAD_DIM
GATE_END = QKV + SLOTS


def load_block(i, proj_ref, bias_ref, segc_ref, segr_ref):
    here = pl.ds(pl.multiple_of(i * BLOCK, BLOCK), BLOCK)
    pre = proj_ref[here, :QKV]
    sig = jax.nn.sigmoid(pre)
    feats = (pre * sig).astype(jnp.bfloat16)
    q, k, v = (feats[:, n * HEAD_DIM : (n + 1) * HEAD_DIM] for n in range(3))
    logits = proj_ref[here, QKV:GATE_END] + bias_ref[...]
    gate = (jnp.minimum(logits, 0.0) - jnp.log1p(jnp.exp(-jnp.abs(logits)))) / GATE_SOFTENING
    seg_prev = jnp.where(i > 0, segc_ref[pl.ds(jnp.maximum(i * BLOCK - 1, 0), 1), :], -1)
    return here, pre, sig, q, k, v, logits, gate, -small_exp(gate), segc_ref[here, :], segr_ref[i], seg_prev


def small_exp(x):
    near = x * (1.0 + x / 2 * (1.0 + x / 3 * (1.0 + x / 4 * (1.0 + x / 5 * (1.0 + x / 6)))))
    return jnp.where(x > -0.1, near, jnp.exp(x) - 1.0)


def forward_kernel(proj_ref, bias_ref, segc_ref, segr_ref, low_ref, out_hbm, small_hbm, states_hbm,
                   out_ref, small_ref, states_ref, state, sems):
    scale = HEAD_DIM ** -0.5
    blocks = proj_ref.shape[0] // BLOCK
    state[...] = jnp.zeros_like(state)

    def copies(i):
        here = pl.ds(pl.multiple_of(i * BLOCK, BLOCK), BLOCK)
        return [
            pltpu.make_async_copy(a, b, sems.at[n, i])
            for n, (a, b) in enumerate(
                [
                    (out_ref.at[here], out_hbm.at[here]),
                    (small_ref.at[here], small_hbm.at[here]),
                    (states_ref.at[i], states_hbm.at[i]),
                ]
            )
        ]

    def step(i, _):
        here, _, _, q, k, v, _, gate, write, seg_col, seg_row, seg_prev = load_block(i, proj_ref, bias_ref, segc_ref, segr_ref)
        same, cum, enter, tail, fade, falls, rises = block_decay(gate, write, seg_col, seg_row, seg_prev)
        keys_in, values_in = state[:SLOTS], state[SLOTS:]
        states_ref[i] = state[...]
        keep = fade.reshape(SLOTS, 1)
        send = tail * write
        state[:SLOTS] = keep * keys_in + tn(send, k)
        state[SLOTS:] = keep * values_in + fine(send, v, TN)
        pairs = nt(q, k) * same
        score = scale * (over_sources(pairs, cum, write, falls, rises) + enter * nt(q, keys_in))
        prob = jnp.exp(score - jnp.max(score, axis=1, keepdims=True))
        prob = prob / jnp.sum(prob, axis=1, keepdims=True)
        mix = over_slots(prob, cum, write, falls, rises) * same
        out = fine(mix, v, NN) + fine(prob * enter, values_in, NN)
        low_ref[here, :] = (out * lax.rsqrt(jnp.mean(out * out, axis=1, keepdims=True) + NORM_EPS)).astype(jnp.bfloat16)
        out_ref[here, :] = out
        small_ref[here, :] = jnp.concatenate([score, prob, pairs, mix], axis=1)
        for copy in copies(i):
            copy.start()
        return 0

    lax.fori_loop(0, blocks, step, 0, unroll=4)

    def finish(i, _):
        for copy in copies(i):
            copy.wait()
        return 0

    lax.fori_loop(0, blocks, finish, 0)


def backward_kernel(proj_ref, bias_ref, segc_ref, segr_ref, out_ref, small_ref, states_ref, don_ref,
                    grad_ref, bias_grad_ref, state, state_next):
    scale = HEAD_DIM ** -0.5
    blocks = proj_ref.shape[0] // BLOCK
    state[...] = jnp.zeros_like(state)
    state_next[...] = jnp.zeros_like(state)
    bias_grad_ref[...] = jnp.zeros_like(bias_grad_ref)

    def step(lap, _):
        i = blocks - 1 - lap
        here, pre, sig, q, k, v, logits, gate, write, seg_col, seg_row, seg_prev = load_block(i, proj_ref, bias_ref, segc_ref, segr_ref)
        same, cum, enter, tail, fade, falls, rises = block_decay(gate, write, seg_col, seg_row, seg_prev)
        last = jnp.where(seg_col == seg_col[BLOCK - 1 :], 1.0, 0.0)
        score, prob, pairs, mix = (small_ref[here, n * SLOTS : (n + 1) * SLOTS] for n in range(4))
        states_in = states_ref[i]
        keys_in, values_in = states_in[:SLOTS], states_in[SLOTS:]
        out, don = out_ref[here, :], don_ref[here, :]
        unit = lax.rsqrt(jnp.mean(out * out, axis=1, keepdims=True) + NORM_EPS)
        normed = out * unit
        dout = unit * (don - normed * jnp.mean(don * normed, axis=1, keepdims=True))
        dmix = fine(dout, v, NT) * same
        dprob = over_sources(dmix, cum, write, falls, rises) + enter * fine(dout, values_in, NT)
        inner = prob * dprob
        dscore = inner - prob * jnp.sum(inner, axis=1, keepdims=True)
        slope = scale * dscore
        dpairs = over_slots(slope, cum, write, falls, rises) * same
        dcross = slope * enter
        dstate = state[...]
        dkeys, dvalues = dstate[:SLOTS], dstate[SLOTS:]
        send = tail * write
        dfeats = jnp.concatenate(
            [
                nn(dpairs, k) + nn(dcross, keys_in),
                tn(dpairs, q) + nn(send, dkeys),
                tn(mix, dout) + nn(send, dvalues),
            ],
            axis=1,
        )
        grad_ref[here, :QKV] = (dfeats * (sig * (1.0 + pre * (1.0 - sig)))).astype(jnp.bfloat16)
        heard = over_targets([(pairs, slope), (dmix, prob)], cum, falls, rises)
        heard = heard + tail * (nt(k, dkeys) + nt(v, dvalues))
        product = dstate * state_next[...]
        held = lax.dot_general(jnp.ones((8, HEAD_DIM), jnp.float32), product[:SLOTS] + product[SLOTS:],
                               (((1,), (1,)), ((), ())), precision=lax.Precision.HIGHEST, preferred_element_type=jnp.float32)[:1]
        flow = exact(same.T, dscore * score + inner - write * heard)
        dgate = flow - (1.0 - write) * heard + last * held
        dlogits = (dgate * jax.nn.sigmoid(-logits) / GATE_SOFTENING).astype(jnp.bfloat16)
        grad_ref[here, QKV:] = jnp.concatenate([dlogits, jnp.zeros_like(dlogits)], axis=1)
        bias_grad_ref[...] += jnp.sum(dlogits.astype(jnp.float32), axis=0, keepdims=True)
        keep = fade.reshape(SLOTS, 1)
        state[:SLOTS] = keep * dkeys + tn(dcross, q)
        state[SLOTS:] = keep * dvalues + fine(prob * enter, dout, TN)
        state_next[...] = states_in
        return 0

    lax.fori_loop(0, blocks, step, 0)


VMEM = pl.BlockSpec(memory_space=pltpu.VMEM)


def slot_call(kernel, outs, out_specs, scratch, args, cost):
    return pl.pallas_call(
        kernel,
        out_shape=outs,
        in_specs=[VMEM] * len(args),
        out_specs=out_specs,
        scratch_shapes=scratch,
        cost_estimate=pl.CostEstimate(flops=cost, bytes_accessed=0, transcendentals=0),
        compiler_params=pltpu.CompilerParams(vmem_limit_bytes=58 * 2**20),
    )(*args)


def forward_mix(proj, bias, seg):
    length = proj.shape[0]
    blocks = length // BLOCK
    shapes = [(length, HEAD_DIM), (length, 4 * SLOTS), (blocks, 2 * SLOTS, HEAD_DIM)]
    outs = [jax.ShapeDtypeStruct((length, HEAD_DIM), jnp.bfloat16)] + [jax.ShapeDtypeStruct(n, jnp.float32) for n in shapes]
    specs = [VMEM] + [pl.BlockSpec(memory_space=pltpu.HBM)] * 3
    scratch = [pltpu.VMEM(n, jnp.float32) for n in shapes]
    scratch += [pltpu.VMEM((2 * SLOTS, HEAD_DIM), jnp.float32), pltpu.SemaphoreType.DMA((3, blocks))]
    args = (proj, bias.reshape(1, SLOTS), seg.reshape(length, 1), seg.reshape(blocks, 1, BLOCK))
    return slot_call(forward_kernel, outs, specs, scratch, args, 12 * 10**9)


def backward_mix(proj, bias, seg, saved, don):
    length = proj.shape[0]
    blocks = length // BLOCK
    outs = [jax.ShapeDtypeStruct(proj.shape, jnp.bfloat16), jax.ShapeDtypeStruct((1, SLOTS), jnp.float32)]
    scratch = [pltpu.VMEM((2 * SLOTS, HEAD_DIM), jnp.float32)] * 2
    args = (proj, bias.reshape(1, SLOTS), seg.reshape(length, 1), seg.reshape(blocks, 1, BLOCK), *saved, don)
    return slot_call(backward_kernel, outs, [VMEM] * 2, scratch, args, 16 * 10**9)


HEADS = 4


def product_cost(*sizes):
    flops = 2
    for size in sizes:
        flops *= size
    return pl.CostEstimate(flops=flops, bytes_accessed=2 * sizes[1] * sizes[2], transcendentals=0)


def move_cost(nbytes):
    return pl.CostEstimate(flops=0, bytes_accessed=nbytes, transcendentals=0)
FF = 5632


def dot(a, b, dims, kind=jnp.float32):
    out = lax.dot_general(a, b, (dims, ((), ())), preferred_element_type=jnp.float32)
    return out.astype(kind)


def rms_scale(values):
    return lax.rsqrt(jnp.mean(values * values, axis=-1, keepdims=True) + NORM_EPS)


def plus(a, b):
    return (a.astype(jnp.float32) + b.astype(jnp.float32)).astype(a.dtype)


def behind(value, *others):
    return lax.optimization_barrier((value, others))[0]


def tn_pair_kernel(a_ref, b_ref, c_ref, d_ref, out_ref):
    width = b_ref.shape[1]
    out_ref[:, :width] = dot(a_ref[...], b_ref[...], TN, jnp.bfloat16)
    out_ref[:, width:] = dot(c_ref[...], d_ref[...], TN, jnp.bfloat16)


def tn_kernel(a_ref, b_ref, out_ref):
    out_ref[...] = dot(a_ref[...], b_ref[...], TN, jnp.bfloat16)


def tn_extra_kernel(a_ref, b_ref, e_ref, f_ref, out_ref):
    out, last = dot(a_ref[...], b_ref[...], TN), b_ref.shape[1] - 128
    out_ref[:, :last] = out[:, :last].astype(jnp.bfloat16)
    out_ref[:, last:] = (out[:, last:] + e_ref[...] * f_ref[...]).astype(jnp.bfloat16)


def weight_grads(kernel, block, *operands):
    length, rows = operands[0].shape
    cols = sum(v.shape[1] for v in operands[1:4:2]) if kernel is tn_pair_kernel else operands[1].shape[1]
    whole = lambda v: pl.BlockSpec(v.shape, lambda i: (0, 0))
    strip = pl.BlockSpec((length, block), lambda i: (0, i))
    specs = [strip, whole(operands[1])]
    if kernel is tn_pair_kernel:
        specs += [strip, whole(operands[3])]
    elif kernel is tn_extra_kernel:
        specs += [pl.BlockSpec((block, 1), lambda i: (i, 0)), whole(operands[3])]
    return pl.pallas_call(
        kernel,
        grid=(rows // block,),
        in_specs=specs,
        out_specs=pl.BlockSpec((block, cols), lambda i: (i, 0)),
        out_shape=jax.ShapeDtypeStruct((rows, cols), jnp.bfloat16),
        cost_estimate=product_cost(length, rows, cols),
        compiler_params=pltpu.CompilerParams(vmem_limit_bytes=48 * 2**20),
    )(*operands)


def hidden_kernel(width, x_ref, y_ref, w_ref, hid_ref, grad_ref, acc):
    step = pl.program_id(0)

    @pl.when(step == 0)
    def _():
        acc[...] = jnp.zeros_like(acc)

    acc[:, : 2 * width] += dot(x_ref[...], w_ref[:, : 2 * width], NN)
    acc[:, 2 * width :] += dot(y_ref[...], w_ref[:, 2 * width : 3 * width], NN)

    @pl.when(step == pl.num_programs(0) - 1)
    def _():
        gate, up, back = acc[:, :width], acc[:, width : 2 * width], acc[:, 2 * width :]
        sig = jax.nn.sigmoid(gate)
        act = gate * sig
        hid_ref[...] = (act * up).astype(jnp.bfloat16)
        grad_ref[:, :width] = (back * up * (sig * (1.0 + gate * (1.0 - sig)))).astype(jnp.bfloat16)
        grad_ref[:, width:] = (back * act).astype(jnp.bfloat16)


def hidden_and_grads(x, y, weights, width, cols, block):
    length, depth = x.shape
    strip = pl.BlockSpec((length, block), lambda i: (0, i))
    return pl.pallas_call(
        functools.partial(hidden_kernel, width),
        grid=(depth // block,),
        in_specs=[strip, strip, pl.BlockSpec((block, cols), lambda i: (i, 0))],
        out_specs=[pl.BlockSpec((length, n * width), lambda i: (0, 0)) for n in (1, 2)],
        out_shape=[jax.ShapeDtypeStruct((length, n * width), jnp.bfloat16) for n in (1, 2)],
        scratch_shapes=[pltpu.VMEM((length, 3 * width), jnp.float32)],
        cost_estimate=product_cost(length, depth, 3 * width),
        compiler_params=pltpu.CompilerParams(vmem_limit_bytes=56 * 2**20),
    )(x, y, weights)


def head_blocks_kernel(copies, place_ref, w_ref, extra_ref, *out_refs):
    width = HEADS * HEAD_DIM
    for k, out_ref in enumerate(out_refs):
        head = (place_ref[0] ^ k) // copies
        for n in range(3):
            start = pl.multiple_of(n * width + head * HEAD_DIM, HEAD_DIM)
            out_ref[:, n * HEAD_DIM : (n + 1) * HEAD_DIM] = w_ref[:, pl.ds(start, HEAD_DIM)]
        two = w_ref[:, pl.ds(pl.multiple_of(3 * width + head // 2 * 128, 128), 128)].astype(jnp.float32)
        gate = jnp.where(head % 2 == 0, two[:, :SLOTS], two[:, SLOTS:]).astype(jnp.bfloat16)
        out_ref[:, QKV:] = jnp.concatenate([gate, extra_ref[...]], axis=1)


def head_blocks(weight, extra, slot, ranks):
    rows = weight.shape[0]
    shape = jax.ShapeDtypeStruct((rows, QKV + 2 * SLOTS), jnp.bfloat16)
    return pl.pallas_call(
        functools.partial(head_blocks_kernel, ranks // HEADS),
        out_shape=[shape] * ranks,
        in_specs=[pl.BlockSpec(memory_space=pltpu.SMEM), VMEM, VMEM],
        out_specs=[VMEM] * ranks,
        cost_estimate=move_cost(4 * ranks * rows * (QKV + 2 * SLOTS)),
        compiler_params=pltpu.CompilerParams(vmem_limit_bytes=32 * 2**20),
    )(slot.reshape(1).astype(jnp.int32), weight, extra)


def place_kernel(axis, choices, place_ref, *refs):
    pieces, out_ref = refs[:-1], refs[-1]
    size = pieces[0].shape[axis]

    def put(k, piece):
        start = pl.multiple_of((place_ref[0] ^ k) * size, size)
        where = (pl.ds(start, size), slice(None)) if axis == 0 else (slice(None), pl.ds(start, size))
        out_ref[where] = piece[...]

    for k, choice in enumerate(choices):
        if len(choice) == 1:
            put(k, pieces[choice[0]])
        else:
            pl.when(place_ref[1] == 1)(functools.partial(put, k, pieces[choice[0]]))
            pl.when(place_ref[1] == 0)(functools.partial(put, k, pieces[choice[1]]))


def place_pieces(pieces, choices, first, end, axis=0):
    shape = list(pieces[0].shape)
    shape[axis] *= len(choices)
    vmem = pl.BlockSpec(memory_space=pltpu.VMEM)
    return pl.pallas_call(
        functools.partial(place_kernel, axis, choices),
        out_shape=jax.ShapeDtypeStruct(shape, pieces[0].dtype),
        in_specs=[pl.BlockSpec(memory_space=pltpu.SMEM)] + [vmem] * len(pieces),
        out_specs=vmem,
        cost_estimate=move_cost(4 * shape[0] * shape[1]),
        compiler_params=pltpu.CompilerParams(vmem_limit_bytes=48 * 2**20),
    )(jnp.stack([first, end]).astype(jnp.int32), *pieces)


def tokens_kernel(choices, place_ref, gain_ref, *refs):
    pieces, (x_ref, normed_ref) = refs[:-2], refs[-2:]
    size = pieces[0].shape[0]

    def put(k, piece):
        here = pl.ds(pl.multiple_of((place_ref[0] ^ k) * size, size), size)
        x_ref[here, :] = piece[...]
        values = piece[...].astype(jnp.float32)
        normed_ref[here, :] = (values * rms_scale(values) * gain_ref[...]).astype(jnp.bfloat16)

    for k, choice in enumerate(choices):
        if len(choice) == 1:
            put(k, pieces[choice[0]])
        else:
            pl.when(place_ref[1] == 1)(functools.partial(put, k, pieces[choice[0]]))
            pl.when(place_ref[1] == 0)(functools.partial(put, k, pieces[choice[1]]))


def place_tokens(pieces, choices, first, end, gain):
    size, width = pieces[0].shape
    shape = jax.ShapeDtypeStruct((len(choices) * size, width), jnp.bfloat16)
    return pl.pallas_call(
        functools.partial(tokens_kernel, choices),
        out_shape=[shape] * 2,
        in_specs=[pl.BlockSpec(memory_space=pltpu.SMEM)] + [VMEM] * (len(pieces) + 1),
        out_specs=[VMEM] * 2,
        cost_estimate=move_cost(10 * len(choices) * size * width),
        compiler_params=pltpu.CompilerParams(vmem_limit_bytes=48 * 2**20),
    )(jnp.stack([first, end]).astype(jnp.int32), gain, *pieces)


def nt_kernel(a_ref, b_ref, out_ref):
    out_ref[...] = dot(a_ref[...], b_ref[...], NT, out_ref.dtype)


def times_rows(a, weights, cols, place, block=512):
    length = a.shape[0]
    return pl.pallas_call(
        nt_kernel,
        grid=(weights.shape[0] // block,),
        in_specs=[pl.BlockSpec(a.shape, lambda i: (0, 0)), pl.BlockSpec((block, cols), lambda i: (i, place))],
        out_specs=pl.BlockSpec((length, block), lambda i: (0, i)),
        out_shape=jax.ShapeDtypeStruct((length, weights.shape[0]), jnp.bfloat16),
        cost_estimate=product_cost(length, weights.shape[0], cols),
        compiler_params=pltpu.CompilerParams(vmem_limit_bytes=48 * 2**20),
    )(a, weights)


def nn_kernel(a_ref, b_ref, out_ref):
    @pl.when(pl.program_id(0) == 0)
    def _():
        out_ref[...] = jnp.zeros_like(out_ref)

    out_ref[...] += dot(a_ref[...], b_ref[...], NN)


def times(a, weights, block=1024):
    length, depth = a.shape
    cols = weights.shape[1]
    return pl.pallas_call(
        nn_kernel,
        grid=(depth // block,),
        in_specs=[pl.BlockSpec((length, block), lambda i: (0, i)), pl.BlockSpec((block, cols), lambda i: (i, 0))],
        out_specs=pl.BlockSpec((length, cols), lambda i: (0, 0)),
        out_shape=jax.ShapeDtypeStruct((length, cols), jnp.float32),
        cost_estimate=product_cost(length, depth, cols),
        compiler_params=pltpu.CompilerParams(vmem_limit_bytes=48 * 2**20),
    )(a, weights)


class Layout:
    def __init__(self, phases):
        self.seqs, self.span, self.phases = lax.axis_size("seqs"), lax.axis_size("span"), phases
        self.ranks = self.span // phases
        self.half = self.ranks // phases
        place = lax.axis_index("span")
        self.rank, self.phase = place // phases, place % phases
        self.slot = (self.rank % self.half) * phases + self.phase
        self.groups = [
            [s * self.span + z * phases + c for s in range(self.seqs) for c in range(phases)]
            for z in range(self.ranks)
        ]

    def across(self, value, k):
        step = k * self.phases
        return lax.ppermute(value, "span", [(i, i ^ step) for i in range(self.span)])

    def outward(self, k):
        pairs = []
        for i in range(self.span):
            z, c = divmod(i, self.phases)
            slot = (z % self.half) * self.phases + c
            pairs.append((i, (slot ^ k) * self.phases + z // self.half))
        return pairs

    def swap(self, value):
        mine = lax.dynamic_index_in_dim(value, self.phase, 0, False)
        other = lax.dynamic_index_in_dim(value, 1 - self.phase, 0, False)
        got = lax.ppermute(other, "span", [(i, i ^ 1) for i in range(self.span)])
        first = self.phase == 0
        return jnp.stack([jnp.where(first, mine, got), jnp.where(first, got, mine)])

    def between(self, value, pairs):
        p = self.phases
        return lax.ppermute(value, "span", [(a * p + c, b * p + c) for a, b in pairs for c in range(p)])

    def spread_near(self, value, step=1):
        if self.ranks != 4:
            return [self.across(value, k) for k in range(step, self.ranks, step)]
        return [self.across(value, 1), self.between(value, [(1, 2), (2, 1)]), self.between(value, [(0, 3), (3, 0)])]

    def spread_far(self, got):
        if self.ranks != 4:
            return got
        near, middle, ends = got
        near, middle = behind((near, middle))
        inner = self.between(near, [(1, 2), (2, 1)])
        return [near, middle, ends, inner, self.between(middle, [(1, 0), (2, 3)])]

    def choices(self, got):
        if self.ranks == 4:
            near, middle, ends, inner, outer = got
            return [near, outer, inner, ends, middle], ((0,), (1,), (2, 3), (4, 5))
        return got, tuple((k,) for k in range(len(got) + 1))

    def joined(self, own, got, axis=0, step=1):
        pieces, choices = self.choices(got)
        end = (self.rank == 0) | (self.rank == self.ranks - 1)
        return place_pieces([own, *pieces], choices, self.rank // step, end, axis)

    def dealt(self, pieces):
        return place_pieces(pieces, tuple((k,) for k in range(len(pieces))), self.rank, self.rank)

    def in_order(self, pieces, first, axis=0):
        size = pieces[0].shape[axis]
        shape = list(pieces[0].shape)
        shape[axis] = len(pieces) * size
        out = jnp.zeros(shape, pieces[0].dtype)
        for k, piece in enumerate(pieces):
            out = lax.dynamic_update_slice_in_dim(out, piece, (first ^ k) * size, axis)
        return out

    def spread(self, value):
        return behind(self.spread_far(self.spread_near(value)))

    def gather(self, value):
        return self.joined(value, self.spread(value))

    def piece(self, value, k):
        size = value.shape[0] // self.ranks
        return lax.dynamic_slice_in_dim(value, (self.rank ^ k) * size, size, 0)

    def split(self, value):
        return [self.piece(value, k) for k in range(self.ranks)]

    def sum_far(self, pieces):
        if self.ranks != 4:
            return [self.across(pieces[k], k) for k in range(1, self.ranks)]
        inner, outer = (self.between(pieces[2], pairs) for pairs in ([(1, 2), (2, 1)], [(0, 1), (3, 2)]))
        return [inner, outer, self.between(pieces[3], [(0, 3), (3, 0)])]

    def sum_near(self, pieces, got):
        if self.ranks != 4:
            return got
        inner, outer, ends = got
        inner, outer = behind((inner, outer))
        near = self.across(plus(pieces[1], inner), 1)
        return [near, self.between(plus(pieces[3], outer), [(1, 2), (2, 1)]), ends]

    def total(self, pieces, got):
        out = pieces[0].astype(jnp.float32)
        for piece in got:
            out = out + piece.astype(jnp.float32)
        return out

    def deal(self, blocks):
        return [lax.ppermute(block, "span", self.outward(k)) for k, block in enumerate(blocks)]

    def home(self, rows_of, places):
        blocks = rows_of.reshape(self.ranks, -1, rows_of.shape[1])
        pieces = []
        for k in places:
            block = lax.dynamic_index_in_dim(blocks, self.rank ^ k, 0, False)
            pieces.append(lax.ppermute(block, "span", [(b, a) for a, b in self.outward(k)]))
        return pieces

    def fetch(self, value):
        return lax.all_gather(value, ("seqs", "span"), axis=0, tiled=True, axis_index_groups=self.groups)

    def share(self, value):
        return lax.psum_scatter(
            value, ("seqs", "span"), scatter_dimension=0, tiled=True, axis_index_groups=self.groups
        )


def segment_ids(lengths_row, count):
    offsets = jnp.cumsum(lengths_row) - lengths_row
    positions = jnp.arange(count, dtype=jnp.int32)
    return jnp.sum((positions[:, None] >= offsets[None, 1:]).astype(jnp.int32), axis=1)


def local(tokens, attn_weight, mlp_weight, norm1_gain, norm2_gain, gate_bias, lengths, cotangent):
    phases, block_len, width = tokens.shape[1:]
    at = Layout(phases)
    rows = attn_weight.shape[0]
    ranks, copies = at.ranks, at.ranks // HEADS
    proj_cols = 3 * width + HEADS * SLOTS
    share_ff = FF // ranks
    qkv = 3 * HEAD_DIM
    gate_end = qkv + SLOTS
    bias_len = gate_bias.shape[0]
    head = at.rank // copies

    def columns(weight, *cuts):
        return [lax.dynamic_slice_in_dim(weight, start, size, 1) for start, size in cuts]

    across = lambda v: jnp.pad(v, (0, SLOTS - v.shape[0]))[None, :]
    row = lax.broadcasted_iota(jnp.int32, (rows, SLOTS), 0)
    extra = jnp.where(row == 1, across(norm1_gain), jnp.where(row == 2, across(norm2_gain), 0))
    extra = jnp.where(row == 0, across(gate_bias), extra).astype(jnp.bfloat16)
    in_blocks, late_blocks = head_blocks(attn_weight[:, :proj_cols], extra, at.slot, ranks), []
    for j in range(ranks):
        cuts = [(n * FF + (at.slot ^ j) * share_ff, share_ff) for n in range(3)]
        late_blocks.append(jnp.concatenate(columns(mlp_weight, *cuts), axis=1))
    in_pieces = at.deal(in_blocks)
    out_own = attn_weight[:, proj_cols:]

    rest = at.swap(tokens[0]).reshape(-1, width)
    dy = at.swap(cotangent[0]).reshape(-1, width)
    shard = rest.shape[0]
    in_pieces = behind(in_pieces, rest, dy, late_blocks)
    w_in = at.fetch(at.dealt(in_pieces))
    x_near, out_near = behind((at.spread_near(behind(rest, in_pieces)), at.spread_near(behind(out_own, in_pieces))))
    both_got, out_got = behind((at.spread_far(x_near), at.spread_far(out_near)))
    out_rows = at.swap(at.joined(out_own, out_got).reshape(phases, at.half * rows, width))
    out_rows = out_rows.reshape(phases, at.half, rows, width).swapaxes(0, 1).reshape(-1, width)
    w_out = at.fetch(out_rows)
    late_pieces = at.deal(behind(late_blocks, both_got))

    extras = w_in.reshape(-1, rows, w_in.shape[1])[:, :3, gate_end:]
    bias = lax.dynamic_slice_in_dim(extras[:, 0, :bias_len].reshape(-1), head * SLOTS, SLOTS, 0).astype(jnp.float32)
    gain_one = extras[:, 1, :rows].reshape(1, -1).astype(jnp.float32)
    gain_two = extras[:, 2, :rows].reshape(1, -1).astype(jnp.float32)
    lengths_row = lax.dynamic_index_in_dim(lengths[0], at.phase, 0, False)
    seg = segment_ids(lengths_row, ranks * shard)
    both_got, bias, gain_one, gain_two, seg = behind((both_got, bias, gain_one, gain_two, seg))

    got, choices = at.choices(both_got)
    end = (at.rank == 0) | (at.rank == ranks - 1)
    x_all, in_one = place_tokens([rest, *got], choices, at.rank, end, gain_one)
    projected = times(in_one, w_in)
    projected = behind(projected, late_pieces[0], late_pieces[1])
    low, *saved = forward_mix(projected, bias, seg)
    low_near = at.spread_near(low, copies)
    w_mlp = at.fetch(at.dealt(behind(late_pieces, low)))
    w_gate_up, w_down = w_mlp[:, : 2 * share_ff], w_mlp[:, 2 * share_ff :]
    low_got = behind(at.spread_far(low_near))
    low_all = at.joined(low, low_got, 1, copies)

    dy_near = at.spread_near(behind(dy, low_got))
    dy_far = at.spread_far(dy_near)
    after_all = x_all.astype(jnp.float32) + dot(low_all, w_out, NT)
    in_two = (after_all * rms_scale(after_all) * gain_two).astype(jnp.bfloat16)
    after = at.piece(after_all, 0)
    scale_two = rms_scale(after)
    normed_two = after * scale_two

    dyl = at.joined(dy, behind(dy_far, after_all))
    hidden, grad_gate_up = hidden_and_grads(in_two, dyl, w_mlp, share_ff, w_mlp.shape[1], 512)
    aligned = share_ff % 128 == 0
    two_part = times_rows(grad_gate_up, w_mlp if aligned else w_gate_up, 2 * share_ff, 0)
    two_pieces = at.split(two_part)
    two_far = at.sum_far(two_pieces)
    hidden_later, grad_later = behind((hidden, grad_gate_up), two_pieces)
    grad_mlp_w = weight_grads(tn_pair_kernel, 256, in_two, grad_later, dyl, hidden_later)
    passed = behind(two_far[:2], grad_mlp_w)
    two_far = [*passed, *two_far[2:]]
    share_mlp = at.share(behind(grad_mlp_w, passed))
    mlp_part = times_rows(behind(hidden, grad_mlp_w), w_mlp if aligned else w_down, share_ff, 2 if aligned else 0)
    two_near = behind(at.sum_near(two_pieces, two_far), mlp_part)
    back_two = at.total(two_pieces, two_near)
    scaled_two = back_two * gain_two

    grad_after = dy.astype(jnp.float32) + scale_two * (
        scaled_two - normed_two * jnp.mean(scaled_two * normed_two, axis=1, keepdims=True)
    )
    dal = grad_after.astype(jnp.bfloat16)
    don_all = dot(dal, w_out, NN, jnp.bfloat16)
    don_blocks = [
        lax.dynamic_slice_in_dim(don_all, (at.rank ^ j) // copies * HEAD_DIM, HEAD_DIM, 1) for j in range(ranks)
    ]
    don_got = behind([at.across(don_blocks[j], j) for j in range(1, ranks)])
    each = tuple((j,) for j in range(ranks))
    don = place_pieces([don_blocks[0], *don_got], each, at.rank, at.rank)
    dal_parts = dal.reshape(shard, at.seqs, ranks, -1)
    dal_blocks = [lax.dynamic_index_in_dim(dal_parts, at.rank ^ j, 2, False).reshape(shard, -1) for j in range(ranks)]
    dal_blocks = behind(dal_blocks, don_got)
    dal_got = [at.across(dal_blocks[j], j) for j in range(1, ranks)]
    mlp_pieces = at.split(behind(mlp_part, don_got))
    mlp_far = at.sum_far(mlp_pieces)

    grad_proj, bias_grad = backward_mix(projected, bias, seg, saved, don)

    bias_grad = jnp.concatenate([jnp.zeros_like(bias_grad), bias_grad], axis=1)
    row_ids = jnp.arange(width, dtype=jnp.int32)
    owners = SLOTS // bias_len
    holds = ((row_ids % rows == 0) & (row_ids // (rows * owners) == head)).astype(jnp.float32)
    mlp_far, dal_got, grad_proj = behind((mlp_far, dal_got, grad_proj))
    mlp_near = at.sum_near(mlp_pieces, mlp_far)
    grad_in_w = weight_grads(tn_extra_kernel, 512, in_one, grad_proj, holds[:, None], bias_grad)
    one_part = times_rows(behind(grad_proj, grad_in_w), w_in, w_in.shape[1], 0)
    one_pieces = behind(at.split(one_part), mlp_near)
    one_far = at.sum_far(one_pieces)
    quarter = ranks // 4
    dal_rows = place_pieces([dal_blocks[0], *dal_got], each, at.rank, at.rank)
    dal_rows = behind(dal_rows, one_pieces)
    grad_out_w = weight_grads(tn_kernel, min(512, dal_rows.shape[1]), dal_rows, low_all)
    share_mlp = behind(share_mlp, grad_out_w)
    share_in = at.share(behind(grad_in_w, share_mlp))
    share_out = at.share(behind(grad_out_w, grad_in_w))
    home_first = at.home(share_mlp, range(2 * quarter))
    mlp_out = at.total(mlp_pieces, mlp_near)
    mixed_rows = (after + mlp_out).astype(jnp.bfloat16)
    mixed = at.swap(mixed_rows.reshape(phases, block_len, width))[None]
    one_far, home_first, mixed = behind((one_far, home_first, mixed), grad_out_w)
    one_near = at.sum_near(one_pieces, one_far)
    home_second = at.home(behind(share_mlp, home_first), range(2 * quarter, ranks))
    in_home = at.home(behind(share_in, home_first), range(0, ranks, copies))
    back_one = at.total(one_pieces, behind(one_near, home_second[0])) / copies
    scaled_one = back_one * gain_one
    rest_float = rest.astype(jnp.float32)
    scale_one = rms_scale(rest_float)
    normed_one = rest_float * scale_one
    grad_rows = grad_after + scale_one * (
        scaled_one - normed_one * jnp.mean(scaled_one * normed_one, axis=1, keepdims=True)
    )
    grad_tokens = at.swap(grad_rows.reshape(phases, block_len, width))[None]

    mlp_home = home_first + home_second
    gate_up_weight = mlp_weight[:, : 2 * FF].astype(jnp.float32)
    down = at.in_order([p[:, 2 * share_ff :] for p in mlp_home], at.slot, 1).astype(jnp.float32)
    gates = at.in_order([p[:, :share_ff] for p in mlp_home], at.slot, 1).astype(jnp.float32)
    ups = at.in_order([p[:, share_ff : 2 * share_ff] for p in mlp_home], at.slot, 1).astype(jnp.float32)
    grad_mlp = jnp.concatenate([gates, ups, down], axis=1)
    gain_grad_two = jnp.sum(grad_mlp[:, : 2 * FF] * gate_up_weight, axis=1) / norm2_gain.astype(jnp.float32)

    slot_head = at.slot // copies
    parts = [
        at.in_order([p[:, j * HEAD_DIM : (j + 1) * HEAD_DIM] for p in in_home], slot_head, 1) for j in range(3)
    ]
    for j in range(HEADS):
        parts.append(sum(jnp.where(slot_head ^ n == j, p[:, qkv:gate_end], 0) for n, p in enumerate(in_home)))
    parts.append(share_out)
    grad_attn = jnp.concatenate(parts, axis=1).astype(jnp.float32)
    attn_float = attn_weight[:, :proj_cols].astype(jnp.float32)
    gain_grad_one = jnp.sum(grad_attn[:, :proj_cols] * attn_float, axis=1) / norm1_gain.astype(jnp.float32)
    bias_sums = sum(p[0, gate_end : gate_end + SLOTS].astype(jnp.float32) for p in in_home)
    owner = lax.axis_index("seqs") * at.span + lax.axis_index("span")
    bias_home = lax.dynamic_slice_in_dim(bias_sums, owner % owners * bias_len, bias_len, 0)
    return (mixed, grad_tokens, grad_attn, grad_mlp, gain_grad_one, gain_grad_two, bias_home)


def solution(mesh):
    placed = (
        P("seqs", None, "span", None),
        P(("seqs", "span"), None),
        P(("seqs", "span"), None),
        P(("seqs", "span")),
        P(("seqs", "span")),
        P(("seqs", "span")),
        P("seqs", None, None),
        P("seqs", None, "span", None),
    )
    return jax.shard_map(
        local,
        mesh=mesh,
        in_specs=placed,
        out_specs=(
            P("seqs", None, "span", None),
            P("seqs", None, "span", None),
            P(("seqs", "span"), None),
            P(("seqs", "span"), None),
            P(("seqs", "span")),
            P(("seqs", "span")),
            P(("seqs", "span")),
        ),
        check_vma=False,
    )
```

```python
import functools
import jax
import jax.numpy as jnp
from jax import lax
from jax.experimental import pallas as pl
from jax.experimental.pallas import tpu as pltpu
from jax.sharding import PartitionSpec as P

BLOCK = 64
GATE_SOFTENING = 8.0
SUB = 16
SLOTS = 64
HEAD_DIM = 512
NORM_EPS = 1e-05


def mm(a, b, dims):
    return lax.dot_general(
        a.astype(jnp.bfloat16), b.astype(jnp.bfloat16), (dims, ((), ())), preferred_element_type=jnp.float32
    )


def halves(a):
    if a.dtype == jnp.bfloat16:
        return a, None
    high = a.astype(jnp.bfloat16)
    return high, (a - high.astype(jnp.float32)).astype(jnp.bfloat16)


def fine(a, b, dims):
    (a_high, a_low), (b_high, b_low) = halves(a), halves(b)
    out = mm(a_high, b_high, dims)
    if b_low is not None:
        out = out + mm(a_high, b_low, dims)
    if a_low is not None:
        out = out + mm(a_low, b_high, dims)
    return out


NN, NT, TN = ((1,), (0,)), ((1,), (1,)), ((0,), (0,))


def nn(a, b):
    return mm(a, b, NN)


def nt(a, b):
    return mm(a, b, NT)


def tn(a, b):
    return mm(a, b, TN)


def exact(a, b):
    return lax.dot_general(
        a, b, (((1,), (0,)), ((), ())), precision=lax.Precision.HIGHEST, preferred_element_type=jnp.float32
    )


def iota(shape, dim):
    return lax.broadcasted_iota(jnp.int32, shape, dim)


def block_decay(gate, write, seg_col, seg_row, seg_prev):
    row, col = iota((BLOCK, BLOCK), 0), iota((BLOCK, BLOCK), 1)
    same = jnp.where((seg_col == seg_row) & (row >= col), 1.0, 0.0)
    lower = jnp.where(row >= col, 1.0, 0.0)
    cum = exact(lower, gate)
    total = cum[BLOCK - 1 :]
    carry = jnp.where(seg_col == seg_prev, 1.0, 0.0)
    last = jnp.where(seg_col == seg_col[BLOCK - 1 :], 1.0, 0.0)
    enter = jnp.exp(cum) * carry
    tail = jnp.exp(total - cum) * last
    fade = jnp.exp(total) * carry[BLOCK - 1 :]
    falls, rises = [], []
    for i in range(1, BLOCK // SUB):
        base = cum[i * SUB - 1 : i * SUB]
        falls.append(jnp.exp(cum[i * SUB : (i + 1) * SUB] - base))
        rises.append(jnp.exp(base - cum[: i * SUB]))
    return same, cum, enter, tail, fade, falls, rises


def diagonal(square):
    return jnp.concatenate([square[i : i + SUB, i : i + SUB] for i in range(0, BLOCK, SUB)], axis=0)


def undiagonal(strip):
    row, col = iota((BLOCK, BLOCK), 0), iota((BLOCK, BLOCK), 1)
    wide = jnp.concatenate([strip] * (BLOCK // SUB), axis=1)
    return jnp.where(row // SUB == col // SUB, wide, 0.0)


def parts(values):
    return values.reshape(BLOCK // SUB, SUB, values.shape[-1])


def decay_at(cum, j):
    cum_parts = parts(cum)
    return jnp.exp(jnp.minimum(cum_parts - cum_parts[:, j : j + 1], 0.0))


def over_sources(pairs, cum, write, falls, rises):
    strip = parts(diagonal(pairs))
    write_parts = parts(write)
    near = jnp.zeros((BLOCK // SUB, SUB, SLOTS), jnp.float32)
    for j in range(SUB):
        near = near + strip[:, :, j : j + 1] * (decay_at(cum, j) * write_parts[:, j : j + 1])
    near = near.reshape(BLOCK, SLOTS)
    far = [jnp.zeros((SUB, SLOTS), jnp.float32)]
    for i in range(1, BLOCK // SUB):
        rows = pairs[i * SUB : (i + 1) * SUB, : i * SUB]
        far.append(falls[i - 1] * fine(rows, rises[i - 1] * write[: i * SUB], NN))
    return near + jnp.concatenate(far, axis=0)


def over_slots(values, cum, write, falls, rises):
    value_parts, write_parts = parts(values), parts(write)
    lane = iota((BLOCK // SUB, SUB, SUB), 2)
    strip = jnp.zeros((BLOCK // SUB, SUB, SUB), jnp.float32)
    for j in range(SUB):
        term = value_parts * (decay_at(cum, j) * write_parts[:, j : j + 1])
        strip = jnp.where(lane == j, jnp.sum(term, axis=2, keepdims=True), strip)
    out = undiagonal(strip.reshape(BLOCK, SUB))
    far = [jnp.zeros((SUB, BLOCK), jnp.float32)]
    for i in range(1, BLOCK // SUB):
        rows = values[i * SUB : (i + 1) * SUB] * falls[i - 1]
        piece = fine(rows, rises[i - 1] * write[: i * SUB], NT)
        far.append(jnp.concatenate([piece, jnp.zeros((SUB, BLOCK - i * SUB), jnp.float32)], axis=1))
    return out + jnp.concatenate(far, axis=0)


def over_targets(pairs_values, cum, falls, rises):
    row = iota((BLOCK // SUB, SUB, SLOTS), 1)
    near = jnp.zeros((BLOCK // SUB, SUB, SLOTS), jnp.float32)
    strips = [(parts(diagonal(p)), parts(v)) for p, v in pairs_values]
    for j in range(SUB):
        term = sum(strip[:, :, j : j + 1] * value for strip, value in strips) * decay_at(cum, j)
        near = jnp.where(row == j, jnp.sum(term, axis=1, keepdims=True), near)
    out = near.reshape(BLOCK, SLOTS)
    far = jnp.zeros((BLOCK, SLOTS), jnp.float32)
    for i in range(1, BLOCK // SUB):
        here = slice(i * SUB, (i + 1) * SUB)
        piece = sum(fine(p[here, : i * SUB], v[here] * falls[i - 1], TN) for p, v in pairs_values)
        piece = rises[i - 1] * piece
        far = far + jnp.concatenate([piece, jnp.zeros((BLOCK - i * SUB, SLOTS), jnp.float32)], axis=0)
    return out + far


QKV = 3 * HEAD_DIM
GATE_END = QKV + SLOTS


def load_block(i, proj_ref, bias_ref, segc_ref, segr_ref):
    here = pl.ds(pl.multiple_of(i * BLOCK, BLOCK), BLOCK)
    pre = proj_ref[here, :QKV]
    sig = jax.nn.sigmoid(pre)
    feats = (pre * sig).astype(jnp.bfloat16)
    q, k, v = (feats[:, n * HEAD_DIM : (n + 1) * HEAD_DIM] for n in range(3))
    logits = proj_ref[here, QKV:GATE_END] + bias_ref[...]
    gate = (jnp.minimum(logits, 0.0) - jnp.log1p(jnp.exp(-jnp.abs(logits)))) / GATE_SOFTENING
    seg_prev = jnp.where(i > 0, segc_ref[pl.ds(jnp.maximum(i * BLOCK - 1, 0), 1), :], -1)
    return here, pre, sig, q, k, v, logits, gate, -small_exp(gate), segc_ref[here, :], segr_ref[i], seg_prev


def small_exp(x):
    near = x * (1.0 + x / 2 * (1.0 + x / 3 * (1.0 + x / 4 * (1.0 + x / 5 * (1.0 + x / 6)))))
    return jnp.where(x > -0.1, near, jnp.exp(x) - 1.0)


def forward_kernel(proj_ref, bias_ref, segc_ref, segr_ref, low_ref, out_hbm, small_hbm, states_hbm,
                   out_ref, small_ref, states_ref, state, sems):
    scale = HEAD_DIM ** -0.5
    blocks = proj_ref.shape[0] // BLOCK
    state[...] = jnp.zeros_like(state)

    def copies(i):
        here = pl.ds(pl.multiple_of(i * BLOCK, BLOCK), BLOCK)
        return [
            pltpu.make_async_copy(a, b, sems.at[n, i])
            for n, (a, b) in enumerate(
                [
                    (out_ref.at[here], out_hbm.at[here]),
                    (small_ref.at[here], small_hbm.at[here]),
                    (states_ref.at[i], states_hbm.at[i]),
                ]
            )
        ]

    def step(i, _):
        here, _, _, q, k, v, _, gate, write, seg_col, seg_row, seg_prev = load_block(i, proj_ref, bias_ref, segc_ref, segr_ref)
        same, cum, enter, tail, fade, falls, rises = block_decay(gate, write, seg_col, seg_row, seg_prev)
        keys_in, values_in = state[:SLOTS], state[SLOTS:]
        states_ref[i] = state[...]
        keep = fade.reshape(SLOTS, 1)
        send = tail * write
        state[:SLOTS] = keep * keys_in + fine(send, k, TN)
        state[SLOTS:] = keep * values_in + fine(send, v, TN)
        pairs = nt(q, k) * same
        score = scale * (over_sources(pairs, cum, write, falls, rises) + enter * fine(q, keys_in, NT))
        prob = jnp.exp(score - jnp.max(score, axis=1, keepdims=True))
        prob = prob / jnp.sum(prob, axis=1, keepdims=True)
        mix = over_slots(prob, cum, write, falls, rises) * same
        out = fine(mix, v, NN) + fine(prob * enter, values_in, NN)
        low_ref[here, :] = (out * lax.rsqrt(jnp.mean(out * out, axis=1, keepdims=True) + NORM_EPS)).astype(jnp.bfloat16)
        out_ref[here, :] = out
        small_ref[here, :] = jnp.concatenate([score, prob, pairs, mix], axis=1)
        for copy in copies(i):
            copy.start()
        return 0

    lax.fori_loop(0, blocks, step, 0, unroll=4)

    def finish(i, _):
        for copy in copies(i):
            copy.wait()
        return 0

    lax.fori_loop(0, blocks, finish, 0)


def backward_kernel(proj_ref, bias_ref, segc_ref, segr_ref, out_ref, small_ref, states_ref, don_ref,
                    grad_ref, bias_grad_ref, state, state_next):
    scale = HEAD_DIM ** -0.5
    blocks = proj_ref.shape[0] // BLOCK
    state[...] = jnp.zeros_like(state)
    state_next[...] = jnp.zeros_like(state)
    bias_grad_ref[...] = jnp.zeros_like(bias_grad_ref)

    def step(lap, _):
        i = blocks - 1 - lap
        here, pre, sig, q, k, v, logits, gate, write, seg_col, seg_row, seg_prev = load_block(i, proj_ref, bias_ref, segc_ref, segr_ref)
        same, cum, enter, tail, fade, falls, rises = block_decay(gate, write, seg_col, seg_row, seg_prev)
        last = jnp.where(seg_col == seg_col[BLOCK - 1 :], 1.0, 0.0)
        score, prob, pairs, mix = (small_ref[here, n * SLOTS : (n + 1) * SLOTS] for n in range(4))
        states_in = states_ref[i]
        keys_in, values_in = states_in[:SLOTS], states_in[SLOTS:]
        out, don = out_ref[here, :], don_ref[here, :]
        unit = lax.rsqrt(jnp.mean(out * out, axis=1, keepdims=True) + NORM_EPS)
        normed = out * unit
        dout = unit * (don - normed * jnp.mean(don * normed, axis=1, keepdims=True))
        dmix = fine(dout, v, NT) * same
        dprob = over_sources(dmix, cum, write, falls, rises) + enter * fine(dout, values_in, NT)
        inner = prob * dprob
        dscore = inner - prob * jnp.sum(inner, axis=1, keepdims=True)
        slope = scale * dscore
        dpairs = over_slots(slope, cum, write, falls, rises) * same
        dcross = slope * enter
        dstate = state[...]
        dkeys, dvalues = dstate[:SLOTS], dstate[SLOTS:]
        send = tail * write
        dfeats = jnp.concatenate(
            [
                nn(dpairs, k) + nn(dcross, keys_in),
                tn(dpairs, q) + nn(send, dkeys),
                tn(mix, dout) + nn(send, dvalues),
            ],
            axis=1,
        )
        grad_ref[here, :QKV] = (dfeats * (sig * (1.0 + pre * (1.0 - sig)))).astype(jnp.bfloat16)
        heard = over_targets([(pairs, slope), (dmix, prob)], cum, falls, rises)
        heard = heard + tail * (fine(k, dkeys, NT) + fine(v, dvalues, NT))
        product = dstate * state_next[...]
        held = lax.dot_general(jnp.ones((8, HEAD_DIM), jnp.float32), product[:SLOTS] + product[SLOTS:],
                               (((1,), (1,)), ((), ())), precision=lax.Precision.HIGHEST, preferred_element_type=jnp.float32)[:1]
        flow = exact(same.T, dscore * score + inner - write * heard)
        dgate = flow - (1.0 - write) * heard + last * held
        dlogits = (dgate * jax.nn.sigmoid(-logits) / GATE_SOFTENING).astype(jnp.bfloat16)
        grad_ref[here, QKV:] = jnp.concatenate([dlogits, jnp.zeros_like(dlogits)], axis=1)
        bias_grad_ref[...] += jnp.sum(dlogits.astype(jnp.float32), axis=0, keepdims=True)
        keep = fade.reshape(SLOTS, 1)
        state[:SLOTS] = keep * dkeys + fine(dcross, q, TN)
        state[SLOTS:] = keep * dvalues + fine(prob * enter, dout, TN)
        state_next[...] = states_in
        return 0

    lax.fori_loop(0, blocks, step, 0)


VMEM = pl.BlockSpec(memory_space=pltpu.VMEM)


def slot_call(kernel, outs, out_specs, scratch, args, cost):
    return pl.pallas_call(
        kernel,
        out_shape=outs,
        in_specs=[VMEM] * len(args),
        out_specs=out_specs,
        scratch_shapes=scratch,
        cost_estimate=pl.CostEstimate(flops=cost, bytes_accessed=0, transcendentals=0),
        compiler_params=pltpu.CompilerParams(vmem_limit_bytes=58 * 2**20),
    )(*args)


def forward_mix(proj, bias, seg):
    length = proj.shape[0]
    blocks = length // BLOCK
    shapes = [(length, HEAD_DIM), (length, 4 * SLOTS), (blocks, 2 * SLOTS, HEAD_DIM)]
    outs = [jax.ShapeDtypeStruct((length, HEAD_DIM), jnp.bfloat16)] + [jax.ShapeDtypeStruct(n, jnp.float32) for n in shapes]
    specs = [VMEM] + [pl.BlockSpec(memory_space=pltpu.HBM)] * 3
    scratch = [pltpu.VMEM(n, jnp.float32) for n in shapes]
    scratch += [pltpu.VMEM((2 * SLOTS, HEAD_DIM), jnp.float32), pltpu.SemaphoreType.DMA((3, blocks))]
    args = (proj, bias.reshape(1, SLOTS), seg.reshape(length, 1), seg.reshape(blocks, 1, BLOCK))
    return slot_call(forward_kernel, outs, specs, scratch, args, 12 * 10**9)


def backward_mix(proj, bias, seg, saved, don):
    length = proj.shape[0]
    blocks = length // BLOCK
    outs = [jax.ShapeDtypeStruct(proj.shape, jnp.bfloat16), jax.ShapeDtypeStruct((1, SLOTS), jnp.float32)]
    scratch = [pltpu.VMEM((2 * SLOTS, HEAD_DIM), jnp.float32)] * 2
    args = (proj, bias.reshape(1, SLOTS), seg.reshape(length, 1), seg.reshape(blocks, 1, BLOCK), *saved, don)
    return slot_call(backward_kernel, outs, [VMEM] * 2, scratch, args, 16 * 10**9)


HEADS = 4


def product_cost(*sizes):
    flops = 2
    for size in sizes:
        flops *= size
    return pl.CostEstimate(flops=flops, bytes_accessed=2 * sizes[1] * sizes[2], transcendentals=0)


def move_cost(nbytes):
    return pl.CostEstimate(flops=0, bytes_accessed=nbytes, transcendentals=0)
FF = 5632


def dot(a, b, dims, kind=jnp.float32):
    out = lax.dot_general(a, b, (dims, ((), ())), preferred_element_type=jnp.float32)
    return out.astype(kind)


def rms_scale(values):
    return lax.rsqrt(jnp.mean(values * values, axis=-1, keepdims=True) + NORM_EPS)


def plus(a, b):
    return (a.astype(jnp.float32) + b.astype(jnp.float32)).astype(a.dtype)


def behind(value, *others):
    return lax.optimization_barrier((value, others))[0]


def tn_pair_kernel(a_ref, b_ref, c_ref, d_ref, out_ref):
    width = b_ref.shape[1]
    out_ref[:, :width] = dot(a_ref[...], b_ref[...], TN, jnp.bfloat16)
    out_ref[:, width:] = dot(c_ref[...], d_ref[...], TN, jnp.bfloat16)


def tn_kernel(a_ref, b_ref, out_ref):
    out_ref[...] = dot(a_ref[...], b_ref[...], TN, jnp.bfloat16)


def tn_extra_kernel(a_ref, b_ref, e_ref, f_ref, out_ref):
    out, last = dot(a_ref[...], b_ref[...], TN), b_ref.shape[1] - 128
    out_ref[:, :last] = out[:, :last].astype(jnp.bfloat16)
    out_ref[:, last:] = (out[:, last:] + e_ref[...] * f_ref[...]).astype(jnp.bfloat16)


def weight_grads(kernel, block, *operands):
    length, rows = operands[0].shape
    cols = sum(v.shape[1] for v in operands[1:4:2]) if kernel is tn_pair_kernel else operands[1].shape[1]
    whole = lambda v: pl.BlockSpec(v.shape, lambda i: (0, 0))
    strip = pl.BlockSpec((length, block), lambda i: (0, i))
    specs = [strip, whole(operands[1])]
    if kernel is tn_pair_kernel:
        specs += [strip, whole(operands[3])]
    elif kernel is tn_extra_kernel:
        specs += [pl.BlockSpec((block, 1), lambda i: (i, 0)), whole(operands[3])]
    return pl.pallas_call(
        kernel,
        grid=(rows // block,),
        in_specs=specs,
        out_specs=pl.BlockSpec((block, cols), lambda i: (i, 0)),
        out_shape=jax.ShapeDtypeStruct((rows, cols), jnp.bfloat16),
        cost_estimate=product_cost(length, rows, cols),
        compiler_params=pltpu.CompilerParams(vmem_limit_bytes=48 * 2**20),
    )(*operands)


def hidden_kernel(width, x_ref, y_ref, w_ref, hid_ref, grad_ref, acc):
    step = pl.program_id(0)

    @pl.when(step == 0)
    def _():
        acc[...] = jnp.zeros_like(acc)

    acc[:, : 2 * width] += dot(x_ref[...], w_ref[:, : 2 * width], NN)
    acc[:, 2 * width :] += dot(y_ref[...], w_ref[:, 2 * width : 3 * width], NN)

    @pl.when(step == pl.num_programs(0) - 1)
    def _():
        gate, up, back = acc[:, :width], acc[:, width : 2 * width], acc[:, 2 * width :]
        sig = jax.nn.sigmoid(gate)
        act = gate * sig
        hid_ref[...] = (act * up).astype(jnp.bfloat16)
        grad_ref[:, :width] = (back * up * (sig * (1.0 + gate * (1.0 - sig)))).astype(jnp.bfloat16)
        grad_ref[:, width:] = (back * act).astype(jnp.bfloat16)


def hidden_and_grads(x, y, weights, width, cols, block):
    length, depth = x.shape
    strip = pl.BlockSpec((length, block), lambda i: (0, i))
    return pl.pallas_call(
        functools.partial(hidden_kernel, width),
        grid=(depth // block,),
        in_specs=[strip, strip, pl.BlockSpec((block, cols), lambda i: (i, 0))],
        out_specs=[pl.BlockSpec((length, n * width), lambda i: (0, 0)) for n in (1, 2)],
        out_shape=[jax.ShapeDtypeStruct((length, n * width), jnp.bfloat16) for n in (1, 2)],
        scratch_shapes=[pltpu.VMEM((length, 3 * width), jnp.float32)],
        cost_estimate=product_cost(length, depth, 3 * width),
        compiler_params=pltpu.CompilerParams(vmem_limit_bytes=56 * 2**20),
    )(x, y, weights)


def head_blocks_kernel(copies, place_ref, w_ref, extra_ref, *out_refs):
    width = HEADS * HEAD_DIM
    for k, out_ref in enumerate(out_refs):
        head = (place_ref[0] ^ k) // copies
        for n in range(3):
            start = pl.multiple_of(n * width + head * HEAD_DIM, HEAD_DIM)
            out_ref[:, n * HEAD_DIM : (n + 1) * HEAD_DIM] = w_ref[:, pl.ds(start, HEAD_DIM)]
        two = w_ref[:, pl.ds(pl.multiple_of(3 * width + head // 2 * 128, 128), 128)].astype(jnp.float32)
        gate = jnp.where(head % 2 == 0, two[:, :SLOTS], two[:, SLOTS:]).astype(jnp.bfloat16)
        out_ref[:, QKV:] = jnp.concatenate([gate, extra_ref[...]], axis=1)


def head_blocks(weight, extra, slot, ranks):
    rows = weight.shape[0]
    shape = jax.ShapeDtypeStruct((rows, QKV + 2 * SLOTS), jnp.bfloat16)
    return pl.pallas_call(
        functools.partial(head_blocks_kernel, ranks // HEADS),
        out_shape=[shape] * ranks,
        in_specs=[pl.BlockSpec(memory_space=pltpu.SMEM), VMEM, VMEM],
        out_specs=[VMEM] * ranks,
        cost_estimate=move_cost(4 * ranks * rows * (QKV + 2 * SLOTS)),
        compiler_params=pltpu.CompilerParams(vmem_limit_bytes=32 * 2**20),
    )(slot.reshape(1).astype(jnp.int32), weight, extra)


def place_kernel(axis, choices, place_ref, *refs):
    pieces, out_ref = refs[:-1], refs[-1]
    size = pieces[0].shape[axis]

    def put(k, piece):
        start = pl.multiple_of((place_ref[0] ^ k) * size, size)
        where = (pl.ds(start, size), slice(None)) if axis == 0 else (slice(None), pl.ds(start, size))
        out_ref[where] = piece[...]

    for k, choice in enumerate(choices):
        if len(choice) == 1:
            put(k, pieces[choice[0]])
        else:
            pl.when(place_ref[1] == 1)(functools.partial(put, k, pieces[choice[0]]))
            pl.when(place_ref[1] == 0)(functools.partial(put, k, pieces[choice[1]]))


def place_pieces(pieces, choices, first, end, axis=0):
    shape = list(pieces[0].shape)
    shape[axis] *= len(choices)
    vmem = pl.BlockSpec(memory_space=pltpu.VMEM)
    return pl.pallas_call(
        functools.partial(place_kernel, axis, choices),
        out_shape=jax.ShapeDtypeStruct(shape, pieces[0].dtype),
        in_specs=[pl.BlockSpec(memory_space=pltpu.SMEM)] + [vmem] * len(pieces),
        out_specs=vmem,
        cost_estimate=move_cost(4 * shape[0] * shape[1]),
        compiler_params=pltpu.CompilerParams(vmem_limit_bytes=48 * 2**20),
    )(jnp.stack([first, end]).astype(jnp.int32), *pieces)


def tokens_kernel(choices, place_ref, gain_ref, *refs):
    pieces, (x_ref, normed_ref) = refs[:-2], refs[-2:]
    size = pieces[0].shape[0]

    def put(k, piece):
        here = pl.ds(pl.multiple_of((place_ref[0] ^ k) * size, size), size)
        x_ref[here, :] = piece[...]
        values = piece[...].astype(jnp.float32)
        normed_ref[here, :] = (values * rms_scale(values) * gain_ref[...]).astype(jnp.bfloat16)

    for k, choice in enumerate(choices):
        if len(choice) == 1:
            put(k, pieces[choice[0]])
        else:
            pl.when(place_ref[1] == 1)(functools.partial(put, k, pieces[choice[0]]))
            pl.when(place_ref[1] == 0)(functools.partial(put, k, pieces[choice[1]]))


def place_tokens(pieces, choices, first, end, gain):
    size, width = pieces[0].shape
    shape = jax.ShapeDtypeStruct((len(choices) * size, width), jnp.bfloat16)
    return pl.pallas_call(
        functools.partial(tokens_kernel, choices),
        out_shape=[shape] * 2,
        in_specs=[pl.BlockSpec(memory_space=pltpu.SMEM)] + [VMEM] * (len(pieces) + 1),
        out_specs=[VMEM] * 2,
        cost_estimate=move_cost(10 * len(choices) * size * width),
        compiler_params=pltpu.CompilerParams(vmem_limit_bytes=48 * 2**20),
    )(jnp.stack([first, end]).astype(jnp.int32), gain, *pieces)


def nt_kernel(a_ref, b_ref, out_ref):
    out_ref[...] = dot(a_ref[...], b_ref[...], NT, out_ref.dtype)


def times_rows(a, weights, cols, place, block=512):
    length = a.shape[0]
    return pl.pallas_call(
        nt_kernel,
        grid=(weights.shape[0] // block,),
        in_specs=[pl.BlockSpec(a.shape, lambda i: (0, 0)), pl.BlockSpec((block, cols), lambda i: (i, place))],
        out_specs=pl.BlockSpec((length, block), lambda i: (0, i)),
        out_shape=jax.ShapeDtypeStruct((length, weights.shape[0]), jnp.bfloat16),
        cost_estimate=product_cost(length, weights.shape[0], cols),
        compiler_params=pltpu.CompilerParams(vmem_limit_bytes=48 * 2**20),
    )(a, weights)


def nn_kernel(a_ref, b_ref, out_ref):
    @pl.when(pl.program_id(0) == 0)
    def _():
        out_ref[...] = jnp.zeros_like(out_ref)

    out_ref[...] += dot(a_ref[...], b_ref[...], NN)


def times(a, weights, block=1024):
    length, depth = a.shape
    cols = weights.shape[1]
    return pl.pallas_call(
        nn_kernel,
        grid=(depth // block,),
        in_specs=[pl.BlockSpec((length, block), lambda i: (0, i)), pl.BlockSpec((block, cols), lambda i: (i, 0))],
        out_specs=pl.BlockSpec((length, cols), lambda i: (0, 0)),
        out_shape=jax.ShapeDtypeStruct((length, cols), jnp.float32),
        cost_estimate=product_cost(length, depth, cols),
        compiler_params=pltpu.CompilerParams(vmem_limit_bytes=48 * 2**20),
    )(a, weights)


class Layout:
    def __init__(self, phases):
        self.seqs, self.span, self.phases = lax.axis_size("seqs"), lax.axis_size("span"), phases
        self.ranks = self.span // phases
        self.half = self.ranks // phases
        place = lax.axis_index("span")
        self.rank, self.phase = place // phases, place % phases
        self.slot = (self.rank % self.half) * phases + self.phase
        self.groups = [
            [s * self.span + z * phases + c for s in range(self.seqs) for c in range(phases)]
            for z in range(self.ranks)
        ]

    def across(self, value, k):
        step = k * self.phases
        return lax.ppermute(value, "span", [(i, i ^ step) for i in range(self.span)])

    def outward(self, k):
        pairs = []
        for i in range(self.span):
            z, c = divmod(i, self.phases)
            slot = (z % self.half) * self.phases + c
            pairs.append((i, (slot ^ k) * self.phases + z // self.half))
        return pairs

    def swap(self, value):
        mine = lax.dynamic_index_in_dim(value, self.phase, 0, False)
        other = lax.dynamic_index_in_dim(value, 1 - self.phase, 0, False)
        got = lax.ppermute(other, "span", [(i, i ^ 1) for i in range(self.span)])
        first = self.phase == 0
        return jnp.stack([jnp.where(first, mine, got), jnp.where(first, got, mine)])

    def between(self, value, pairs):
        p = self.phases
        return lax.ppermute(value, "span", [(a * p + c, b * p + c) for a, b in pairs for c in range(p)])

    def spread_near(self, value, step=1):
        if self.ranks != 4:
            return [self.across(value, k) for k in range(step, self.ranks, step)]
        return [self.across(value, 1), self.between(value, [(1, 2), (2, 1)]), self.between(value, [(0, 3), (3, 0)])]

    def spread_far(self, got):
        if self.ranks != 4:
            return got
        near, middle, ends = got
        near, middle = behind((near, middle))
        inner = self.between(near, [(1, 2), (2, 1)])
        return [near, middle, ends, inner, self.between(middle, [(1, 0), (2, 3)])]

    def choices(self, got):
        if self.ranks == 4:
            near, middle, ends, inner, outer = got
            return [near, outer, inner, ends, middle], ((0,), (1,), (2, 3), (4, 5))
        return got, tuple((k,) for k in range(len(got) + 1))

    def joined(self, own, got, axis=0, step=1):
        pieces, choices = self.choices(got)
        end = (self.rank == 0) | (self.rank == self.ranks - 1)
        return place_pieces([own, *pieces], choices, self.rank // step, end, axis)

    def dealt(self, pieces):
        return place_pieces(pieces, tuple((k,) for k in range(len(pieces))), self.rank, self.rank)

    def in_order(self, pieces, first, axis=0):
        size = pieces[0].shape[axis]
        shape = list(pieces[0].shape)
        shape[axis] = len(pieces) * size
        out = jnp.zeros(shape, pieces[0].dtype)
        for k, piece in enumerate(pieces):
            out = lax.dynamic_update_slice_in_dim(out, piece, (first ^ k) * size, axis)
        return out

    def spread(self, value):
        return behind(self.spread_far(self.spread_near(value)))

    def gather(self, value):
        return self.joined(value, self.spread(value))

    def piece(self, value, k):
        size = value.shape[0] // self.ranks
        return lax.dynamic_slice_in_dim(value, (self.rank ^ k) * size, size, 0)

    def split(self, value):
        return [self.piece(value, k) for k in range(self.ranks)]

    def sum_far(self, pieces):
        if self.ranks != 4:
            return [self.across(pieces[k], k) for k in range(1, self.ranks)]
        inner, outer = (self.between(pieces[2], pairs) for pairs in ([(1, 2), (2, 1)], [(0, 1), (3, 2)]))
        return [inner, outer, self.between(pieces[3], [(0, 3), (3, 0)])]

    def sum_near(self, pieces, got):
        if self.ranks != 4:
            return got
        inner, outer, ends = got
        inner, outer = behind((inner, outer))
        near = self.across(plus(pieces[1], inner), 1)
        return [near, self.between(plus(pieces[3], outer), [(1, 2), (2, 1)]), ends]

    def total(self, pieces, got):
        out = pieces[0].astype(jnp.float32)
        for piece in got:
            out = out + piece.astype(jnp.float32)
        return out

    def deal(self, blocks):
        return [lax.ppermute(block, "span", self.outward(k)) for k, block in enumerate(blocks)]

    def home(self, rows_of, places):
        blocks = rows_of.reshape(self.ranks, -1, rows_of.shape[1])
        pieces = []
        for k in places:
            block = lax.dynamic_index_in_dim(blocks, self.rank ^ k, 0, False)
            pieces.append(lax.ppermute(block, "span", [(b, a) for a, b in self.outward(k)]))
        return pieces

    def fetch(self, value):
        return lax.all_gather(value, ("seqs", "span"), axis=0, tiled=True, axis_index_groups=self.groups)

    def share(self, value):
        return lax.psum_scatter(
            value, ("seqs", "span"), scatter_dimension=0, tiled=True, axis_index_groups=self.groups
        )


def segment_ids(lengths_row, count):
    offsets = jnp.cumsum(lengths_row) - lengths_row
    positions = jnp.arange(count, dtype=jnp.int32)
    return jnp.sum((positions[:, None] >= offsets[None, 1:]).astype(jnp.int32), axis=1)


def local(tokens, attn_weight, mlp_weight, norm1_gain, norm2_gain, gate_bias, lengths, cotangent):
    phases, block_len, width = tokens.shape[1:]
    at = Layout(phases)
    rows = attn_weight.shape[0]
    ranks, copies = at.ranks, at.ranks // HEADS
    proj_cols = 3 * width + HEADS * SLOTS
    share_ff = FF // ranks
    qkv = 3 * HEAD_DIM
    gate_end = qkv + SLOTS
    bias_len = gate_bias.shape[0]
    head = at.rank // copies

    def columns(weight, *cuts):
        return [lax.dynamic_slice_in_dim(weight, start, size, 1) for start, size in cuts]

    across = lambda v: jnp.pad(v, (0, SLOTS - v.shape[0]))[None, :]
    row = lax.broadcasted_iota(jnp.int32, (rows, SLOTS), 0)
    extra = jnp.where(row == 1, across(norm1_gain), jnp.where(row == 2, across(norm2_gain), 0))
    extra = jnp.where(row == 0, across(gate_bias), extra).astype(jnp.bfloat16)
    in_blocks, late_blocks = head_blocks(attn_weight[:, :proj_cols], extra, at.slot, ranks), []
    for j in range(ranks):
        cuts = [(n * FF + (at.slot ^ j) * share_ff, share_ff) for n in range(3)]
        late_blocks.append(jnp.concatenate(columns(mlp_weight, *cuts), axis=1))
    in_pieces = at.deal(in_blocks)
    out_own = attn_weight[:, proj_cols:]

    rest = at.swap(tokens[0]).reshape(-1, width)
    dy = at.swap(cotangent[0]).reshape(-1, width)
    shard = rest.shape[0]
    in_pieces = behind(in_pieces, rest, dy, late_blocks)
    w_in = at.fetch(at.dealt(in_pieces))
    x_near, out_near = behind((at.spread_near(behind(rest, in_pieces)), at.spread_near(behind(out_own, in_pieces))))
    both_got, out_got = behind((at.spread_far(x_near), at.spread_far(out_near)))
    out_rows = at.swap(at.joined(out_own, out_got).reshape(phases, at.half * rows, width))
    out_rows = out_rows.reshape(phases, at.half, rows, width).swapaxes(0, 1).reshape(-1, width)
    w_out = at.fetch(out_rows)
    late_pieces = at.deal(behind(late_blocks, both_got))

    extras = w_in.reshape(-1, rows, w_in.shape[1])[:, :3, gate_end:]
    bias = lax.dynamic_slice_in_dim(extras[:, 0, :bias_len].reshape(-1), head * SLOTS, SLOTS, 0).astype(jnp.float32)
    gain_one = extras[:, 1, :rows].reshape(1, -1).astype(jnp.float32)
    gain_two = extras[:, 2, :rows].reshape(1, -1).astype(jnp.float32)
    lengths_row = lax.dynamic_index_in_dim(lengths[0], at.phase, 0, False)
    seg = segment_ids(lengths_row, ranks * shard)
    both_got, bias, gain_one, gain_two, seg = behind((both_got, bias, gain_one, gain_two, seg))

    got, choices = at.choices(both_got)
    end = (at.rank == 0) | (at.rank == ranks - 1)
    x_all, in_one = place_tokens([rest, *got], choices, at.rank, end, gain_one)
    projected = times(in_one, w_in)
    projected = behind(projected, late_pieces[0], late_pieces[1])
    low, *saved = forward_mix(projected, bias, seg)
    low_near = at.spread_near(low, copies)
    w_mlp = at.fetch(at.dealt(behind(late_pieces, low)))
    w_gate_up, w_down = w_mlp[:, : 2 * share_ff], w_mlp[:, 2 * share_ff :]
    low_got = behind(at.spread_far(low_near))
    low_all = at.joined(low, low_got, 1, copies)

    dy_near = at.spread_near(behind(dy, low_got))
    dy_far = at.spread_far(dy_near)
    after_all = x_all.astype(jnp.float32) + dot(low_all, w_out, NT)
    in_two = (after_all * rms_scale(after_all) * gain_two).astype(jnp.bfloat16)
    after = at.piece(after_all, 0)
    scale_two = rms_scale(after)
    normed_two = after * scale_two

    dyl = at.joined(dy, behind(dy_far, after_all))
    hidden, grad_gate_up = hidden_and_grads(in_two, dyl, w_mlp, share_ff, w_mlp.shape[1], 512)
    aligned = share_ff % 128 == 0
    two_part = times_rows(grad_gate_up, w_mlp if aligned else w_gate_up, 2 * share_ff, 0)
    two_pieces = at.split(two_part)
    two_far = at.sum_far(two_pieces)
    hidden_later, grad_later = behind((hidden, grad_gate_up), two_pieces)
    grad_mlp_w = weight_grads(tn_pair_kernel, 256, in_two, grad_later, dyl, hidden_later)
    passed = behind(two_far[:2], grad_mlp_w)
    two_far = [*passed, *two_far[2:]]
    share_mlp = at.share(behind(grad_mlp_w, passed))
    mlp_part = times_rows(behind(hidden, grad_mlp_w), w_mlp if aligned else w_down, share_ff, 2 if aligned else 0)
    two_near = behind(at.sum_near(two_pieces, two_far), mlp_part)
    back_two = at.total(two_pieces, two_near)
    scaled_two = back_two * gain_two

    grad_after = dy.astype(jnp.float32) + scale_two * (
        scaled_two - normed_two * jnp.mean(scaled_two * normed_two, axis=1, keepdims=True)
    )
    dal = grad_after.astype(jnp.bfloat16)
    don_all = dot(dal, w_out, NN, jnp.bfloat16)
    don_blocks = [
        lax.dynamic_slice_in_dim(don_all, (at.rank ^ j) // copies * HEAD_DIM, HEAD_DIM, 1) for j in range(ranks)
    ]
    don_got = behind([at.across(don_blocks[j], j) for j in range(1, ranks)])
    each = tuple((j,) for j in range(ranks))
    don = place_pieces([don_blocks[0], *don_got], each, at.rank, at.rank)
    dal_parts = dal.reshape(shard, at.seqs, ranks, -1)
    dal_blocks = [lax.dynamic_index_in_dim(dal_parts, at.rank ^ j, 2, False).reshape(shard, -1) for j in range(ranks)]
    dal_blocks = behind(dal_blocks, don_got)
    dal_got = [at.across(dal_blocks[j], j) for j in range(1, ranks)]
    mlp_pieces = at.split(behind(mlp_part, don_got))
    mlp_far = at.sum_far(mlp_pieces)

    grad_proj, bias_grad = backward_mix(projected, bias, seg, saved, don)

    bias_grad = jnp.concatenate([jnp.zeros_like(bias_grad), bias_grad], axis=1)
    row_ids = jnp.arange(width, dtype=jnp.int32)
    owners = SLOTS // bias_len
    holds = ((row_ids % rows == 0) & (row_ids // (rows * owners) == head)).astype(jnp.float32)
    mlp_far, dal_got, grad_proj = behind((mlp_far, dal_got, grad_proj))
    mlp_near = at.sum_near(mlp_pieces, mlp_far)
    grad_in_w = weight_grads(tn_extra_kernel, 512, in_one, grad_proj, holds[:, None], bias_grad)
    one_part = times_rows(behind(grad_proj, grad_in_w), w_in, w_in.shape[1], 0)
    one_pieces = behind(at.split(one_part), mlp_near)
    one_far = at.sum_far(one_pieces)
    quarter = ranks // 4
    dal_rows = place_pieces([dal_blocks[0], *dal_got], each, at.rank, at.rank)
    dal_rows = behind(dal_rows, one_pieces)
    grad_out_w = weight_grads(tn_kernel, min(512, dal_rows.shape[1]), dal_rows, low_all)
    share_mlp = behind(share_mlp, grad_out_w)
    share_in = at.share(behind(grad_in_w, share_mlp))
    share_out = at.share(behind(grad_out_w, grad_in_w))
    home_first = at.home(share_mlp, range(2 * quarter))
    mlp_out = at.total(mlp_pieces, mlp_near)
    mixed_rows = (after + mlp_out).astype(jnp.bfloat16)
    mixed = at.swap(mixed_rows.reshape(phases, block_len, width))[None]
    one_far, home_first, mixed = behind((one_far, home_first, mixed), grad_out_w)
    one_near = at.sum_near(one_pieces, one_far)
    home_second = at.home(behind(share_mlp, home_first), range(2 * quarter, ranks))
    in_home = at.home(behind(share_in, home_first), range(0, ranks, copies))
    back_one = at.total(one_pieces, behind(one_near, home_second[0])) / copies
    scaled_one = back_one * gain_one
    rest_float = rest.astype(jnp.float32)
    scale_one = rms_scale(rest_float)
    normed_one = rest_float * scale_one
    grad_rows = grad_after + scale_one * (
        scaled_one - normed_one * jnp.mean(scaled_one * normed_one, axis=1, keepdims=True)
    )
    grad_tokens = at.swap(grad_rows.reshape(phases, block_len, width))[None]

    mlp_home = home_first + home_second
    gate_up_weight = mlp_weight[:, : 2 * FF].astype(jnp.float32)
    down = at.in_order([p[:, 2 * share_ff :] for p in mlp_home], at.slot, 1).astype(jnp.float32)
    gates = at.in_order([p[:, :share_ff] for p in mlp_home], at.slot, 1).astype(jnp.float32)
    ups = at.in_order([p[:, share_ff : 2 * share_ff] for p in mlp_home], at.slot, 1).astype(jnp.float32)
    grad_mlp = jnp.concatenate([gates, ups, down], axis=1)
    gain_grad_two = jnp.sum(grad_mlp[:, : 2 * FF] * gate_up_weight, axis=1) / norm2_gain.astype(jnp.float32)

    slot_head = at.slot // copies
    parts = [
        at.in_order([p[:, j * HEAD_DIM : (j + 1) * HEAD_DIM] for p in in_home], slot_head, 1) for j in range(3)
    ]
    for j in range(HEADS):
        parts.append(sum(jnp.where(slot_head ^ n == j, p[:, qkv:gate_end], 0) for n, p in enumerate(in_home)))
    parts.append(share_out)
    grad_attn = jnp.concatenate(parts, axis=1).astype(jnp.float32)
    attn_float = attn_weight[:, :proj_cols].astype(jnp.float32)
    gain_grad_one = jnp.sum(grad_attn[:, :proj_cols] * attn_float, axis=1) / norm1_gain.astype(jnp.float32)
    bias_sums = sum(p[0, gate_end : gate_end + SLOTS].astype(jnp.float32) for p in in_home)
    owner = lax.axis_index("seqs") * at.span + lax.axis_index("span")
    bias_home = lax.dynamic_slice_in_dim(bias_sums, owner % owners * bias_len, bias_len, 0)
    return (mixed, grad_tokens, grad_attn, grad_mlp, gain_grad_one, gain_grad_two, bias_home)


def solution(mesh):
    placed = (
        P("seqs", None, "span", None),
        P(("seqs", "span"), None),
        P(("seqs", "span"), None),
        P(("seqs", "span")),
        P(("seqs", "span")),
        P(("seqs", "span")),
        P("seqs", None, None),
        P("seqs", None, "span", None),
    )
    return jax.shard_map(
        local,
        mesh=mesh,
        in_specs=placed,
        out_specs=(
            P("seqs", None, "span", None),
            P("seqs", None, "span", None),
            P(("seqs", "span"), None),
            P(("seqs", "span"), None),
            P(("seqs", "span")),
            P(("seqs", "span")),
            P(("seqs", "span")),
        ),
        check_vma=False,
    )
```

```python
import functools
import jax
import jax.numpy as jnp
from jax import lax
from jax.experimental import pallas as pl
from jax.experimental.pallas import tpu as pltpu
from jax.sharding import PartitionSpec as P

BLOCK = 64
GATE_SOFTENING = 8.0
SUB = 16
SLOTS = 64
HEAD_DIM = 512
NORM_EPS = 1e-05


def mm(a, b, dims):
    return lax.dot_general(
        a.astype(jnp.bfloat16), b.astype(jnp.bfloat16), (dims, ((), ())), preferred_element_type=jnp.float32
    )


def halves(a):
    if a.dtype == jnp.bfloat16:
        return a, None
    high = a.astype(jnp.bfloat16)
    return high, (a - high.astype(jnp.float32)).astype(jnp.bfloat16)


def fine(a, b, dims):
    (a_high, a_low), (b_high, b_low) = halves(a), halves(b)
    out = mm(a_high, b_high, dims)
    if b_low is not None:
        out = out + mm(a_high, b_low, dims)
    if a_low is not None:
        out = out + mm(a_low, b_high, dims)
    return out


NN, NT, TN = ((1,), (0,)), ((1,), (1,)), ((0,), (0,))


def nn(a, b):
    return mm(a, b, NN)


def nt(a, b):
    return mm(a, b, NT)


def tn(a, b):
    return mm(a, b, TN)


def exact(a, b):
    return lax.dot_general(
        a, b, (((1,), (0,)), ((), ())), precision=lax.Precision.HIGHEST, preferred_element_type=jnp.float32
    )


def iota(shape, dim):
    return lax.broadcasted_iota(jnp.int32, shape, dim)


def block_decay(gate, write, seg_col, seg_row, seg_prev):
    row, col = iota((BLOCK, BLOCK), 0), iota((BLOCK, BLOCK), 1)
    same = jnp.where((seg_col == seg_row) & (row >= col), 1.0, 0.0)
    lower = jnp.where(row >= col, 1.0, 0.0)
    cum = exact(lower, gate)
    total = cum[BLOCK - 1 :]
    carry = jnp.where(seg_col == seg_prev, 1.0, 0.0)
    last = jnp.where(seg_col == seg_col[BLOCK - 1 :], 1.0, 0.0)
    enter = jnp.exp(cum) * carry
    tail = jnp.exp(total - cum) * last
    fade = jnp.exp(total) * carry[BLOCK - 1 :]
    falls, rises = [], []
    for i in range(1, BLOCK // SUB):
        base = cum[i * SUB - 1 : i * SUB]
        falls.append(jnp.exp(cum[i * SUB : (i + 1) * SUB] - base))
        rises.append(jnp.exp(base - cum[: i * SUB]))
    return same, cum, enter, tail, fade, falls, rises


def diagonal(square):
    return jnp.concatenate([square[i : i + SUB, i : i + SUB] for i in range(0, BLOCK, SUB)], axis=0)


def undiagonal(strip):
    row, col = iota((BLOCK, BLOCK), 0), iota((BLOCK, BLOCK), 1)
    wide = jnp.concatenate([strip] * (BLOCK // SUB), axis=1)
    return jnp.where(row // SUB == col // SUB, wide, 0.0)


def parts(values):
    return values.reshape(BLOCK // SUB, SUB, values.shape[-1])


def decay_at(cum, j):
    cum_parts = parts(cum)
    return jnp.exp(jnp.minimum(cum_parts - cum_parts[:, j : j + 1], 0.0))


def over_sources(pairs, cum, write, falls, rises):
    strip = parts(diagonal(pairs))
    write_parts = parts(write)
    near = jnp.zeros((BLOCK // SUB, SUB, SLOTS), jnp.float32)
    for j in range(SUB):
        near = near + strip[:, :, j : j + 1] * (decay_at(cum, j) * write_parts[:, j : j + 1])
    near = near.reshape(BLOCK, SLOTS)
    far = [jnp.zeros((SUB, SLOTS), jnp.float32)]
    for i in range(1, BLOCK // SUB):
        rows = pairs[i * SUB : (i + 1) * SUB, : i * SUB]
        far.append(falls[i - 1] * fine(rows, rises[i - 1] * write[: i * SUB], NN))
    return near + jnp.concatenate(far, axis=0)


def over_slots(values, cum, write, falls, rises):
    value_parts, write_parts = parts(values), parts(write)
    lane = iota((BLOCK // SUB, SUB, SUB), 2)
    strip = jnp.zeros((BLOCK // SUB, SUB, SUB), jnp.float32)
    for j in range(SUB):
        term = value_parts * (decay_at(cum, j) * write_parts[:, j : j + 1])
        strip = jnp.where(lane == j, jnp.sum(term, axis=2, keepdims=True), strip)
    out = undiagonal(strip.reshape(BLOCK, SUB))
    far = [jnp.zeros((SUB, BLOCK), jnp.float32)]
    for i in range(1, BLOCK // SUB):
        rows = values[i * SUB : (i + 1) * SUB] * falls[i - 1]
        piece = fine(rows, rises[i - 1] * write[: i * SUB], NT)
        far.append(jnp.concatenate([piece, jnp.zeros((SUB, BLOCK - i * SUB), jnp.float32)], axis=1))
    return out + jnp.concatenate(far, axis=0)


def over_targets(pairs_values, cum, falls, rises):
    row = iota((BLOCK // SUB, SUB, SLOTS), 1)
    near = jnp.zeros((BLOCK // SUB, SUB, SLOTS), jnp.float32)
    strips = [(parts(diagonal(p)), parts(v)) for p, v in pairs_values]
    for j in range(SUB):
        term = sum(strip[:, :, j : j + 1] * value for strip, value in strips) * decay_at(cum, j)
        near = jnp.where(row == j, jnp.sum(term, axis=1, keepdims=True), near)
    out = near.reshape(BLOCK, SLOTS)
    far = jnp.zeros((BLOCK, SLOTS), jnp.float32)
    for i in range(1, BLOCK // SUB):
        here = slice(i * SUB, (i + 1) * SUB)
        piece = sum(fine(p[here, : i * SUB], v[here] * falls[i - 1], TN) for p, v in pairs_values)
        piece = rises[i - 1] * piece
        far = far + jnp.concatenate([piece, jnp.zeros((BLOCK - i * SUB, SLOTS), jnp.float32)], axis=0)
    return out + far


QKV = 3 * HEAD_DIM
GATE_END = QKV + SLOTS


def load_block(i, proj_ref, bias_ref, segc_ref, segr_ref):
    here = pl.ds(pl.multiple_of(i * BLOCK, BLOCK), BLOCK)
    pre = proj_ref[here, :QKV]
    sig = jax.nn.sigmoid(pre)
    feats = (pre * sig).astype(jnp.bfloat16)
    q, k, v = (feats[:, n * HEAD_DIM : (n + 1) * HEAD_DIM] for n in range(3))
    logits = proj_ref[here, QKV:GATE_END] + bias_ref[...]
    gate = (jnp.minimum(logits, 0.0) - jnp.log1p(jnp.exp(-jnp.abs(logits)))) / GATE_SOFTENING
    seg_prev = jnp.where(i > 0, segc_ref[pl.ds(jnp.maximum(i * BLOCK - 1, 0), 1), :], -1)
    return here, pre, sig, q, k, v, logits, gate, -small_exp(gate), segc_ref[here, :], segr_ref[i], seg_prev


def small_exp(x):
    near = x * (1.0 + x / 2 * (1.0 + x / 3 * (1.0 + x / 4 * (1.0 + x / 5 * (1.0 + x / 6)))))
    return jnp.where(x > -0.1, near, jnp.exp(x) - 1.0)


def forward_kernel(proj_ref, bias_ref, segc_ref, segr_ref, low_ref, out_hbm, small_hbm, states_hbm,
                   out_ref, small_ref, states_ref, state, sems):
    scale = HEAD_DIM ** -0.5
    blocks = proj_ref.shape[0] // BLOCK
    state[...] = jnp.zeros_like(state)

    def copies(i):
        here = pl.ds(pl.multiple_of(i * BLOCK, BLOCK), BLOCK)
        return [
            pltpu.make_async_copy(a, b, sems.at[n, i])
            for n, (a, b) in enumerate(
                [
                    (out_ref.at[here], out_hbm.at[here]),
                    (small_ref.at[here], small_hbm.at[here]),
                    (states_ref.at[i], states_hbm.at[i]),
                ]
            )
        ]

    def step(i, _):
        here, _, _, q, k, v, _, gate, write, seg_col, seg_row, seg_prev = load_block(i, proj_ref, bias_ref, segc_ref, segr_ref)
        same, cum, enter, tail, fade, falls, rises = block_decay(gate, write, seg_col, seg_row, seg_prev)
        keys_in, values_in = state[:SLOTS], state[SLOTS:]
        states_ref[i] = state[...]
        keep = fade.reshape(SLOTS, 1)
        send = tail * write
        state[:SLOTS] = keep * keys_in + fine(send, k, TN)
        state[SLOTS:] = keep * values_in + fine(send, v, TN)
        pairs = nt(q, k) * same
        score = scale * (over_sources(pairs, cum, write, falls, rises) + enter * fine(q, keys_in, NT))
        prob = jnp.exp(score - jnp.max(score, axis=1, keepdims=True))
        prob = prob / jnp.sum(prob, axis=1, keepdims=True)
        mix = over_slots(prob, cum, write, falls, rises) * same
        out = fine(mix, v, NN) + fine(prob * enter, values_in, NN)
        low_ref[here, :] = (out * lax.rsqrt(jnp.mean(out * out, axis=1, keepdims=True) + NORM_EPS)).astype(jnp.bfloat16)
        out_ref[here, :] = out
        small_ref[here, :] = jnp.concatenate([score, prob, pairs, mix], axis=1)
        for copy in copies(i):
            copy.start()
        return 0

    lax.fori_loop(0, blocks, step, 0, unroll=4)

    def finish(i, _):
        for copy in copies(i):
            copy.wait()
        return 0

    lax.fori_loop(0, blocks, finish, 0)


def backward_kernel(proj_ref, bias_ref, segc_ref, segr_ref, out_ref, small_ref, states_ref, don_ref,
                    grad_ref, bias_grad_ref, state, state_next):
    scale = HEAD_DIM ** -0.5
    blocks = proj_ref.shape[0] // BLOCK
    state[...] = jnp.zeros_like(state)
    state_next[...] = jnp.zeros_like(state)
    bias_grad_ref[...] = jnp.zeros_like(bias_grad_ref)

    def step(lap, _):
        i = blocks - 1 - lap
        here, pre, sig, q, k, v, logits, gate, write, seg_col, seg_row, seg_prev = load_block(i, proj_ref, bias_ref, segc_ref, segr_ref)
        same, cum, enter, tail, fade, falls, rises = block_decay(gate, write, seg_col, seg_row, seg_prev)
        last = jnp.where(seg_col == seg_col[BLOCK - 1 :], 1.0, 0.0)
        score, prob, pairs, mix = (small_ref[here, n * SLOTS : (n + 1) * SLOTS] for n in range(4))
        states_in = states_ref[i]
        keys_in, values_in = states_in[:SLOTS], states_in[SLOTS:]
        out, don = out_ref[here, :], don_ref[here, :]
        unit = lax.rsqrt(jnp.mean(out * out, axis=1, keepdims=True) + NORM_EPS)
        normed = out * unit
        dout = unit * (don - normed * jnp.mean(don * normed, axis=1, keepdims=True))
        dmix = fine(dout, v, NT) * same
        dprob = over_sources(dmix, cum, write, falls, rises) + enter * fine(dout, values_in, NT)
        inner = prob * dprob
        dscore = inner - prob * jnp.sum(inner, axis=1, keepdims=True)
        slope = scale * dscore
        dpairs = over_slots(slope, cum, write, falls, rises) * same
        dcross = slope * enter
        dstate = state[...]
        dkeys, dvalues = dstate[:SLOTS], dstate[SLOTS:]
        send = tail * write
        dfeats = jnp.concatenate(
            [
                nn(dpairs, k) + nn(dcross, keys_in),
                tn(dpairs, q) + nn(send, dkeys),
                tn(mix, dout) + nn(send, dvalues),
            ],
            axis=1,
        )
        grad_ref[here, :QKV] = (dfeats * (sig * (1.0 + pre * (1.0 - sig)))).astype(jnp.bfloat16)
        heard = over_targets([(pairs, slope), (dmix, prob)], cum, falls, rises)
        heard = heard + tail * (fine(k, dkeys, NT) + fine(v, dvalues, NT))
        product = dstate * state_next[...]
        held = lax.dot_general(jnp.ones((8, HEAD_DIM), jnp.float32), product[:SLOTS] + product[SLOTS:],
                               (((1,), (1,)), ((), ())), precision=lax.Precision.HIGHEST, preferred_element_type=jnp.float32)[:1]
        flow = exact(same.T, dscore * score + inner - write * heard)
        dgate = flow - (1.0 - write) * heard + last * held
        dlogits = (dgate * jax.nn.sigmoid(-logits) / GATE_SOFTENING).astype(jnp.bfloat16)
        grad_ref[here, QKV:] = jnp.concatenate([dlogits, jnp.zeros_like(dlogits)], axis=1)
        bias_grad_ref[...] += jnp.sum(dlogits.astype(jnp.float32), axis=0, keepdims=True)
        keep = fade.reshape(SLOTS, 1)
        state[:SLOTS] = keep * dkeys + fine(dcross, q, TN)
        state[SLOTS:] = keep * dvalues + fine(prob * enter, dout, TN)
        state_next[...] = states_in
        return 0

    lax.fori_loop(0, blocks, step, 0)


VMEM = pl.BlockSpec(memory_space=pltpu.VMEM)


def slot_call(kernel, outs, out_specs, scratch, args, cost):
    return pl.pallas_call(
        kernel,
        out_shape=outs,
        in_specs=[VMEM] * len(args),
        out_specs=out_specs,
        scratch_shapes=scratch,
        cost_estimate=pl.CostEstimate(flops=cost, bytes_accessed=0, transcendentals=0),
        compiler_params=pltpu.CompilerParams(vmem_limit_bytes=58 * 2**20),
    )(*args)


def forward_mix(proj, bias, seg):
    length = proj.shape[0]
    blocks = length // BLOCK
    shapes = [(length, HEAD_DIM), (length, 4 * SLOTS), (blocks, 2 * SLOTS, HEAD_DIM)]
    outs = [jax.ShapeDtypeStruct((length, HEAD_DIM), jnp.bfloat16)] + [jax.ShapeDtypeStruct(n, jnp.float32) for n in shapes]
    specs = [VMEM] + [pl.BlockSpec(memory_space=pltpu.HBM)] * 3
    scratch = [pltpu.VMEM(n, jnp.float32) for n in shapes]
    scratch += [pltpu.VMEM((2 * SLOTS, HEAD_DIM), jnp.float32), pltpu.SemaphoreType.DMA((3, blocks))]
    args = (proj, bias.reshape(1, SLOTS), seg.reshape(length, 1), seg.reshape(blocks, 1, BLOCK))
    return slot_call(forward_kernel, outs, specs, scratch, args, 12 * 10**9)


def backward_mix(proj, bias, seg, saved, don):
    length = proj.shape[0]
    blocks = length // BLOCK
    outs = [jax.ShapeDtypeStruct(proj.shape, jnp.bfloat16), jax.ShapeDtypeStruct((1, SLOTS), jnp.float32)]
    scratch = [pltpu.VMEM((2 * SLOTS, HEAD_DIM), jnp.float32)] * 2
    args = (proj, bias.reshape(1, SLOTS), seg.reshape(length, 1), seg.reshape(blocks, 1, BLOCK), *saved, don)
    return slot_call(backward_kernel, outs, [VMEM] * 2, scratch, args, 16 * 10**9)


HEADS = 4


def product_cost(*sizes):
    flops = 2
    for size in sizes:
        flops *= size
    return pl.CostEstimate(flops=flops, bytes_accessed=2 * sizes[1] * sizes[2], transcendentals=0)


def move_cost(nbytes):
    return pl.CostEstimate(flops=0, bytes_accessed=nbytes, transcendentals=0)
FF = 5632


def dot(a, b, dims, kind=jnp.float32):
    out = lax.dot_general(a, b, (dims, ((), ())), preferred_element_type=jnp.float32)
    return out.astype(kind)


def rms_scale(values):
    return lax.rsqrt(jnp.mean(values * values, axis=-1, keepdims=True) + NORM_EPS)


def plus(a, b):
    return (a.astype(jnp.float32) + b.astype(jnp.float32)).astype(a.dtype)


def behind(value, *others):
    return lax.optimization_barrier((value, others))[0]


def tn_pair_kernel(a_ref, b_ref, c_ref, d_ref, out_ref):
    width = b_ref.shape[1]
    out_ref[:, :width] = dot(a_ref[...], b_ref[...], TN, jnp.bfloat16)
    out_ref[:, width:] = dot(c_ref[...], d_ref[...], TN, jnp.bfloat16)


def tn_kernel(a_ref, b_ref, out_ref):
    out_ref[...] = dot(a_ref[...], b_ref[...], TN, jnp.bfloat16)


def tn_extra_kernel(a_ref, b_ref, e_ref, f_ref, out_ref):
    out, last = dot(a_ref[...], b_ref[...], TN), b_ref.shape[1] - 128
    out_ref[:, :last] = out[:, :last].astype(jnp.bfloat16)
    out_ref[:, last:] = (out[:, last:] + e_ref[...] * f_ref[...]).astype(jnp.bfloat16)


def weight_grads(kernel, block, *operands):
    length, rows = operands[0].shape
    cols = sum(v.shape[1] for v in operands[1:4:2]) if kernel is tn_pair_kernel else operands[1].shape[1]
    whole = lambda v: pl.BlockSpec(v.shape, lambda i: (0, 0))
    strip = pl.BlockSpec((length, block), lambda i: (0, i))
    specs = [strip, whole(operands[1])]
    if kernel is tn_pair_kernel:
        specs += [strip, whole(operands[3])]
    elif kernel is tn_extra_kernel:
        specs += [pl.BlockSpec((block, 1), lambda i: (i, 0)), whole(operands[3])]
    return pl.pallas_call(
        kernel,
        grid=(rows // block,),
        in_specs=specs,
        out_specs=pl.BlockSpec((block, cols), lambda i: (i, 0)),
        out_shape=jax.ShapeDtypeStruct((rows, cols), jnp.bfloat16),
        cost_estimate=product_cost(length, rows, cols),
        compiler_params=pltpu.CompilerParams(vmem_limit_bytes=48 * 2**20),
    )(*operands)


def attn_grads_kernel(owned, parts, a_ref, b_ref, holds_ref, bias_ref, c_ref, d_ref, out_ref):
    width, cols = b_ref.shape[1], d_ref.shape[1] // parts
    first = dot(a_ref[...], b_ref[...], TN)
    out_ref[:, : width - 128] = first[:, : width - 128].astype(jnp.bfloat16)
    extra = holds_ref[...] * bias_ref[...]
    out_ref[:, width - 128 : width] = (first[:, width - 128 :] + extra).astype(jnp.bfloat16)
    second = dot(c_ref[...], d_ref[...], TN, jnp.bfloat16)
    for owner in range(second.shape[0] // owned):
        for part in range(parts):
            place = (owner * parts + part) * owned
            tile = second[owner * owned : (owner + 1) * owned, part * cols : (part + 1) * cols]
            out_ref[place : place + owned, width:] = tile


def attn_grads(a, b, holds, bias, c, d, owned, parts):
    (length, rows), width = a.shape, b.shape[1]
    step = 128 // owned
    block, cols = step * owned * parts, width + d.shape[1] // parts
    whole = lambda v: pl.BlockSpec(v.shape, lambda i: (0, 0))
    return pl.pallas_call(
        functools.partial(attn_grads_kernel, owned, parts),
        grid=(rows // block,),
        in_specs=[
            pl.BlockSpec((length, block), lambda i: (0, i)), whole(b), pl.BlockSpec((block, 1), lambda i: (i, 0)),
            whole(bias), pl.BlockSpec((length, 128), lambda i: (0, i)), whole(d),
        ],
        out_specs=pl.BlockSpec((block, cols), lambda i: (i, 0)),
        out_shape=jax.ShapeDtypeStruct((rows, cols), jnp.bfloat16),
        cost_estimate=product_cost(length, rows, cols),
        compiler_params=pltpu.CompilerParams(vmem_limit_bytes=56 * 2**20),
    )(a, b, holds, bias, c, d)


def hidden_kernel(width, x_ref, y_ref, w_ref, hid_ref, grad_ref, acc):
    step = pl.program_id(0)

    @pl.when(step == 0)
    def _():
        acc[...] = jnp.zeros_like(acc)

    acc[:, : 2 * width] += dot(x_ref[...], w_ref[:, : 2 * width], NN)
    acc[:, 2 * width :] += dot(y_ref[...], w_ref[:, 2 * width : 3 * width], NN)

    @pl.when(step == pl.num_programs(0) - 1)
    def _():
        gate, up, back = acc[:, :width], acc[:, width : 2 * width], acc[:, 2 * width :]
        sig = jax.nn.sigmoid(gate)
        act = gate * sig
        hid_ref[...] = (act * up).astype(jnp.bfloat16)
        grad_ref[:, :width] = (back * up * (sig * (1.0 + gate * (1.0 - sig)))).astype(jnp.bfloat16)
        grad_ref[:, width:] = (back * act).astype(jnp.bfloat16)


def hidden_and_grads(x, y, weights, width, cols, block):
    length, depth = x.shape
    strip = pl.BlockSpec((length, block), lambda i: (0, i))
    return pl.pallas_call(
        functools.partial(hidden_kernel, width),
        grid=(depth // block,),
        in_specs=[strip, strip, pl.BlockSpec((block, cols), lambda i: (i, 0))],
        out_specs=[pl.BlockSpec((length, n * width), lambda i: (0, 0)) for n in (1, 2)],
        out_shape=[jax.ShapeDtypeStruct((length, n * width), jnp.bfloat16) for n in (1, 2)],
        scratch_shapes=[pltpu.VMEM((length, 3 * width), jnp.float32)],
        cost_estimate=product_cost(length, depth, 3 * width),
        compiler_params=pltpu.CompilerParams(vmem_limit_bytes=56 * 2**20),
    )(x, y, weights)


def head_blocks_kernel(copies, place_ref, w_ref, extra_ref, *out_refs):
    width = HEADS * HEAD_DIM
    for k, out_ref in enumerate(out_refs):
        head = (place_ref[0] ^ k) // copies
        for n in range(3):
            start = pl.multiple_of(n * width + head * HEAD_DIM, HEAD_DIM)
            out_ref[:, n * HEAD_DIM : (n + 1) * HEAD_DIM] = w_ref[:, pl.ds(start, HEAD_DIM)]
        two = w_ref[:, pl.ds(pl.multiple_of(3 * width + head // 2 * 128, 128), 128)].astype(jnp.float32)
        gate = jnp.where(head % 2 == 0, two[:, :SLOTS], two[:, SLOTS:]).astype(jnp.bfloat16)
        out_ref[:, QKV:] = jnp.concatenate([gate, extra_ref[...]], axis=1)


def head_blocks(weight, extra, slot, ranks):
    rows = weight.shape[0]
    shape = jax.ShapeDtypeStruct((rows, QKV + 2 * SLOTS), jnp.bfloat16)
    return pl.pallas_call(
        functools.partial(head_blocks_kernel, ranks // HEADS),
        out_shape=[shape] * ranks,
        in_specs=[pl.BlockSpec(memory_space=pltpu.SMEM), VMEM, VMEM],
        out_specs=[VMEM] * ranks,
        cost_estimate=move_cost(4 * ranks * rows * (QKV + 2 * SLOTS)),
        compiler_params=pltpu.CompilerParams(vmem_limit_bytes=32 * 2**20),
    )(slot.reshape(1).astype(jnp.int32), weight, extra)


def place_kernel(axis, choices, place_ref, *refs):
    pieces, out_ref = refs[:-1], refs[-1]
    size = pieces[0].shape[axis]

    def put(k, piece):
        start = pl.multiple_of((place_ref[0] ^ k) * size, size)
        where = (pl.ds(start, size), slice(None)) if axis == 0 else (slice(None), pl.ds(start, size))
        out_ref[where] = piece[...]

    for k, choice in enumerate(choices):
        if len(choice) == 1:
            put(k, pieces[choice[0]])
        else:
            pl.when(place_ref[1] == 1)(functools.partial(put, k, pieces[choice[0]]))
            pl.when(place_ref[1] == 0)(functools.partial(put, k, pieces[choice[1]]))


def place_pieces(pieces, choices, first, end, axis=0):
    shape = list(pieces[0].shape)
    shape[axis] *= len(choices)
    vmem = pl.BlockSpec(memory_space=pltpu.VMEM)
    return pl.pallas_call(
        functools.partial(place_kernel, axis, choices),
        out_shape=jax.ShapeDtypeStruct(shape, pieces[0].dtype),
        in_specs=[pl.BlockSpec(memory_space=pltpu.SMEM)] + [vmem] * len(pieces),
        out_specs=vmem,
        cost_estimate=move_cost(4 * shape[0] * shape[1]),
        compiler_params=pltpu.CompilerParams(vmem_limit_bytes=48 * 2**20),
    )(jnp.stack([first, end]).astype(jnp.int32), *pieces)


def tokens_kernel(choices, place_ref, gain_ref, *refs):
    pieces, (x_ref, normed_ref) = refs[:-2], refs[-2:]
    size = pieces[0].shape[0]

    def put(k, piece):
        here = pl.ds(pl.multiple_of((place_ref[0] ^ k) * size, size), size)
        x_ref[here, :] = piece[...]
        values = piece[...].astype(jnp.float32)
        normed_ref[here, :] = (values * rms_scale(values) * gain_ref[...]).astype(jnp.bfloat16)

    for k, choice in enumerate(choices):
        if len(choice) == 1:
            put(k, pieces[choice[0]])
        else:
            pl.when(place_ref[1] == 1)(functools.partial(put, k, pieces[choice[0]]))
            pl.when(place_ref[1] == 0)(functools.partial(put, k, pieces[choice[1]]))


def place_tokens(pieces, choices, first, end, gain):
    size, width = pieces[0].shape
    shape = jax.ShapeDtypeStruct((len(choices) * size, width), jnp.bfloat16)
    return pl.pallas_call(
        functools.partial(tokens_kernel, choices),
        out_shape=[shape] * 2,
        in_specs=[pl.BlockSpec(memory_space=pltpu.SMEM)] + [VMEM] * (len(pieces) + 1),
        out_specs=[VMEM] * 2,
        cost_estimate=move_cost(10 * len(choices) * size * width),
        compiler_params=pltpu.CompilerParams(vmem_limit_bytes=48 * 2**20),
    )(jnp.stack([first, end]).astype(jnp.int32), gain, *pieces)


def nt_kernel(a_ref, b_ref, out_ref):
    out_ref[...] = dot(a_ref[...], b_ref[...], NT, out_ref.dtype)


def times_rows(a, weights, cols, place, block=512):
    length = a.shape[0]
    return pl.pallas_call(
        nt_kernel,
        grid=(weights.shape[0] // block,),
        in_specs=[pl.BlockSpec(a.shape, lambda i: (0, 0)), pl.BlockSpec((block, cols), lambda i: (i, place))],
        out_specs=pl.BlockSpec((length, block), lambda i: (0, i)),
        out_shape=jax.ShapeDtypeStruct((length, weights.shape[0]), jnp.bfloat16),
        cost_estimate=product_cost(length, weights.shape[0], cols),
        compiler_params=pltpu.CompilerParams(vmem_limit_bytes=48 * 2**20),
    )(a, weights)


def nn_kernel(a_ref, b_ref, out_ref):
    @pl.when(pl.program_id(0) == 0)
    def _():
        out_ref[...] = jnp.zeros_like(out_ref)

    out_ref[...] += dot(a_ref[...], b_ref[...], NN)


def times(a, weights, block=1024):
    length, depth = a.shape
    cols = weights.shape[1]
    return pl.pallas_call(
        nn_kernel,
        grid=(depth // block,),
        in_specs=[pl.BlockSpec((length, block), lambda i: (0, i)), pl.BlockSpec((block, cols), lambda i: (i, 0))],
        out_specs=pl.BlockSpec((length, cols), lambda i: (0, 0)),
        out_shape=jax.ShapeDtypeStruct((length, cols), jnp.float32),
        cost_estimate=product_cost(length, depth, cols),
        compiler_params=pltpu.CompilerParams(vmem_limit_bytes=48 * 2**20),
    )(a, weights)


class Layout:
    def __init__(self, phases):
        self.seqs, self.span, self.phases = lax.axis_size("seqs"), lax.axis_size("span"), phases
        self.ranks = self.span // phases
        self.half = self.ranks // phases
        place = lax.axis_index("span")
        self.rank, self.phase = place // phases, place % phases
        self.slot = (self.rank % self.half) * phases + self.phase
        self.groups = [
            [s * self.span + z * phases + c for s in range(self.seqs) for c in range(phases)]
            for z in range(self.ranks)
        ]

    def across(self, value, k):
        step = k * self.phases
        return lax.ppermute(value, "span", [(i, i ^ step) for i in range(self.span)])

    def outward(self, k):
        pairs = []
        for i in range(self.span):
            z, c = divmod(i, self.phases)
            slot = (z % self.half) * self.phases + c
            pairs.append((i, (slot ^ k) * self.phases + z // self.half))
        return pairs

    def swap(self, value):
        mine = lax.dynamic_index_in_dim(value, self.phase, 0, False)
        other = lax.dynamic_index_in_dim(value, 1 - self.phase, 0, False)
        got = lax.ppermute(other, "span", [(i, i ^ 1) for i in range(self.span)])
        first = self.phase == 0
        return jnp.stack([jnp.where(first, mine, got), jnp.where(first, got, mine)])

    def between(self, value, pairs):
        p = self.phases
        return lax.ppermute(value, "span", [(a * p + c, b * p + c) for a, b in pairs for c in range(p)])

    def spread_near(self, value, step=1):
        if self.ranks != 4:
            return [self.across(value, k) for k in range(step, self.ranks, step)]
        return [self.across(value, 1), self.between(value, [(1, 2), (2, 1)]), self.between(value, [(0, 3), (3, 0)])]

    def spread_far(self, got):
        if self.ranks != 4:
            return got
        near, middle, ends = got
        near, middle = behind((near, middle))
        inner = self.between(near, [(1, 2), (2, 1)])
        return [near, middle, ends, inner, self.between(middle, [(1, 0), (2, 3)])]

    def choices(self, got):
        if self.ranks == 4:
            near, middle, ends, inner, outer = got
            return [near, outer, inner, ends, middle], ((0,), (1,), (2, 3), (4, 5))
        return got, tuple((k,) for k in range(len(got) + 1))

    def joined(self, own, got, axis=0, step=1):
        pieces, choices = self.choices(got)
        end = (self.rank == 0) | (self.rank == self.ranks - 1)
        return place_pieces([own, *pieces], choices, self.rank // step, end, axis)

    def dealt(self, pieces):
        return place_pieces(pieces, tuple((k,) for k in range(len(pieces))), self.rank, self.rank)

    def in_order(self, pieces, first, axis=0):
        size = pieces[0].shape[axis]
        shape = list(pieces[0].shape)
        shape[axis] = len(pieces) * size
        out = jnp.zeros(shape, pieces[0].dtype)
        for k, piece in enumerate(pieces):
            out = lax.dynamic_update_slice_in_dim(out, piece, (first ^ k) * size, axis)
        return out

    def spread(self, value):
        return behind(self.spread_far(self.spread_near(value)))

    def gather(self, value):
        return self.joined(value, self.spread(value))

    def piece(self, value, k):
        size = value.shape[0] // self.ranks
        return lax.dynamic_slice_in_dim(value, (self.rank ^ k) * size, size, 0)

    def split(self, value):
        return [self.piece(value, k) for k in range(self.ranks)]

    def sum_far(self, pieces):
        if self.ranks != 4:
            return [self.across(pieces[k], k) for k in range(1, self.ranks)]
        inner, outer = (self.between(pieces[2], pairs) for pairs in ([(1, 2), (2, 1)], [(0, 1), (3, 2)]))
        return [inner, outer, self.between(pieces[3], [(0, 3), (3, 0)])]

    def sum_near(self, pieces, got):
        if self.ranks != 4:
            return got
        inner, outer, ends = got
        inner, outer = behind((inner, outer))
        near = self.across(plus(pieces[1], inner), 1)
        return [near, self.between(plus(pieces[3], outer), [(1, 2), (2, 1)]), ends]

    def total(self, pieces, got):
        out = pieces[0].astype(jnp.float32)
        for piece in got:
            out = out + piece.astype(jnp.float32)
        return out

    def deal(self, blocks):
        return [lax.ppermute(block, "span", self.outward(k)) for k, block in enumerate(blocks)]

    def home(self, rows_of, places):
        blocks = rows_of.reshape(self.ranks, -1, rows_of.shape[1])
        pieces = []
        for k in places:
            block = lax.dynamic_index_in_dim(blocks, self.rank ^ k, 0, False)
            pieces.append(lax.ppermute(block, "span", [(b, a) for a, b in self.outward(k)]))
        return pieces

    def fetch(self, value):
        return lax.all_gather(value, ("seqs", "span"), axis=0, tiled=True, axis_index_groups=self.groups)

    def share(self, value):
        return lax.psum_scatter(
            value, ("seqs", "span"), scatter_dimension=0, tiled=True, axis_index_groups=self.groups
        )


def segment_ids(lengths_row, count):
    offsets = jnp.cumsum(lengths_row) - lengths_row
    positions = jnp.arange(count, dtype=jnp.int32)
    return jnp.sum((positions[:, None] >= offsets[None, 1:]).astype(jnp.int32), axis=1)


def local(tokens, attn_weight, mlp_weight, norm1_gain, norm2_gain, gate_bias, lengths, cotangent):
    phases, block_len, width = tokens.shape[1:]
    at = Layout(phases)
    rows = attn_weight.shape[0]
    ranks, copies = at.ranks, at.ranks // HEADS
    proj_cols = 3 * width + HEADS * SLOTS
    share_ff = FF // ranks
    qkv = 3 * HEAD_DIM
    gate_end = qkv + SLOTS
    bias_len = gate_bias.shape[0]
    head = at.rank // copies

    def columns(weight, *cuts):
        return [lax.dynamic_slice_in_dim(weight, start, size, 1) for start, size in cuts]

    across = lambda v: jnp.pad(v, (0, SLOTS - v.shape[0]))[None, :]
    row = lax.broadcasted_iota(jnp.int32, (rows, SLOTS), 0)
    extra = jnp.where(row == 1, across(norm1_gain), jnp.where(row == 2, across(norm2_gain), 0))
    extra = jnp.where(row == 0, across(gate_bias), extra).astype(jnp.bfloat16)
    in_blocks, late_blocks = head_blocks(attn_weight[:, :proj_cols], extra, at.slot, ranks), []
    for j in range(ranks):
        cuts = [(n * FF + (at.slot ^ j) * share_ff, share_ff) for n in range(3)]
        late_blocks.append(jnp.concatenate(columns(mlp_weight, *cuts), axis=1))
    in_pieces = at.deal(in_blocks)
    out_own = attn_weight[:, proj_cols:]

    rest = at.swap(tokens[0]).reshape(-1, width)
    dy = at.swap(cotangent[0]).reshape(-1, width)
    shard = rest.shape[0]
    in_pieces = behind(in_pieces, rest, dy, late_blocks)
    w_in = at.fetch(at.dealt(in_pieces))
    x_near, out_near = behind((at.spread_near(behind(rest, in_pieces)), at.spread_near(behind(out_own, in_pieces))))
    both_got, out_got = behind((at.spread_far(x_near), at.spread_far(out_near)))
    out_rows = at.swap(at.joined(out_own, out_got).reshape(phases, at.half * rows, width))
    out_rows = out_rows.reshape(phases, at.half, rows, width).swapaxes(0, 1).reshape(-1, width)
    w_out = at.fetch(out_rows)
    late_pieces = at.deal(behind(late_blocks, both_got))

    extras = w_in.reshape(-1, rows, w_in.shape[1])[:, :3, gate_end:]
    bias = lax.dynamic_slice_in_dim(extras[:, 0, :bias_len].reshape(-1), head * SLOTS, SLOTS, 0).astype(jnp.float32)
    gain_one = extras[:, 1, :rows].reshape(1, -1).astype(jnp.float32)
    gain_two = extras[:, 2, :rows].reshape(1, -1).astype(jnp.float32)
    lengths_row = lax.dynamic_index_in_dim(lengths[0], at.phase, 0, False)
    seg = segment_ids(lengths_row, ranks * shard)
    both_got, bias, gain_one, gain_two, seg = behind((both_got, bias, gain_one, gain_two, seg))

    got, choices = at.choices(both_got)
    end = (at.rank == 0) | (at.rank == ranks - 1)
    x_all, in_one = place_tokens([rest, *got], choices, at.rank, end, gain_one)
    projected = times(in_one, w_in)
    projected = behind(projected, late_pieces[0], late_pieces[1])
    low, *saved = forward_mix(projected, bias, seg)
    low_near = at.spread_near(low, copies)
    w_mlp = at.fetch(at.dealt(behind(late_pieces, low)))
    w_gate_up, w_down = w_mlp[:, : 2 * share_ff], w_mlp[:, 2 * share_ff :]
    low_got = behind(at.spread_far(low_near))
    low_all = at.joined(low, low_got, 1, copies)

    dy_near = at.spread_near(behind(dy, low_near[:2]))
    dy_far = at.spread_far(dy_near)
    after_all = x_all.astype(jnp.float32) + dot(low_all, w_out, NT)
    in_two = (after_all * rms_scale(after_all) * gain_two).astype(jnp.bfloat16)
    after = at.piece(after_all, 0)
    scale_two = rms_scale(after)
    normed_two = after * scale_two

    dyl = at.joined(dy, behind(dy_far, after_all))
    hidden, grad_gate_up = hidden_and_grads(in_two, dyl, w_mlp, share_ff, w_mlp.shape[1], 512)
    aligned = share_ff % 128 == 0
    two_part = times_rows(grad_gate_up, w_mlp if aligned else w_gate_up, 2 * share_ff, 0)
    two_pieces = at.split(two_part)
    two_far = at.sum_far(two_pieces)
    hidden_later, grad_later = behind((hidden, grad_gate_up), two_pieces)
    grad_mlp_w = weight_grads(tn_pair_kernel, 256, in_two, grad_later, dyl, hidden_later)
    passed = behind(two_far[:2], grad_mlp_w)
    two_far = [*passed, *two_far[2:]]
    share_mlp = at.share(behind(grad_mlp_w, passed))
    mlp_part = times_rows(behind(hidden, grad_mlp_w), w_mlp if aligned else w_down, share_ff, 2 if aligned else 0)
    two_near = behind(at.sum_near(two_pieces, two_far), mlp_part)
    back_two = at.total(two_pieces, two_near)
    scaled_two = back_two * gain_two

    grad_after = dy.astype(jnp.float32) + scale_two * (
        scaled_two - normed_two * jnp.mean(scaled_two * normed_two, axis=1, keepdims=True)
    )
    dal = grad_after.astype(jnp.bfloat16)
    don_all = dot(dal, w_out, NN, jnp.bfloat16)
    don_blocks = [
        lax.dynamic_slice_in_dim(don_all, (at.rank ^ j) // copies * HEAD_DIM, HEAD_DIM, 1) for j in range(ranks)
    ]
    don_got = behind([at.across(don_blocks[j], j) for j in range(1, ranks)])
    each = tuple((j,) for j in range(ranks))
    don = place_pieces([don_blocks[0], *don_got], each, at.rank, at.rank)
    dal_parts = dal.reshape(shard, at.seqs, ranks, -1)
    dal_blocks = [lax.dynamic_index_in_dim(dal_parts, at.rank ^ j, 2, False).reshape(shard, -1) for j in range(ranks)]
    dal_blocks = behind(dal_blocks, don_got)
    dal_got = [at.across(dal_blocks[j], j) for j in range(1, ranks)]
    mlp_pieces = at.split(behind(mlp_part, don_got))
    mlp_far = at.sum_far(mlp_pieces)

    grad_proj, bias_grad = backward_mix(projected, bias, seg, saved, don)

    bias_grad = jnp.concatenate([jnp.zeros_like(bias_grad), bias_grad], axis=1)
    row_ids = jnp.arange(width, dtype=jnp.int32)
    owners = SLOTS // bias_len
    holds = ((row_ids % rows == 0) & (row_ids // (rows * owners) == head)).astype(jnp.float32)
    mlp_far, dal_got, grad_proj = behind((mlp_far, dal_got, grad_proj))
    mlp_near = at.sum_near(mlp_pieces, mlp_far)
    dal_rows = place_pieces([dal_blocks[0], *dal_got], each, at.rank, at.rank)
    grad_attn_w = attn_grads(in_one, grad_proj, holds[:, None], bias_grad, dal_rows, low_all, rows, ranks)
    one_part = times_rows(behind(grad_proj, grad_attn_w), w_in, w_in.shape[1], 0)
    one_pieces = behind(at.split(one_part), mlp_near)
    one_far = at.sum_far(one_pieces)
    quarter = ranks // 4
    share_mlp = behind(share_mlp, one_pieces)
    share_attn = at.share(behind(grad_attn_w, share_mlp))
    home_first = at.home(share_mlp, range(2 * quarter))
    mlp_out = at.total(mlp_pieces, mlp_near)
    mixed_rows = (after + mlp_out).astype(jnp.bfloat16)
    mixed = at.swap(mixed_rows.reshape(phases, block_len, width))[None]
    one_far, home_first, mixed = behind((one_far, home_first, mixed))
    one_near = at.sum_near(one_pieces, one_far)
    home_second = at.home(behind(share_mlp, home_first), range(2 * quarter, ranks))
    in_home = at.home(behind(share_attn[:, : gate_end + SLOTS], home_first), range(0, ranks, copies))
    back_one = at.total(one_pieces, behind(one_near, home_second[0], in_home[0], in_home[1])) / copies
    scaled_one = back_one * gain_one
    rest_float = rest.astype(jnp.float32)
    scale_one = rms_scale(rest_float)
    normed_one = rest_float * scale_one
    grad_rows = grad_after + scale_one * (
        scaled_one - normed_one * jnp.mean(scaled_one * normed_one, axis=1, keepdims=True)
    )
    grad_tokens = at.swap(grad_rows.reshape(phases, block_len, width))[None]

    mlp_home = home_first + home_second
    gate_up_weight = mlp_weight[:, : 2 * FF].astype(jnp.float32)
    down = at.in_order([p[:, 2 * share_ff :] for p in mlp_home], at.slot, 1).astype(jnp.float32)
    gates = at.in_order([p[:, :share_ff] for p in mlp_home], at.slot, 1).astype(jnp.float32)
    ups = at.in_order([p[:, share_ff : 2 * share_ff] for p in mlp_home], at.slot, 1).astype(jnp.float32)
    grad_mlp = jnp.concatenate([gates, ups, down], axis=1)
    gain_grad_two = jnp.sum(grad_mlp[:, : 2 * FF] * gate_up_weight, axis=1) / norm2_gain.astype(jnp.float32)

    slot_head = at.slot // copies
    parts = [
        at.in_order([p[:, j * HEAD_DIM : (j + 1) * HEAD_DIM] for p in in_home], slot_head, 1) for j in range(3)
    ]
    for j in range(HEADS):
        parts.append(sum(jnp.where(slot_head ^ n == j, p[:, qkv:gate_end], 0) for n, p in enumerate(in_home)))
    by_part = share_attn[:, gate_end + SLOTS :].reshape(ranks, rows, -1)
    parts += [by_part[j] for j in range(ranks)]
    grad_attn = jnp.concatenate(parts, axis=1).astype(jnp.float32)
    attn_float = attn_weight[:, :proj_cols].astype(jnp.float32)
    gain_grad_one = jnp.sum(grad_attn[:, :proj_cols] * attn_float, axis=1) / norm1_gain.astype(jnp.float32)
    bias_sums = sum(p[0, gate_end : gate_end + SLOTS].astype(jnp.float32) for p in in_home)
    owner = lax.axis_index("seqs") * at.span + lax.axis_index("span")
    bias_home = lax.dynamic_slice_in_dim(bias_sums, owner % owners * bias_len, bias_len, 0)
    return (mixed, grad_tokens, grad_attn, grad_mlp, gain_grad_one, gain_grad_two, bias_home)


def solution(mesh):
    placed = (
        P("seqs", None, "span", None),
        P(("seqs", "span"), None),
        P(("seqs", "span"), None),
        P(("seqs", "span")),
        P(("seqs", "span")),
        P(("seqs", "span")),
        P("seqs", None, None),
        P("seqs", None, "span", None),
    )
    return jax.shard_map(
        local,
        mesh=mesh,
        in_specs=placed,
        out_specs=(
            P("seqs", None, "span", None),
            P("seqs", None, "span", None),
            P(("seqs", "span"), None),
            P(("seqs", "span"), None),
            P(("seqs", "span")),
            P(("seqs", "span")),
            P(("seqs", "span")),
        ),
        check_vma=False,
    )
```
